32 devices in a mesh: fsdp: 32 (over z, y, x, core).
Axes of the slice: x: 2, y: 2, z: 4, core: 2. Of those that a mesh axis runs over, the one named last changes fastest.
Arguments:
- tokens: bfloat16 [4096, 768], P('fsdp')
- doc_ids: int32 [4096], P('fsdp'), may hold values from 0 to 3, as said below
- pad_mask: int32 [4096], P('fsdp'), may hold values from 0 to 1, as said below
- qkv_matrix: bfloat16 [768, 2304], P('fsdp'), may hold values from -0.21875 to 0.21875
- query_bias: bfloat16 [768], P('fsdp'), may hold values from -3 to 3
- value_bias: bfloat16 [768], P('fsdp'), may hold values from -3 to 3
- out_matrix: bfloat16 [768, 768], P('fsdp'), may hold values from -1.75 to 1.75
- out_bias: bfloat16 [768], P('fsdp'), may hold values from -3 to 3
- attn_gain: bfloat16 [768], P('fsdp'), may hold values from 0.25 to 1.75
- attn_shift: bfloat16 [768], P('fsdp'), may hold values from -3 to 3
- up_matrix: bfloat16 [768, 3072], P('fsdp'), may hold values from -0.21875 to 0.21875
- up_bias: bfloat16 [3072], P('fsdp'), may hold values from -3 to 3
- down_matrix: bfloat16 [3072, 768], P('fsdp'), may hold values from -0.109375 to 0.109375
- down_bias: bfloat16 [768], P('fsdp'), may hold values from -3 to 3
- ffn_gain: bfloat16 [768], P('fsdp'), may hold values from 0.25 to 1.75
- ffn_shift: bfloat16 [768], P('fsdp'), may hold values from -3 to 3
- cotangent: bfloat16 [4096, 768], P('fsdp'), may hold values from -6 to 6
Outputs:
- layer_out: bfloat16 [4096, 768], P('fsdp')
- token_grad: float32 [4096, 768], P('fsdp')
- grad_qkv: float32 [768, 2304], P('fsdp')
- grad_qbias: float32 [768], P('fsdp')
- grad_vbias: float32 [768], P('fsdp')
- grad_outmat: float32 [768, 768], P('fsdp')
- grad_outbias: float32 [768], P('fsdp')
- grad_gain_one: float32 [768], P('fsdp')
- grad_shift_one: float32 [768], P('fsdp')
- grad_upmat: float32 [768, 3072], P('fsdp')
- grad_upbias: float32 [3072], P('fsdp')
- grad_downmat: float32 [3072, 768], P('fsdp')
- grad_downbias: float32 [768], P('fsdp')
- grad_gain_two: float32 [768], P('fsdp')
- grad_shift_two: float32 [768], P('fsdp')
The draws below stay inside these ranges and needn't reach their ends.
Inputs may be any that keep to these rules, and one draw needn't show every extreme that they name: `doc_ids`: within each block of 128 rows the ids never fall; the first row has 0 and the last 3; rows with one id are one sequence, padding continues the last one. `pad_mask`: within each block of 128 rows the ones come first and number from 32 to 128; some block is all ones and some has exactly 32.
All inputs are finite; a program needn't handle non-finite values.
Results may differ from the reference program's by a relative error of at most 0.01.
Values may be sent and summed in bfloat16 or wider, within the bound.
A program may use at most 192 MiB of HBM per device.

```python
import math
import jax
import jax.numpy as jnp
from jax import lax

D = 768
FF = 3072
HEADS = 12
ROWS_DEV = 128
TOKENS = 4096


def layout_rows(key):
    key = jax.random.fold_in(key, 11)
    blocks = TOKENS // ROWS_DEV
    key_valid, key_order, key_one, key_two, key_three = jax.random.split(key, 5)
    valid = jax.random.randint(key_valid, (blocks,), ROWS_DEV // 4, ROWS_DEV + 1)
    order = jax.random.permutation(key_order, blocks)
    valid = valid.at[order[0]].set(ROWS_DEV).at[order[1]].set(ROWS_DEV // 4)
    third = valid // 3
    first_cut = jax.random.randint(key_one, (blocks,), 1, third + 1)
    second_cut = jax.random.randint(key_two, (blocks,), third + 1, 2 * third + 1)
    third_cut = jax.random.randint(key_three, (blocks,), 2 * third + 1, 3 * third + 1)
    positions = jnp.arange(ROWS_DEV)[None, :]
    docs = (positions >= first_cut[:, None]).astype(jnp.int32) + (positions >= second_cut[:, None]).astype(jnp.int32) + (positions >= third_cut[:, None]).astype(jnp.int32)
    live = (positions < valid[:, None]).astype(jnp.int32)
    return (docs.reshape(TOKENS), live.reshape(TOKENS))


def draw_doc_ids(key, part):
    return layout_rows(key)[0]


def draw_pad_mask(key, part):
    return layout_rows(key)[1]


def draw_tokens(key, part):
    key_base = jax.random.fold_in(jax.random.fold_in(key, 5), 0)
    values = jax.random.normal(key_base, (TOKENS, D), jnp.float32)
    return values.astype(jnp.bfloat16)


def with_spikes(drawn, stream_key, source, target, shards_of, factor):
    def block_of(axis_at):
        return (jnp.arange(drawn.shape[axis_at]) // (drawn.shape[axis_at] // shards_of)).reshape((-1,) + (1,) * (drawn.ndim - 1 - axis_at))

    one_side = jax.random.permutation(stream_key, shards_of)[block_of(target)]
    other_side = (block_of(target) + shards_of // 2) % shards_of
    return jnp.where((block_of(source) == one_side) | (block_of(source) == other_side), factor * drawn, drawn)


def steps_of(key, dims, cuts, smallest, high):
    level = 1.0
    for position, shards_of in cuts:
        heights = jax.random.uniform(jax.random.fold_in(jax.random.fold_in(key, 6), position), (shards_of,), jnp.float32, smallest / len(cuts), high / len(cuts))
        level = level * jnp.repeat(jnp.exp(heights), dims[position] // shards_of).reshape((-1,) + (1,) * (len(dims) - 1 - position))
    return level


def bell_draw(key, shape, width, reach, cuts=(), held_as=jnp.bfloat16):
    level = steps_of(key, shape, cuts, -0.22, 0.18) if cuts else 1.0
    drawn = jax.random.normal(key, shape, jnp.float32) * width * level
    return jnp.minimum(jnp.maximum(drawn, -reach), reach).astype(held_as)


def noise_with(key, shape, width, reach, cuts, heavy, kind=jnp.bfloat16):
    array = width * jax.random.normal(key, shape, jnp.float32)
    if cuts:
        array = array * steps_of(key, shape, cuts, -0.22, 0.18)
    return jnp.clip(with_spikes(array, jax.random.fold_in(key, 3), *heavy), -reach, reach).astype(kind)


def setup_inputs(seed: int = 0) -> dict:
    streams_of = jax.random.split(jax.random.key(seed), 18)
    return {
        "tokens": draw_tokens(jax.random.fold_in(streams_of[17], 71), 0),
        "doc_ids": draw_doc_ids(jax.random.fold_in(streams_of[17], 71), 0),
        "pad_mask": draw_pad_mask(jax.random.fold_in(streams_of[17], 71), 0),
        "qkv_matrix": bell_draw(streams_of[3], (D, 3 * D), D ** -0.5, 0.21875, ((0, 32),)),
        "query_bias": bell_draw(streams_of[4], (D,), 0.5, 3.0, ((0, 32),)),
        "value_bias": bell_draw(streams_of[5], (D,), 0.5, 3.0, ((0, 32),)),
        "out_matrix": bell_draw(streams_of[6], (D, D), (D // 64) ** -0.5, 1.75, ((0, 32),)),
        "out_bias": bell_draw(streams_of[7], (D,), 0.5, 3.0, ((0, 32),)),
        "attn_gain": jnp.clip(1.0 + 0.15 * jax.random.normal(streams_of[8], (D,), jnp.float32), 0.25, 1.75).astype(jnp.bfloat16),
        "attn_shift": bell_draw(streams_of[9], (D,), 0.5, 3.0, ((0, 32),)),
        "up_matrix": bell_draw(streams_of[10], (D, FF), D ** -0.5, 0.21875, ((0, 32),)),
        "up_bias": bell_draw(streams_of[11], (FF,), 0.5, 3.0, ((0, 32),)),
        "down_matrix": bell_draw(streams_of[12], (FF, D), FF ** -0.5, 0.109375, ((0, 32),)),
        "down_bias": bell_draw(streams_of[13], (D,), 0.5, 3.0, ((0, 32),)),
        "ffn_gain": jnp.clip(1.0 + 0.15 * jax.random.normal(streams_of[14], (D,), jnp.float32), 0.25, 1.75).astype(jnp.bfloat16),
        "ffn_shift": bell_draw(streams_of[15], (D,), 0.5, 3.0, ((0, 32),)),
        "cotangent": noise_with(streams_of[16], (TOKENS, D), 1.0, 6.0, ((0, 32),), (0, 1, 32, 2.75)),
    }


norm_eps = 1e-06
root_half = 0.7071067811865476
inv_root_two_pi = 0.3989422804014327

def layer_norm(values, gain, shift):
    centred = values - lax.optimization_barrier(jnp.mean(values, axis=-1, keepdims=True))
    inverse = lax.rsqrt(lax.optimization_barrier(jnp.mean(centred * centred, axis=-1, keepdims=True)) + norm_eps)
    normed = centred * inverse
    return (normed * gain + shift, normed, inverse)

def norm_back(upstream, normed, inverse, gain):
    scaled = upstream * gain
    return inverse * (scaled - lax.optimization_barrier(jnp.mean(scaled, axis=-1, keepdims=True)) - normed * lax.optimization_barrier(jnp.mean(scaled * normed, axis=-1, keepdims=True)))

def block_pass(tokens, doc_ids, pad_mask, cotangent, params):
    qkv_m, qbias, vbias, out_m, out_b, gain_one, shift_one, up_m, up_b, down_m, down_b, gain_two, shift_two = params
    fl = jnp.float32
    row_count, model_width = tokens.shape
    head_size = model_width // HEADS
    score_scale = 1.0 / math.sqrt(head_size)
    zero_part = jnp.zeros((model_width,), fl)
    qkv = jnp.dot(tokens, qkv_m, preferred_element_type=fl)
    qkv = (qkv + jnp.concatenate([qbias.astype(fl), zero_part, vbias.astype(fl)])).astype(jnp.bfloat16)
    query = qkv[:, :model_width].reshape(row_count, HEADS, head_size)
    key_rows = qkv[:, model_width:2 * model_width].reshape(row_count, HEADS, head_size)
    value_rows = qkv[:, 2 * model_width:].reshape(row_count, HEADS, head_size)
    positions = jnp.arange(row_count)
    visible = (doc_ids[:, None] == doc_ids[None, :]) & ((pad_mask[None, :] == 1) | (positions[:, None] == positions[None, :]))
    scores = jnp.einsum('qhd,khd->hqk', query.astype(fl), key_rows.astype(fl)) * score_scale
    scores = jnp.where(visible[None], scores, -1e+30)
    row_max = lax.optimization_barrier(jnp.max(scores, axis=-1, keepdims=True))
    log_total = row_max + jnp.log(lax.optimization_barrier(jnp.sum(jnp.exp(scores - row_max), axis=-1, keepdims=True)))
    probs_f = jnp.exp(scores - log_total)
    probs_b = probs_f.astype(jnp.bfloat16)
    context = jnp.einsum('hqk,khd->qhd', probs_b.astype(fl), value_rows.astype(fl))
    context = context.reshape(row_count, model_width).astype(jnp.bfloat16)
    attn_sum = tokens.astype(fl) + jnp.dot(context, out_m, preferred_element_type=fl) + out_b.astype(fl)
    hidden, normed_one, inverse_one = layer_norm(attn_sum, gain_one.astype(fl), shift_one.astype(fl))
    hidden_b = hidden.astype(jnp.bfloat16)
    pre_act = jnp.dot(hidden_b, up_m, preferred_element_type=fl) + up_b.astype(fl)
    cdf_part = 0.5 * (1.0 + jax.scipy.special.erf(pre_act * root_half))
    pdf_part = jnp.exp(-0.5 * pre_act * pre_act) * inv_root_two_pi
    activation = (pre_act * cdf_part).astype(jnp.bfloat16)
    ffn_sum = hidden + jnp.dot(activation, down_m, preferred_element_type=fl) + down_b.astype(fl)
    normed_out, normed_two, inverse_two = layer_norm(ffn_sum, gain_two.astype(fl), shift_two.astype(fl))
    layer_out = normed_out.astype(jnp.bfloat16)
    upstream = cotangent.astype(fl)
    g_gain_two = lax.optimization_barrier(jnp.sum(upstream * normed_two, axis=0))
    g_shift_two = lax.optimization_barrier(jnp.sum(upstream, axis=0))
    d_ffn = norm_back(upstream, normed_two, inverse_two, gain_two.astype(fl))
    g_down_b = lax.optimization_barrier(jnp.sum(d_ffn, axis=0))
    d_ffn_b = d_ffn.astype(jnp.bfloat16)
    g_down_m = jnp.dot(activation.T, d_ffn_b, preferred_element_type=fl)
    d_act = jnp.dot(d_ffn_b, down_m.T, preferred_element_type=fl)
    d_pre = d_act * (cdf_part + pre_act * pdf_part)
    g_up_b = lax.optimization_barrier(jnp.sum(d_pre, axis=0))
    d_pre_b = d_pre.astype(jnp.bfloat16)
    g_up_m = jnp.dot(hidden_b.T, d_pre_b, preferred_element_type=fl)
    d_hidden = d_ffn + jnp.dot(d_pre_b, up_m.T, preferred_element_type=fl)
    g_gain_one = lax.optimization_barrier(jnp.sum(d_hidden * normed_one, axis=0))
    g_shift_one = lax.optimization_barrier(jnp.sum(d_hidden, axis=0))
    d_attn = norm_back(d_hidden, normed_one, inverse_one, gain_one.astype(fl))
    g_out_b = lax.optimization_barrier(jnp.sum(d_attn, axis=0))
    d_attn_b = d_attn.astype(jnp.bfloat16)
    g_out_m = jnp.dot(context.T, d_attn_b, preferred_element_type=fl)
    d_context = jnp.dot(d_attn_b, out_m.T, preferred_element_type=fl).astype(jnp.bfloat16)
    d_context = d_context.reshape(row_count, HEADS, head_size).astype(fl)
    d_value = jnp.einsum('hqk,qhd->khd', probs_b.astype(fl), d_context)
    d_probs = jnp.einsum('qhd,khd->hqk', d_context, value_rows.astype(fl))
    delta = lax.optimization_barrier(jnp.sum(probs_f * d_probs, axis=-1, keepdims=True))
    d_scores = (probs_f * (d_probs - delta) * score_scale).astype(jnp.bfloat16).astype(fl)
    d_query = jnp.einsum('hqk,khd->qhd', d_scores, key_rows.astype(fl)).reshape(row_count, model_width)
    d_key = jnp.einsum('hqk,qhd->khd', d_scores, query.astype(fl)).reshape(row_count, model_width)
    d_value = d_value.reshape(row_count, model_width)
    g_qbias = lax.optimization_barrier(jnp.sum(d_query, axis=0))
    g_vbias = lax.optimization_barrier(jnp.sum(d_value, axis=0))
    d_qkv = jnp.concatenate([d_query, d_key, d_value], axis=1).astype(jnp.bfloat16)
    g_qkv_m = jnp.dot(tokens.T, d_qkv, preferred_element_type=fl)
    token_grad = d_attn + jnp.dot(d_qkv, qkv_m.T, preferred_element_type=fl)
    grads = (g_qkv_m, g_qbias, g_vbias, g_out_m, g_out_b, g_gain_one, g_shift_one, g_up_m, g_up_b, g_down_m, g_down_b, g_gain_two, g_shift_two)
    return (layer_out, token_grad, grads)

def reference(tokens, doc_ids, pad_mask, qkv_matrix, query_bias, value_bias, out_matrix, out_bias, attn_gain, attn_shift, up_matrix, up_bias, down_matrix, down_bias, ffn_gain, ffn_shift, cotangent):
    params = (qkv_matrix, query_bias, value_bias, out_matrix, out_bias, attn_gain, attn_shift, up_matrix, up_bias, down_matrix, down_bias, ffn_gain, ffn_shift)
    blocks = TOKENS // ROWS_DEV
    inputs = (tokens.reshape(blocks, ROWS_DEV, D), doc_ids.reshape(blocks, ROWS_DEV), pad_mask.reshape(blocks, ROWS_DEV), cotangent.reshape(blocks, ROWS_DEV, D))
    start = tuple((jnp.zeros(p.shape, jnp.float32) for p in params))

    def advance(carry, item):
        layer_out, token_grad, grads = block_pass(item[0], item[1], item[2], item[3], params)
        return (tuple((c + g for c, g in zip(carry, grads))), (layer_out, token_grad))
    totals, (outputs, grads_in) = lax.scan(advance, start, inputs)
    return (outputs.reshape(TOKENS, D), grads_in.reshape(TOKENS, D), totals[0], totals[1], totals[2], totals[3], totals[4], totals[5], totals[6], totals[7], totals[8], totals[9], totals[10], totals[11], totals[12])
```

```python
import functools
import heapq
import math
import types

import jax
import jax.numpy as jnp
from jax import lax
from jax.experimental import pallas as pl
from jax.experimental.pallas import tpu as pltpu
from jax.sharding import PartitionSpec as P

HEADS = 12
AXIS = "fsdp"
MESH_IDS = pl.DeviceIdType.MESH
GROUP = 32


norm_eps = 1e-06
root_half = 0.7071067811865476
inv_root_two_pi = 0.3989422804014327


def layer_norm(values, gain, shift):
    centred = values - jnp.mean(values, axis=-1, keepdims=True)
    inverse = lax.rsqrt(jnp.mean(centred * centred, axis=-1, keepdims=True) + norm_eps)
    normed = centred * inverse
    return (normed * gain + shift, normed, inverse)


def norm_back(upstream, normed, inverse, gain):
    scaled = upstream * gain
    return inverse * (
        scaled
        - jnp.mean(scaled, axis=-1, keepdims=True)
        - normed * jnp.mean(scaled * normed, axis=-1, keepdims=True)
    )


def masked_scores(query, key_rows, visible, score_scale):
    scores = (
        jnp.einsum("qhd,khd->hqk", query, key_rows, preferred_element_type=jnp.float32)
        * score_scale
    )
    return jnp.where(visible[None], scores, -1e30)


def vector_rows(vectors):
    rows = [jnp.pad(v, ((0, 0), (0, 128 - v.shape[1]))) for v in vectors]
    rows = rows + [jnp.zeros_like(rows[0])] * (16 - len(rows))
    return jnp.stack(rows, axis=1)


def attention_back_kernel(
    scale, qkv_ref, back_ref, doc_col, doc_row, pad_row, d_qkv_ref, sums_ref
):
    fl = jnp.float32
    rows, width = back_ref.shape
    size = width // HEADS
    across, down, both = ((1,), (0,)), ((0,), (0,)), ((1,), (1,))

    def dot(a, b, over):
        return lax.dot_general(a, b, (over, ((), ())), preferred_element_type=fl)

    square = (rows, rows)
    same = lax.broadcasted_iota(jnp.int32, square, 0) == lax.broadcasted_iota(
        jnp.int32, square, 1
    )
    visible = (doc_col[...] == doc_row[...]) & ((pad_row[...] == 1) | same)
    for pair in range(HEADS // 2):
        results = []
        for h in (2 * pair, 2 * pair + 1):
            query, key_rows, value_rows = (
                qkv_ref[:, part * width + h * size : part * width + (h + 1) * size]
                for part in range(3)
            )
            back = back_ref[:, h * size : (h + 1) * size]
            scores = jnp.where(visible, dot(query, key_rows, both) * scale, -1e30)
            row_max = jnp.max(scores, axis=-1, keepdims=True)
            total = jnp.sum(jnp.exp(scores - row_max), axis=-1, keepdims=True)
            probs = jnp.exp(scores - (row_max + jnp.log(total)))
            d_value = dot(probs.astype(jnp.bfloat16), back, down)
            d_probs = dot(back, value_rows, both)
            delta = jnp.sum(probs * d_probs, axis=-1, keepdims=True)
            d_scores = (probs * (d_probs - delta) * scale).astype(jnp.bfloat16)
            results.append(
                (dot(d_scores, key_rows, across), dot(d_scores, query, down), d_value)
            )
        for part in range(3):
            block = jnp.concatenate([results[0][part], results[1][part]], axis=1)
            at = pair * 2 * size
            d_qkv_ref[:, part * width + at : part * width + at + 2 * size] = block.astype(
                jnp.bfloat16
            )
            if part != 1:
                row = part // 2
                sums_ref[row : row + 1, at : at + 2 * size] = jnp.sum(
                    block, axis=0, keepdims=True
                )


def attention_back(qkv, d_context, doc_ids, pad_mask):
    rows, width = d_context.shape
    return pl.pallas_call(
        functools.partial(attention_back_kernel, 1.0 / math.sqrt(width // HEADS)),
        out_shape=(
            jax.ShapeDtypeStruct(qkv.shape, jnp.bfloat16),
            jax.ShapeDtypeStruct((2, width), jnp.float32),
        ),
        compiler_params=pltpu.CompilerParams(vmem_limit_bytes=24 * 1024 * 1024),
        name="attention_back",
    )(qkv, d_context, doc_ids[:, None], doc_ids[None], pad_mask[None])


def grad_rows(left, right):
    return jnp.einsum("ra,rb->ab", left, right, preferred_element_type=jnp.float32)


X, Y, Z1, Z2 = 0, 1, 2, 3
GATHER_ORDERS = (
    (Z2, Z1, X, Y),
    (Z2, Z1, Y, X),
    (X, Z2, Z1, Y),
    (Y, Z2, Z1, X),
    (Z2, Z1, X, Y),
)
SCATTER_ORDERS = tuple(tuple(reversed(o)) for o in GATHER_ORDERS)
PAIRS = 16
PIECE_ROWS = (48, 48, 48, 192, 32)
PIECE_COLS = (1152, 384, 1536, 384, 128)
COUNT = 5
HOPS = {X: ((0, 1),), Y: ((1, 1),), Z1: ((2, 1),), Z2: ((2, 1), (3, 2))}
LINK_BYTES_PER_US = 46e3
HOP_US = 1.0
FUSED_VMEM = 58 * 1024 * 1024


class Plan:
    def __init__(self):
        self.now = 0.0
        self.free = {}
        self.pending = []
        self.seq = 0

    def travel(self, dim, size, key):
        us = size / LINK_BYTES_PER_US
        begin = max([self.now] + [self.free.get(link, 0.0) for link, _ in HOPS[dim]])
        end = begin
        for link, cost in HOPS[dim]:
            self.free[link] = begin + cost * us
            end = max(end, begin + cost * us)
        heapq.heappush(self.pending, (end + HOP_US, self.seq, key))
        self.seq += 1


def subsets(order, step):
    blocks = [0]
    for b in reversed(order[step + 1 :]):
        blocks = [r | (1 << b) for r in blocks] + blocks
    return blocks


def dot(a, b, over=((1,), (0,))):
    return lax.dot_general(a, b, (over, ((), ())), preferred_element_type=jnp.float32)


ROWS_BOTH, COLS_BOTH = ((0,), (0,)), ((1,), (1,))

SIBLING_COPIES = 25


def scratch_of(rows, width, hidden):
    fl, bf = jnp.float32, jnp.bfloat16
    both, half, hhalf = 2 * rows, width // 2, hidden // 2
    lists = []
    for shape_of in (
        lambda pr, pc: ((PAIRS * pr, pc), bf),
        lambda pr, pc: ((PAIRS * pr, pc), bf),
        lambda pr, pc: ((PAIRS - 1, pr, pc), bf),
        lambda pr, pc: (((pr // 2 + 15) // 16 * 16, pc), bf),
        lambda pr, pc: (((pr // 2 + 15) // 16 * 16, pc), bf),
        lambda pr, pc: ((pr, pc), fl),
    ):
        lists += [shape_of(PIECE_ROWS[k], PIECE_COLS[k]) for k in range(COUNT)]
    named = dict(
        peer_part4=((PAIRS * PIECE_ROWS[4], PIECE_COLS[4]), bf),
        stage_part4=((PAIRS * PIECE_ROWS[4], PIECE_COLS[4]), bf),
        tok=((both, width), bf),
        marks=((2, 8, rows), fl),
        vec32=((PAIRS * 32, 128), fl),
        vecs=((16, width), fl),
        upb=((8, hhalf), fl),
        qkv=((both, 3 * half), bf),
        probs=((HEADS, rows, rows), fl),
        ctx=((both, width), bf),
        proj_s=((rows, half), fl),
        proj_r=((rows, half), fl),
        proj_o=((rows, half), fl),
        hid=((rows, width), fl),
        n1=((rows, width), fl),
        i1=((rows, 128), fl),
        hb=((both, width), bf),
        act=((both, hidden), bf),
        fac=((both, hhalf), fl),
        ffn_s=((rows, half), fl),
        ffn_r=((rows, half), fl),
        ffn_o=((rows, half), fl),
        dff=((rows, width), fl),
        dfb=((both, width), bf),
        dact_s=((both, hhalf), fl),
        dact_r=((both, hhalf), fl),
        dact_o=((both, hhalf), fl),
        dpre=((both, hhalf), bf),
        dhid_s=((rows, width), fl),
        dhid_r=((rows, width), fl),
        dhid_o=((rows, width), fl),
        dat=((rows, width), fl),
        datb=((both, width), bf),
        dctx_s=((both, half), fl),
        dctx_r=((both, half), fl),
        dctx_o=((both, half), fl),
        dctx=((both, half), bf),
        dqkv=((both, 3 * half), bf),
        tg_s=((rows, width), fl),
        tg_r=((rows, width), fl),
        tg_o=((rows, width), fl),
        sums=((16, width), fl),
        upsum=((8, hhalf), fl),
    )
    return lists, named


def layer_kernel(names, *refs):
    refs = list(refs)

    def take(count):
        taken, refs[:count] = refs[:count], []
        return taken

    R = types.SimpleNamespace()
    R.tokens, R.doc, R.pad = take(3)
    R.w, R.v, R.cotangent = take(4), take(9), take(1)[0]
    R.layer_out, R.token_grad = take(2)
    R.g, R.gv = take(4), take(1)[0]
    R.whole, R.part, R.land, R.stage, R.peer, R.fin = (take(COUNT) for _ in range(6))
    vars(R).update(zip(names, take(len(names))))
    sib_send, sib_recv, g_send, g_recv, s_send, s_recv = refs
    fl, bf = jnp.float32, jnp.bfloat16
    rows, width = R.tokens.shape
    hidden = R.w[2].shape[1]
    half, hhalf = width // 2, hidden // 2
    size = width // HEADS
    scale = 1.0 / math.sqrt(size)
    me = lax.axis_index(AXIS)
    core = lax.rem(me, 2)
    pair = lax.div(me, 2)
    bits = [lax.rem(lax.div(pair, 1 << b), 2) for b in range(4)]
    sibling = me + 1 - 2 * core
    is_first = core == 0

    def pair_of(r):
        p = pair
        for b in range(4):
            if r >> b & 1:
                p = p + (1 << b) * (1 - 2 * bits[b])
        return p

    def device_along(b):
        return me + (2 << b) * (1 - 2 * bits[b])

    def by_core(step, which=None):
        at = core if which is None else 1 - core
        return pl.multiple_of(at * step, step)

    own_rows, sib_rows = pl.ds(by_core(rows), rows), pl.ds(by_core(rows, 1), rows)
    own_half, sib_half = pl.ds(by_core(half), half), pl.ds(by_core(half, 1), half)
    own_hh, sib_hh = pl.ds(by_core(hhalf), hhalf), pl.ds(by_core(hhalf, 1), hhalf)

    barrier = pltpu.get_barrier_semaphore()
    for other in [sibling] + [device_along(b) for b in range(4)]:
        pl.semaphore_signal(barrier, inc=1, device_id=(other,), device_id_type=MESH_IDS)
    pl.semaphore_wait(barrier, 5)

    sib = {}
    sent = []

    def to_sibling(i, src, dst):
        copy = pltpu.make_async_remote_copy(
            src_ref=src,
            dst_ref=dst,
            send_sem=sib_send.at[i],
            recv_sem=sib_recv.at[i],
            device_id=(sibling,),
            device_id_type=MESH_IDS,
        )
        copy.start()
        sib[i] = copy
        sent.append(copy)

    def side_by_side(own, other):
        return jnp.concatenate(
            [jnp.where(is_first, own, other), jnp.where(is_first, other, own)], axis=1
        )

    def shard_half(k, mine):
        ref = R.w[k]
        if k == 0:
            cols = [
                ref[:, pl.ds(pl.multiple_of(p * width + (core if mine else 1 - core) * half, 128), half)]
                for p in range(3)
            ]
            return jnp.concatenate([c.astype(fl) for c in cols], axis=1)
        cols = PIECE_COLS[k]
        return ref[:, pl.ds(by_core(cols, None if mine else 1), cols)].astype(fl)

    def padded(value):
        short = -value.shape[0] % 16
        if short:
            value = jnp.concatenate([value, jnp.zeros((short, value.shape[1]), fl)], axis=0)
        return value.astype(bf)

    R.stage[4][...] = jnp.zeros(R.stage[4].shape, bf)
    R.vec32[pl.ds(0, 16), :] = jnp.zeros((16, 128), fl)
    for j in range(9):
        v = R.v[j]
        R.vec32[j : j + 1, 0 : v.shape[1]] = v[...].astype(fl)
    R.stage[4][...] = R.vec32[pl.ds(0, 16), :].astype(bf)
    for k in (0, 4, 1, 2, 3):
        if k < 4:
            R.stage[k][...] = padded(shard_half(k, False))
        to_sibling(k, R.stage[k], R.peer[k])
    to_sibling(5, R.tokens, R.tok.at[own_rows])
    own_marks = jnp.concatenate(
        [R.doc[...].astype(fl), R.pad[...].astype(fl), jnp.zeros((6, rows), fl)], axis=0
    )
    R.marks[core] = own_marks
    to_sibling(6, R.marks.at[core], R.marks.at[core])
    R.tok[own_rows, :] = R.tokens[...]

    plan = Plan()
    piece_bytes = [2 * PIECE_ROWS[k] * PIECE_COLS[k] for k in range(COUNT)]
    done = [1] * COUNT

    def piece_at(k, r):
        n = PIECE_ROWS[k]
        return pl.ds(pl.multiple_of(pair_of(r) * n, n), n)

    def gather_move(k, r, b):
        at = piece_at(k, r)
        slot = r | (1 << b)
        copy = pltpu.make_async_remote_copy(
            src_ref=R.whole[k].at[at],
            dst_ref=R.whole[k].at[at],
            send_sem=g_send.at[k, slot],
            recv_sem=g_recv.at[k, slot],
            device_id=(device_along(b),),
            device_id_type=MESH_IDS,
        )
        copy.start()
        sent.append(copy)
        plan.travel(b, piece_bytes[k], (True, k, slot, b))

    for k in (0, 4, 1, 2, 3):
        sib[k].wait_recv()
        if k < 4:
            mine = shard_half(k, True)
        else:
            mine = R.vec32[pl.ds(0, 16), :]
        theirs = R.peer[k][...].astype(fl)[: mine.shape[0]]
        R.whole[k][piece_at(k, 0), :] = jnp.concatenate(
            [jnp.where(is_first, mine, theirs), jnp.where(is_first, theirs, mine)], axis=0
        ).astype(bf)
        for b in GATHER_ORDERS[k]:
            gather_move(k, 0, b)

    def on_gather(k, r, b):
        here = R.whole[k].at[piece_at(k, r)]
        pltpu.make_async_remote_copy(
            src_ref=here,
            dst_ref=here,
            send_sem=g_send.at[k, r],
            recv_sem=g_recv.at[k, r],
            device_id=(device_along(b),),
            device_id_type=MESH_IDS,
        ).wait_recv()
        order = GATHER_ORDERS[k]
        for later in order[order.index(b) + 1 :]:
            gather_move(k, r, later)
        done[k] += 1

    slot_of = []
    for k in range(COUNT):
        table = {}
        for step in range(4):
            for r in subsets(SCATTER_ORDERS[k], step):
                table[step, r] = len(table)
        slot_of.append(table)
    copies = {}

    def held(k, step, r):
        if step < 0:
            return R.part[k].at[piece_at(k, r)]
        return R.land[k].at[slot_of[k][step, r]]

    def scatter_move(k, step, r):
        b = SCATTER_ORDERS[k][step]
        low = r & ~(1 << b)
        slot = slot_of[k][step, low]
        copy = pltpu.make_async_remote_copy(
            src_ref=held(k, step - 1, r),
            dst_ref=R.land[k].at[slot],
            send_sem=s_send.at[k, slot],
            recv_sem=s_recv.at[k, slot],
            device_id=(device_along(b),),
            device_id_type=MESH_IDS,
        )
        copy.start()
        sent.append(copy)
        copies[k, step, low] = copy
        plan.travel(b, piece_bytes[k], (False, k, step, low))

    def scatter_start(k):
        order = SCATTER_ORDERS[k]
        for r in subsets(order, 0):
            scatter_move(k, 0, r | (1 << order[0]))

    def finish(k):
        if k == 4:
            R.gv[...] = R.fin[4][pl.ds(by_core(16), 16), :]
            return
        n = PIECE_ROWS[k] // 2
        mine = R.fin[k].at[pl.ds(by_core(n), n)]
        theirs = R.fin[k].at[pl.ds(by_core(n, 1), n)]
        if k == 0:
            for p in range(3):
                at = pl.ds(pl.multiple_of(p * width + core * half, 128), half)
                part = pl.ds(p * half, half)
                to_sibling(18 + p, theirs.at[:, part], R.g[0].at[:, at])
                R.g[0][:, at] = mine[:, part]
        else:
            at = pl.ds(by_core(PIECE_COLS[k]), PIECE_COLS[k])
            to_sibling(20 + k, theirs, R.g[k].at[:, at])
            R.g[k][:, at] = mine[...]

    summed = set()
    early = {}

    def on_scatter(k, step, r):
        if step and (k, step - 1, r) not in summed:
            early[k, step - 1, r] = step
            return
        summed.add((k, step, r))
        add_piece(k, step, r)
        if (k, step, r) in early:
            on_scatter(k, early[k, step, r], r)

    def add_piece(k, step, r):
        copies[k, step, r].wait_recv()
        order = SCATTER_ORDERS[k]
        before, now = held(k, step - 1, r), held(k, step, r)
        total = now[...].astype(fl) + before[...].astype(fl)
        if step == 3:
            R.fin[k][...] = total
            finish(k)
            return
        now[...] = total.astype(bf)
        if r >> order[step + 1] & 1:
            scatter_move(k, step + 1, r)

    def column_of(n, period):
        return jnp.floor((n + 0.5) * (1.0 / period))

    def pick(count, period):
        n = lax.broadcasted_iota(jnp.int32, (128, count), 1).astype(fl)
        i = lax.broadcasted_iota(jnp.int32, (128, count), 0).astype(fl)
        return jnp.where(n - period * column_of(n, period) == i, 1.0, 0.0).astype(bf)

    def owner_is(count, period, first):
        n = lax.broadcasted_iota(jnp.int32, (GROUP, count), 1).astype(fl)
        d = lax.broadcasted_iota(jnp.int32, (GROUP, count), 0).astype(fl)
        return column_of(n, period) + first == d

    small, large = width // GROUP, hidden // GROUP

    def half_first():
        return jnp.where(is_first, 0.0, GROUP / 2.0)

    def task_vectors():
        R.vec32[...] = R.whole[4][...].astype(fl)
        chosen, owner = pick(width, small), owner_is(width, small, 0.0)
        for j in range(8):
            v = R.vec32[pl.ds(j, GROUP, stride=16), :].astype(bf)
            R.vecs[j : j + 1, :] = jnp.sum(
                jnp.where(owner, dot(v, chosen), 0.0), axis=0, keepdims=True
            )
        v = R.vec32[pl.ds(8, GROUP, stride=16), :].astype(bf)
        R.upb[0:1, :] = jnp.sum(
            jnp.where(owner_is(hhalf, large, half_first()), dot(v, pick(hhalf, large)), 0.0),
            axis=0,
            keepdims=True,
        )

    def vec(j):
        return R.vecs[j : j + 1, :]

    def task_qkv():
        sib[5].wait_recv()
        sib[6].wait_recv()
        for p in range(3):
            at = pl.ds(p * half, half)
            value = dot(R.tok[...], R.whole[0][:, at])
            if p != 1:
                value = value + R.vecs[p // 2 : p // 2 + 1, own_half]
            R.qkv[:, at] = value.astype(bf)

    def seen(b):
        doc, pad = R.marks[b, 0:1, :], R.marks[b, 1:2, :]
        square = (rows, rows)
        wide = jnp.broadcast_to(doc, square)
        same = lax.broadcasted_iota(jnp.int32, square, 0) == lax.broadcasted_iota(
            jnp.int32, square, 1
        )
        return (wide.T == wide) & ((jnp.broadcast_to(pad, square) == 1.0) | same)

    def head_of(b, h):
        at = b * rows
        return [
            R.qkv[at : at + rows, p * half + h * size : p * half + (h + 1) * size]
            for p in range(3)
        ]

    def task_attention(b, two):
        visible = seen(b)
        found = []
        for h in (2 * two, 2 * two + 1):
            query, key_rows, value_rows = head_of(b, h)
            scores = jnp.where(visible, dot(query, key_rows, COLS_BOTH) * scale, -1e30)
            row_max = jnp.max(scores, axis=-1, keepdims=True)
            total = jnp.sum(jnp.exp(scores - row_max), axis=-1, keepdims=True)
            probs = jnp.exp(scores - (row_max + jnp.log(total)))
            R.probs[b * (HEADS // 2) + h] = probs
            found.append(dot(probs.astype(bf), value_rows))
        at = pl.ds(pl.multiple_of(core * half + two * 2 * size, 128), 2 * size)
        R.ctx[pl.ds(b * rows, rows), at] = jnp.concatenate(found, axis=1).astype(bf)
        if b == 1 and two == HEADS // 4 - 1:
            to_sibling(7, R.ctx.at[:, own_half], R.ctx.at[:, own_half])

    def task_project():
        sib[7].wait_recv()
        R.proj_s[...] = dot(R.ctx[sib_rows, :], R.whole[1][...])
        to_sibling(8, R.proj_s, R.proj_r)
        R.proj_o[...] = dot(R.ctx[own_rows, :], R.whole[1][...])

    def norm(values):
        centred = values - jnp.mean(values, axis=-1, keepdims=True)
        inverse = lax.rsqrt(jnp.mean(centred * centred, axis=-1, keepdims=True) + norm_eps)
        return centred * inverse, inverse

    def task_norm_one():
        sib[8].wait_recv()
        attn = (
            R.tokens[...].astype(fl)
            + side_by_side(R.proj_o[...], R.proj_r[...])
            + vec(2)
        )
        normed, inverse = norm(attn)
        hid = normed * vec(3) + vec(4)
        R.n1[...] = normed
        R.i1[...] = jnp.broadcast_to(inverse, (rows, 128))
        R.hid[...] = hid
        R.hb[own_rows, :] = hid.astype(bf)
        to_sibling(9, R.hb.at[own_rows], R.hb.at[own_rows])

    tile = 384

    def task_up():
        sib[9].wait_recv()

        def body(t, carry):
            at = pl.ds(pl.multiple_of(t * tile, tile), tile)
            pre = dot(R.hb[...], R.whole[2][:, at]) + R.upb[0:1, at]
            cdf = 0.5 * (1.0 + lax.erf(pre * root_half))
            pdf = jnp.exp(-0.5 * pre * pre) * inv_root_two_pi
            R.fac[:, at] = cdf + pre * pdf
            R.act[:, pl.ds(pl.multiple_of(core * hhalf + t * tile, tile), tile)] = (
                pre * cdf
            ).astype(bf)
            return carry

        lax.fori_loop(0, hhalf // tile, body, 0)
        to_sibling(10, R.act.at[:, own_hh], R.act.at[:, own_hh])

    def task_ffn():
        sib[10].wait_recv()
        R.ffn_s[...] = dot(R.act[sib_rows, :], R.whole[3][...])
        to_sibling(11, R.ffn_s, R.ffn_r)
        R.ffn_o[...] = dot(R.act[own_rows, :], R.whole[3][...])

    def back_of_norm(upstream, normed, inverse, gain):
        scaled = upstream * gain
        return inverse * (
            scaled
            - jnp.mean(scaled, axis=-1, keepdims=True)
            - normed * jnp.mean(scaled * normed, axis=-1, keepdims=True)
        )

    def add_sum(j, values):
        R.sums[j : j + 1, :] = jnp.sum(values, axis=0, keepdims=True)

    def task_norm_two():
        sib[11].wait_recv()
        total = R.hid[...] + side_by_side(R.ffn_o[...], R.ffn_r[...]) + vec(5)
        normed, inverse = norm(total)
        R.layer_out[...] = (normed * vec(6) + vec(7)).astype(bf)
        upstream = R.cotangent[...].astype(fl)
        d_ffn = back_of_norm(upstream, normed, inverse, vec(6))
        R.dff[...] = d_ffn
        R.dfb[own_rows, :] = d_ffn.astype(bf)
        to_sibling(12, R.dfb.at[own_rows], R.dfb.at[own_rows])
        add_sum(6, upstream * normed)
        add_sum(7, upstream)
        add_sum(5, d_ffn)

    def task_grad_down():
        sib[12].wait_recv()

        def body(t, carry):
            at = pl.ds(pl.multiple_of(t * tile, tile), tile)
            R.part[3][at, :] = dot(R.act[:, at], R.dfb[:, own_half], ROWS_BOTH).astype(bf)
            return carry

        lax.fori_loop(0, hidden // tile, body, 0)
        scatter_start(3)

    def d_act_half(which, into):
        def body(t, carry):
            src = pl.ds(pl.multiple_of(which * hhalf + t * tile, tile), tile)
            at = pl.ds(pl.multiple_of(t * tile, tile), tile)
            into[:, at] = dot(R.dfb[:, own_half], R.whole[3][src, :], COLS_BOTH)
            return carry

        lax.fori_loop(0, hhalf // tile, body, 0)

    def task_d_act():
        d_act_half(1 - core, R.dact_s)
        to_sibling(13, R.dact_s, R.dact_r)
        d_act_half(core, R.dact_o)

    def task_d_pre():
        sib[13].wait_recv()

        def body(t, carry):
            at = pl.ds(pl.multiple_of(t * tile, tile), tile)
            value = (R.dact_o[:, at] + R.dact_r[:, at]) * R.fac[:, at]
            R.upsum[0:1, at] = jnp.sum(value, axis=0, keepdims=True)
            R.dpre[:, at] = value.astype(bf)
            return carry

        lax.fori_loop(0, hhalf // tile, body, 0)

    def task_d_hidden():
        R.dhid_s[...] = dot(R.dpre[sib_rows, :], R.whole[2][...], COLS_BOTH)
        to_sibling(14, R.dhid_s, R.dhid_r)
        R.dhid_o[...] = dot(R.dpre[own_rows, :], R.whole[2][...], COLS_BOTH)

    def task_grad_up():
        def body(t, carry):
            at = pl.ds(pl.multiple_of(t * tile, tile), tile)
            R.part[2][:, at] = dot(R.hb[...], R.dpre[:, at], ROWS_BOTH).astype(bf)
            return carry

        lax.fori_loop(0, hhalf // tile, body, 0)
        scatter_start(2)

    def task_norm_one_back():
        sib[14].wait_recv()
        d_hid = R.dff[...] + R.dhid_o[...] + R.dhid_r[...]
        normed = R.n1[...]
        d_attn = back_of_norm(d_hid, normed, R.i1[:, 0:1], vec(3))
        R.dat[...] = d_attn
        R.datb[own_rows, :] = d_attn.astype(bf)
        to_sibling(15, R.datb.at[own_rows], R.datb.at[own_rows])
        add_sum(3, d_hid * normed)
        add_sum(4, d_hid)
        add_sum(2, d_attn)

    def task_d_context():
        sib[15].wait_recv()
        right = R.datb[:, own_half]
        R.dctx_s[...] = dot(right, R.whole[1][sib_half, :], COLS_BOTH)
        to_sibling(16, R.dctx_s, R.dctx_r)
        R.dctx_o[...] = dot(right, R.whole[1][own_half, :], COLS_BOTH)

    def task_grad_out():
        R.part[1][...] = dot(R.ctx[...], R.datb[:, own_half], ROWS_BOTH).astype(bf)
        scatter_start(1)

    def task_d_context_sum():
        sib[16].wait_recv()
        R.dctx[...] = (R.dctx_o[...] + R.dctx_r[...]).astype(bf)

    bias_sums = {}

    def task_attention_back(b, two):
        found = []
        at = b * rows
        for h in (2 * two, 2 * two + 1):
            query, key_rows, value_rows = head_of(b, h)
            back = R.dctx[at : at + rows, h * size : (h + 1) * size]
            probs = R.probs[b * (HEADS // 2) + h]
            d_value = dot(probs.astype(bf), back, ROWS_BOTH)
            d_probs = dot(back, value_rows, COLS_BOTH)
            delta = jnp.sum(probs * d_probs, axis=-1, keepdims=True)
            d_scores = (probs * (d_probs - delta) * scale).astype(bf)
            found.append((dot(d_scores, key_rows), dot(d_scores, query, ROWS_BOTH), d_value))
        for p in range(3):
            block = jnp.concatenate([found[0][p], found[1][p]], axis=1)
            cols = p * half + two * 2 * size
            R.dqkv[at : at + rows, cols : cols + 2 * size] = block.astype(bf)
            if p != 1:
                total = jnp.sum(block, axis=0, keepdims=True)
                if b == 0:
                    bias_sums[p, two] = total
                else:
                    to = pl.ds(pl.multiple_of(core * half + two * 2 * size, 128), 2 * size)
                    R.sums[p // 2 : p // 2 + 1, to] = total + bias_sums[p, two]

    def task_clear_sums():
        R.sums[...] = jnp.zeros(R.sums.shape, fl)

    def task_grad_qkv():
        for p in range(3):
            at = pl.ds(p * half, half)
            R.part[0][:, at] = dot(R.tok[...], R.dqkv[:, at], ROWS_BOTH).astype(bf)
        scatter_start(0)

    def task_token_grad():
        R.tg_s[...] = dot(R.dqkv[sib_rows, :], R.whole[0][...], COLS_BOTH)
        to_sibling(17, R.tg_s, R.tg_r)
        R.tg_o[...] = R.dat[...] + dot(R.dqkv[own_rows, :], R.whole[0][...], COLS_BOTH)

    def task_sums():
        chosen, owner = pick(width, small), owner_is(width, small, 0.0)
        R.vec32[...] = jnp.zeros(R.vec32.shape, fl)
        for j in range(8):
            spread = jnp.where(owner, R.sums[j : j + 1, :], 0.0).astype(bf)
            R.vec32[pl.ds(j, GROUP, stride=16), :] = dot(spread, chosen, COLS_BOTH)
        spread = jnp.where(
            owner_is(hhalf, large, half_first()), R.upsum[0:1, :], 0.0
        ).astype(bf)
        R.vec32[pl.ds(8, GROUP, stride=16), :] = dot(spread, pick(hhalf, large), COLS_BOTH)
        R.stage_part4[...] = R.vec32[...].astype(bf)
        to_sibling(24, R.stage_part4, R.peer_part4)

    def task_sums_send():
        sib[24].wait_recv()
        R.part[4][...] = (R.vec32[...] + R.peer_part4[...].astype(fl)).astype(bf)
        scatter_start(4)

    def task_token_grad_sum():
        sib[17].wait_recv()
        R.token_grad[...] = R.tg_o[...] + R.tg_r[...]

    two_heads = [(b, two) for b in range(2) for two in range(HEADS // 4)]
    tasks = [(task_clear_sums, (), 0.1), (task_vectors, (4,), 0.8), (task_qkv, (0,), 1.2)]
    tasks += [(functools.partial(task_attention, b, two), (), 1.0) for b, two in two_heads]
    tasks += [
        (task_project, (1,), 1.5),
        (task_norm_one, (), 1.5),
        (task_up, (2,), 5.0),
        (task_ffn, (3,), 1.5),
        (task_norm_two, (), 2.0),
        (task_grad_down, (), 2.5),
        (task_d_act, (), 1.5),
        (task_d_pre, (), 1.5),
        (task_d_hidden, (), 1.0),
        (task_grad_up, (), 1.5),
        (task_norm_one_back, (), 1.0),
        (task_d_context, (), 1.5),
        (task_grad_out, (), 0.7),
        (task_d_context_sum, (), 0.5),
    ]
    tasks += [(functools.partial(task_attention_back, b, two), (), 1.0) for b, two in two_heads]
    tasks += [
        (task_grad_qkv, (), 1.2),
        (task_token_grad, (), 1.0),
        (task_sums, (), 0.8),
        (task_sums_send, (), 0.8),
        (task_token_grad_sum, (), 0.3),
    ]
    while tasks or plan.pending:
        soonest = plan.pending[0][0] if plan.pending else None
        ready = bool(tasks) and all(done[k] == PAIRS for k in tasks[0][1])
        if plan.pending and (soonest <= plan.now or not ready):
            plan.now = max(plan.now, soonest)
            key = heapq.heappop(plan.pending)[2]
            if key[0]:
                plan.now += 0.1
                on_gather(*key[1:])
            else:
                plan.now += 0.3
                on_scatter(*key[1:])
        else:
            task, _, cost = tasks.pop(0)
            plan.now += cost
            task()
    for i in range(18, 24):
        sib[i].wait_recv()
    for copy in sent:
        copy.wait_send()


def fused(tokens, doc_ids, pad_mask, matrices, vectors, cotangent):
    rows, width = tokens.shape
    hidden = matrices[2].shape[1]
    fl = jnp.float32
    lists, named = scratch_of(rows, width, hidden)
    operands = (
        [tokens, doc_ids[None], pad_mask[None]]
        + list(matrices)
        + [v[None] for v in vectors]
        + [cotangent]
    )
    vmem = pl.BlockSpec(memory_space=pltpu.VMEM)
    dma = pltpu.SemaphoreType.DMA
    layer_out, token_grad, g0, g1, g2, g3, gv = pl.pallas_call(
        functools.partial(layer_kernel, tuple(named)),
        out_shape=[
            jax.ShapeDtypeStruct(tokens.shape, jnp.bfloat16),
            jax.ShapeDtypeStruct(tokens.shape, fl),
        ]
        + [jax.ShapeDtypeStruct(m.shape, fl) for m in matrices]
        + [jax.ShapeDtypeStruct((16, 128), fl)],
        in_specs=[vmem] * len(operands),
        out_specs=[vmem] * 7,
        scratch_shapes=[pltpu.VMEM(shape, kind) for shape, kind in lists + list(named.values())]
        + [
            dma((SIBLING_COPIES,)),
            dma((SIBLING_COPIES,)),
            dma((COUNT, PAIRS)),
            dma((COUNT, PAIRS)),
            dma((COUNT, PAIRS)),
            dma((COUNT, PAIRS)),
        ],
        compiler_params=pltpu.CompilerParams(
            collective_id=0, has_side_effects=True, vmem_limit_bytes=FUSED_VMEM
        ),
        name="layer",
    )(*operands)
    s = [gv[j, : v.shape[0]] for j, v in enumerate(vectors)]
    return (
        layer_out,
        token_grad,
        g0,
        s[0],
        s[1],
        g1,
        s[2],
        s[3],
        s[4],
        g2,
        s[8],
        g3,
        s[5],
        s[6],
        s[7],
    )


def local(
    tokens,
    doc_ids,
    pad_mask,
    qkv_matrix,
    query_bias,
    value_bias,
    out_matrix,
    out_bias,
    attn_gain,
    attn_shift,
    up_matrix,
    up_bias,
    down_matrix,
    down_bias,
    ffn_gain,
    ffn_shift,
    cotangent,
):
    fl = jnp.float32
    if lax.axis_size(AXIS) == GROUP:
        return fused(
            tokens,
            doc_ids,
            pad_mask,
            (qkv_matrix, out_matrix, up_matrix, down_matrix),
            (
                query_bias,
                value_bias,
                out_bias,
                attn_gain,
                attn_shift,
                down_bias,
                ffn_gain,
                ffn_shift,
                up_bias,
            ),
            cotangent,
        )
    owned_vectors = (
        query_bias,
        value_bias,
        out_bias,
        attn_gain,
        attn_shift,
        down_bias,
        ffn_gain,
        ffn_shift,
        up_bias,
    )
    vectors = vector_rows([v[None] for v in owned_vectors])[0]
    wholes = [
        lax.all_gather(w, AXIS, axis=0, tiled=True)
        for w in (qkv_matrix, out_matrix, up_matrix, down_matrix, vectors)
    ]
    qkv_full, outm_full, upm_full, downm_full, vectors_full = wholes
    vectors_full = vectors_full.reshape((-1,) + vectors.shape)
    (
        qbias_full,
        vbias_full,
        outb_full,
        gain_one,
        shift_one,
        downb_full,
        gain_two,
        shift_two,
        upb_full,
    ) = (vectors_full[:, j, : v.shape[0]].reshape(-1) for j, v in enumerate(owned_vectors))
    qkv_back, outm_back, upm_back, downm_back = qkv_full, outm_full, upm_full, downm_full
    gain_one_back, gain_two_back = gain_one, gain_two
    row_count, model_width = tokens.shape
    head_size = model_width // HEADS
    score_scale = 1.0 / math.sqrt(head_size)
    hidden_width = upm_full.shape[1]
    ratio = hidden_width // model_width
    zero_part = jnp.zeros((model_width,), fl)
    qkv = jnp.dot(tokens, qkv_full, preferred_element_type=fl)
    qkv = (qkv + jnp.concatenate([qbias_full.astype(fl), zero_part, vbias_full.astype(fl)])).astype(
        jnp.bfloat16
    )
    query = qkv[:, :model_width].reshape(row_count, HEADS, head_size)
    key_rows = qkv[:, model_width : 2 * model_width].reshape(row_count, HEADS, head_size)
    value_rows = qkv[:, 2 * model_width :].reshape(row_count, HEADS, head_size)
    positions = jnp.arange(row_count)
    visible = (doc_ids[:, None] == doc_ids[None, :]) & (
        (pad_mask[None, :] == 1) | (positions[:, None] == positions[None, :])
    )
    scores = masked_scores(query, key_rows, visible, score_scale)
    row_max = jnp.max(scores, axis=-1, keepdims=True)
    log_total = row_max + jnp.log(jnp.sum(jnp.exp(scores - row_max), axis=-1, keepdims=True))
    probs_b = jnp.exp(scores - log_total).astype(jnp.bfloat16)
    context = jnp.einsum("hqk,khd->qhd", probs_b, value_rows, preferred_element_type=fl)
    context = context.reshape(row_count, model_width).astype(jnp.bfloat16)
    attn_sum = (
        tokens.astype(fl)
        + jnp.dot(context, outm_full, preferred_element_type=fl)
        + outb_full.astype(fl)
    )
    hidden, normed_one, inverse_one = layer_norm(
        attn_sum, gain_one.astype(fl), shift_one.astype(fl)
    )
    hidden_b = hidden.astype(jnp.bfloat16)
    pre_act = jnp.dot(hidden_b, upm_full, preferred_element_type=fl) + upb_full.astype(fl)
    cdf_part = 0.5 * (1.0 + jax.scipy.special.erf(pre_act * root_half))
    pdf_part = jnp.exp(-0.5 * pre_act * pre_act) * inv_root_two_pi
    activation = (pre_act * cdf_part).astype(jnp.bfloat16)
    ffn_sum = (
        hidden + jnp.dot(activation, downm_full, preferred_element_type=fl) + downb_full.astype(fl)
    )
    normed_out, normed_two, inverse_two = layer_norm(
        ffn_sum, gain_two.astype(fl), shift_two.astype(fl)
    )
    layer_out = normed_out.astype(jnp.bfloat16)
    upstream = cotangent.astype(fl)
    g_gain_two = jnp.sum(upstream * normed_two, axis=0)
    g_shift_two = jnp.sum(upstream, axis=0)
    d_ffn = norm_back(upstream, normed_two, inverse_two, gain_two_back.astype(fl))
    g_down_b = jnp.sum(d_ffn, axis=0)
    d_ffn_b = d_ffn.astype(jnp.bfloat16)
    d_act = jnp.einsum("rd,fd->rf", d_ffn_b, downm_back, preferred_element_type=fl)
    d_pre = d_act * (cdf_part + pre_act * pdf_part)
    g_up_b = jnp.sum(d_pre, axis=0)
    d_pre_b = d_pre.astype(jnp.bfloat16)
    d_hidden = d_ffn + jnp.einsum("rf,df->rd", d_pre_b, upm_back, preferred_element_type=fl)
    g_gain_one = jnp.sum(d_hidden * normed_one, axis=0)
    g_shift_one = jnp.sum(d_hidden, axis=0)
    d_attn = norm_back(d_hidden, normed_one, inverse_one, gain_one_back.astype(fl))
    g_out_b = jnp.sum(d_attn, axis=0)
    d_attn_b = d_attn.astype(jnp.bfloat16)
    d_context = jnp.einsum("re,de->rd", d_attn_b, outm_back, preferred_element_type=fl).astype(
        jnp.bfloat16
    )
    d_qkv, attn_sums = attention_back(qkv, d_context, doc_ids, pad_mask)
    g_qbias, g_vbias = attn_sums[0], attn_sums[1]
    token_grad = d_attn + jnp.einsum("re,de->rd", d_qkv, qkv_back, preferred_element_type=fl)
    sums = vector_rows(
        [
            g.reshape((lax.axis_size(AXIS), -1))
            for g in (
                g_qbias,
                g_vbias,
                g_out_b,
                g_gain_one,
                g_shift_one,
                g_down_b,
                g_gain_two,
                g_shift_two,
                g_up_b,
            )
        ]
    )
    pairs = ((tokens, d_qkv), (context, d_attn_b), (hidden_b, d_pre_b), (activation, d_ffn_b))
    owned = [
        lax.psum_scatter(p, AXIS, scatter_dimension=0, tiled=True)
        for p in [grad_rows(left, right) for left, right in pairs]
        + [sums.reshape((-1, sums.shape[2]))]
    ]
    grad_qkv, grad_outmat, grad_upmat, grad_downmat, vec = owned
    owned_sums = [vec[j, : v.shape[0]] for j, v in enumerate(owned_vectors)]
    return (
        layer_out,
        token_grad,
        grad_qkv,
        owned_sums[0],
        owned_sums[1],
        grad_outmat,
        owned_sums[2],
        owned_sums[3],
        owned_sums[4],
        grad_upmat,
        owned_sums[8],
        grad_downmat,
        owned_sums[5],
        owned_sums[6],
        owned_sums[7],
    )


def solution(mesh):
    placed = (
        P("fsdp", None),
        P("fsdp"),
        P("fsdp"),
        P("fsdp", None),
        P("fsdp"),
        P("fsdp"),
        P("fsdp", None),
        P("fsdp"),
        P("fsdp"),
        P("fsdp"),
        P("fsdp", None),
        P("fsdp"),
        P("fsdp", None),
        P("fsdp"),
        P("fsdp"),
        P("fsdp"),
        P("fsdp", None),
    )
    return jax.shard_map(
        local,
        mesh=mesh,
        in_specs=placed,
        out_specs=(
            P("fsdp", None),
            P("fsdp", None),
            P("fsdp", None),
            P("fsdp"),
            P("fsdp"),
            P("fsdp", None),
            P("fsdp"),
            P("fsdp"),
            P("fsdp"),
            P("fsdp", None),
            P("fsdp"),
            P("fsdp", None),
            P("fsdp"),
            P("fsdp"),
            P("fsdp"),
        ),
        check_vma=False,
    )
```

```python
import functools
import heapq
import math
import types

import jax
import jax.numpy as jnp
from jax import lax
from jax.experimental import pallas as pl
from jax.experimental.pallas import tpu as pltpu
from jax.sharding import PartitionSpec as P

HEADS = 12
AXIS = "fsdp"
MESH_IDS = pl.DeviceIdType.MESH
GROUP = 32


norm_eps = 1e-06
root_half = 0.7071067811865476
inv_root_two_pi = 0.3989422804014327


def layer_norm(values, gain, shift):
    centred = values - jnp.mean(values, axis=-1, keepdims=True)
    inverse = lax.rsqrt(jnp.mean(centred * centred, axis=-1, keepdims=True) + norm_eps)
    normed = centred * inverse
    return (normed * gain + shift, normed, inverse)


def norm_back(upstream, normed, inverse, gain):
    scaled = upstream * gain
    return inverse * (
        scaled
        - jnp.mean(scaled, axis=-1, keepdims=True)
        - normed * jnp.mean(scaled * normed, axis=-1, keepdims=True)
    )


def masked_scores(query, key_rows, visible, score_scale):
    scores = (
        jnp.einsum("qhd,khd->hqk", query, key_rows, preferred_element_type=jnp.float32)
        * score_scale
    )
    return jnp.where(visible[None], scores, -1e30)


def vector_rows(vectors):
    rows = [jnp.pad(v, ((0, 0), (0, 128 - v.shape[1]))) for v in vectors]
    rows = rows + [jnp.zeros_like(rows[0])] * (16 - len(rows))
    return jnp.stack(rows, axis=1)


def attention_back_kernel(
    scale, qkv_ref, back_ref, doc_col, doc_row, pad_row, d_qkv_ref, sums_ref
):
    fl = jnp.float32
    rows, width = back_ref.shape
    size = width // HEADS
    across, down, both = ((1,), (0,)), ((0,), (0,)), ((1,), (1,))

    def dot(a, b, over):
        return lax.dot_general(a, b, (over, ((), ())), preferred_element_type=fl)

    square = (rows, rows)
    same = lax.broadcasted_iota(jnp.int32, square, 0) == lax.broadcasted_iota(
        jnp.int32, square, 1
    )
    visible = (doc_col[...] == doc_row[...]) & ((pad_row[...] == 1) | same)
    for pair in range(HEADS // 2):
        results = []
        for h in (2 * pair, 2 * pair + 1):
            query, key_rows, value_rows = (
                qkv_ref[:, part * width + h * size : part * width + (h + 1) * size]
                for part in range(3)
            )
            back = back_ref[:, h * size : (h + 1) * size]
            scores = jnp.where(visible, dot(query, key_rows, both) * scale, -1e30)
            row_max = jnp.max(scores, axis=-1, keepdims=True)
            total = jnp.sum(jnp.exp(scores - row_max), axis=-1, keepdims=True)
            probs = jnp.exp(scores - (row_max + jnp.log(total)))
            d_value = dot(probs.astype(jnp.bfloat16), back, down)
            d_probs = dot(back, value_rows, both)
            delta = jnp.sum(probs * d_probs, axis=-1, keepdims=True)
            d_scores = (probs * (d_probs - delta) * scale).astype(jnp.bfloat16)
            results.append(
                (dot(d_scores, key_rows, across), dot(d_scores, query, down), d_value)
            )
        for part in range(3):
            block = jnp.concatenate([results[0][part], results[1][part]], axis=1)
            at = pair * 2 * size
            d_qkv_ref[:, part * width + at : part * width + at + 2 * size] = block.astype(
                jnp.bfloat16
            )
            if part != 1:
                row = part // 2
                sums_ref[row : row + 1, at : at + 2 * size] = jnp.sum(
                    block, axis=0, keepdims=True
                )


def attention_back(qkv, d_context, doc_ids, pad_mask):
    rows, width = d_context.shape
    return pl.pallas_call(
        functools.partial(attention_back_kernel, 1.0 / math.sqrt(width // HEADS)),
        out_shape=(
            jax.ShapeDtypeStruct(qkv.shape, jnp.bfloat16),
            jax.ShapeDtypeStruct((2, width), jnp.float32),
        ),
        compiler_params=pltpu.CompilerParams(vmem_limit_bytes=24 * 1024 * 1024),
        name="attention_back",
    )(qkv, d_context, doc_ids[:, None], doc_ids[None], pad_mask[None])


def grad_rows(left, right):
    return jnp.einsum("ra,rb->ab", left, right, preferred_element_type=jnp.float32)


X, Y, Z1, Z2 = 0, 1, 2, 3
GATHER_ORDERS = (
    (Z2, Z1, Y, X),
    (Z2, Z1, X, Y),
    (Y, Z2, Z1, X),
    (Z2, Z1, Y, X),
    (Z2, Z1, Y),
    (Z2, Z1, Y),
    (Z2, Z1, Y, X),
)
SCATTER_ORDERS = (
    (X, Z1, Z2, Y),
    (Y, X, Z1, Z2),
    (X, Y, Z1, Z2),
    (X, Y, Z1, Z2),
    (Y, Z1, Z2),
    (Y, Z1, Z2),
    (Y, Z1, Z2, X),
)
GATHER_FIRST = (0, 0, 2, 2, 4, 5, 0)
SCATTER_FIRST = (3, 0, 2, 1, 2, 3, 2)
ADDS_BETWEEN = 2
ADD_US = (0.15, 0.15, 0.15, 0.15, 0.3, 0.3, 0.08)
PAIRS = 16
PIECES = (16, 16, 16, 16, 8, 8, 16)
PIECE_ROWS = (48, 48, 48, 48, 96, 192, 32)
PIECE_COLS = (384, 384, 384, 384, 768, 384, 128)
OUT, UP, DOWN, VEC = 3, 4, 5, 6
QUAD = 4
COUNT = 7
HOPS = {X: ((0, 1),), Y: ((1, 1),), Z1: ((2, 1),), Z2: ((2, 1), (3, 2))}
LINK_BYTES_PER_US = 46e3
HOP_US = 1.0
CORE_BYTES_PER_US = 600e3
BACKLOG_US = 1.5
FUSED_VMEM = 58 * 1024 * 1024


class Plan:
    def __init__(self):
        self.now = 0.0
        self.free = {}
        self.pending = []
        self.waiting = []
        self.here = set()
        self.seq = 0

    def travel(self, dim, size, key):
        if dim is None:
            us, hops = size / CORE_BYTES_PER_US, ((4, 1),)
        else:
            us, hops = size / LINK_BYTES_PER_US, HOPS[dim]
        begin = max([self.now] + [self.free.get(link, 0.0) for link, _ in hops])
        end = begin
        for link, cost in hops:
            self.free[link] = begin + cost * us
            end = max(end, begin + cost * us)
        self.seq += 1
        heapq.heappush(self.pending, (end + HOP_US, self.seq, key))

    def ask(self, first, dim, size, key, start):
        self.seq += 1
        self.waiting.append((first, self.seq, dim, size, key, start))
        self.waiting.sort(key=lambda entry: entry[:2])

    def pump(self):
        left = []
        for entry in self.waiting:
            _, _, dim, size, key, start = entry
            if max(self.free.get(link, 0.0) for link, _ in HOPS[dim]) - self.now < BACKLOG_US:
                start()
                self.travel(dim, size, key)
            else:
                left.append(entry)
        self.waiting = left


def subsets(order, step):
    blocks = [0]
    for b in reversed(order[step + 1 :]):
        blocks = [r | (1 << b) for r in blocks] + blocks
    return blocks


def dot(a, b, over=((1,), (0,))):
    return lax.dot_general(a, b, (over, ((), ())), preferred_element_type=jnp.float32)


ROWS_BOTH, COLS_BOTH = ((0,), (0,)), ((1,), (1,))

SIBLING_COPIES = 58
INPUTS, OUTPUTS = 17, 7


def stage_shape(k):
    if k == UP:
        return ((QUAD, 32, PIECE_COLS[k]), jnp.bfloat16)
    return (((PIECE_ROWS[k] // 2 + 15) // 16 * 16, PIECE_COLS[k]), jnp.bfloat16)


def scratch_of(rows, width, hidden):
    fl, bf = jnp.float32, jnp.bfloat16
    both, half, quad = 2 * rows, width // 2, QUAD * rows
    hhalf, hquarter = hidden // 2, hidden // 4
    lists = []
    for shape_of in (
        lambda k: ((PIECES[k] * PIECE_ROWS[k], PIECE_COLS[k]), bf),
        lambda k: ((PIECES[k] * PIECE_ROWS[k], PIECE_COLS[k]), bf),
        lambda k: ((PIECES[k] - 1, PIECE_ROWS[k], PIECE_COLS[k]), bf),
        stage_shape,
        stage_shape,
        lambda k: ((PIECE_ROWS[k], PIECE_COLS[k]), fl),
    ):
        lists += [shape_of(k) for k in range(COUNT)]
    named = dict(
        peer_vec=((PAIRS * PIECE_ROWS[VEC], PIECE_COLS[VEC]), bf),
        stage_vec=((PAIRS * PIECE_ROWS[VEC], PIECE_COLS[VEC]), bf),
        tok=((both, width), bf),
        marks=((2, 8, rows), fl),
        vec32=((PAIRS * 32, 128), fl),
        vecs=((16, width), fl),
        upb=((8, hquarter), fl),
        qkv=((both, 3 * half), bf),
        probs=((HEADS, rows, rows), fl),
        ctx=((both, width), bf),
        proj_s=((rows, half), fl),
        proj_r=((rows, half), fl),
        proj_o=((rows, half), fl),
        hid=((rows, width), fl),
        n1=((rows, width), fl),
        i1=((rows, 128), fl),
        hb=((quad, width), bf),
        act=((quad, hhalf), bf),
        fac=((quad, hquarter), fl),
        ffn_s=((rows, half), fl),
        ffn_r=((rows, half), fl),
        ffn_o=((both, half), fl),
        ffn_xs=((both, half), bf),
        ffn_xr=((both, half), bf),
        dff=((rows, width), fl),
        dfb=((quad, width), bf),
        dact_s=((quad, hquarter), fl),
        dact_r=((quad, hquarter), fl),
        dact_o=((quad, hquarter), fl),
        dpre=((quad, hquarter), bf),
        dhid_s=((both, width), fl),
        dhid_r=((both, width), fl),
        dhid_o=((both, width), fl),
        dhid_xs=((rows, width), bf),
        dhid_xr=((rows, width), bf),
        dat=((rows, width), fl),
        datb=((both, width), bf),
        dctx_s=((both, half), fl),
        dctx_r=((both, half), fl),
        dctx_o=((both, half), fl),
        dctx=((both, half), bf),
        dqkv=((both, 3 * half), bf),
        tg_s=((rows, width), fl),
        tg_r=((rows, width), fl),
        tg_o=((rows, width), fl),
        sums=((16, width), fl),
        upsum=((8, hquarter), fl),
        mixed=((width // GROUP, hidden), fl),
        mixed_qkv=((width // GROUP, 3 * width), fl),
    )
    return lists, named


def layer_kernel(names, *refs):
    refs = list(refs)

    def take(count):
        taken, refs[:count] = refs[:count], []
        return taken

    R = types.SimpleNamespace()
    far_in, far_out, near_in, near_out = take(INPUTS), take(OUTPUTS), take(INPUTS), take(OUTPUTS)
    R.tokens, R.doc, R.pad, R.cotangent = near_in[:4]
    R.w, R.v = near_in[4:8], near_in[8:]
    R.layer_out, R.token_grad, R.gv = near_out[:3]
    R.g = near_out[3:]
    R.whole, R.part, R.land, R.stage, R.peer, R.fin = (take(COUNT) for _ in range(6))
    vars(R).update(zip(names, take(len(names))))
    sib_send, sib_recv, g_send, g_recv, s_send, s_recv, in_sem, out_sem = refs
    loads = [
        pltpu.make_async_copy(far, near, in_sem.at[i])
        for i, (far, near) in enumerate(zip(far_in, near_in))
    ]
    for i in (4, *range(8, 17), 5, 6, 7, 0, 1, 2, 3):
        loads[i].start()
    stores = [
        pltpu.make_async_copy(near, far, out_sem.at[i])
        for i, (far, near) in enumerate(zip(far_out, near_out))
    ]
    fl, bf = jnp.float32, jnp.bfloat16
    rows, width = R.tokens.shape
    hidden = R.w[2].shape[1]
    half, hhalf, hquarter = width // 2, hidden // 2, hidden // 4
    size = width // HEADS
    scale = 1.0 / math.sqrt(size)
    me = lax.axis_index(AXIS)
    core = lax.rem(me, 2)
    pair = lax.div(me, 2)
    bits = [lax.rem(lax.div(pair, 1 << b), 2) for b in range(4)]
    sibling = me + 1 - 2 * core
    is_first = core == 0

    def pair_of(r):
        p = pair
        for b in range(4):
            if r >> b & 1:
                p = p + (1 << b) * (1 - 2 * bits[b])
        return p

    def quad_of(r):
        q = lax.div(pair, 2)
        for b in range(1, 4):
            if r >> b & 1:
                q = q + (1 << (b - 1)) * (1 - 2 * bits[b])
        return q

    def device_along(b):
        return me + (2 << b) * (1 - 2 * bits[b])

    def by_core(step, which=None):
        at = core if which is None else 1 - core
        return pl.multiple_of(at * step, step)

    own_rows, sib_rows = pl.ds(by_core(rows), rows), pl.ds(by_core(rows, 1), rows)
    own_half, sib_half = pl.ds(by_core(half), half), pl.ds(by_core(half, 1), half)
    own_hq, sib_hq = pl.ds(by_core(hquarter), hquarter), pl.ds(by_core(hquarter, 1), hquarter)
    x_at = bits[X]
    across = device_along(X)
    diagonal = across + 1 - 2 * core
    member = 2 * x_at + core

    def quad_rows(other_x, other_core, count=rows, skip=0):
        at = 2 * (1 - x_at if other_x else x_at) + (1 - core if other_core else core)
        return pl.ds(pl.multiple_of(at * rows + skip, 64), count)

    def chip_rows(other_x):
        return pl.ds(pl.multiple_of((1 - x_at if other_x else x_at) * 2 * rows, 128), 2 * rows)


    barrier = pltpu.get_barrier_semaphore()
    for other in [sibling, diagonal] + [device_along(b) for b in range(4)]:
        pl.semaphore_signal(barrier, inc=1, device_id=(other,), device_id_type=MESH_IDS)
    pl.semaphore_wait(barrier, 6)

    plan = Plan()
    sib = {}
    sent = []

    def to_sibling(i, src, dst, device=None):
        copy = pltpu.make_async_remote_copy(
            src_ref=src,
            dst_ref=dst,
            send_sem=sib_send.at[i],
            recv_sem=sib_recv.at[i],
            device_id=(sibling if device is None else device,),
            device_id_type=MESH_IDS,
        )
        copy.start()
        sib[i] = copy
        sent.append(copy)
        plan.travel(None if device is None else X, math.prod(src.shape) * src.dtype.itemsize, (None, i))

    def arrived(i):
        sib.pop(i).wait_recv()

    def side_by_side(own, other):
        return jnp.concatenate(
            [jnp.where(is_first, own, other), jnp.where(is_first, other, own)], axis=1
        )

    def shard_half(k, mine):
        which = core if mine else 1 - core
        if k < 3:
            cols = [
                R.w[0][:, pl.ds(pl.multiple_of(p * width + which * half + k * 128, 128), 128)]
                for p in range(3)
            ]
            return jnp.concatenate([c.astype(fl) for c in cols], axis=1)
        cols = PIECE_COLS[k]
        ref = R.w[1] if k == OUT else R.w[3]
        return ref[:, pl.ds(by_core(cols, None if mine else 1), cols)].astype(fl)

    def padded(value):
        short = -value.shape[0] % 16
        if short:
            value = jnp.concatenate([value, jnp.zeros((short, value.shape[1]), fl)], axis=0)
        return value.astype(bf)

    for load in loads[4:]:
        load.wait()
    R.vec32[pl.ds(0, 16), :] = jnp.zeros((16, 128), fl)
    for j in range(9):
        v = R.v[j]
        R.vec32[j : j + 1, 0 : v.shape[1]] = v[...].astype(fl)
    R.stage[VEC][...] = R.vec32[pl.ds(0, 16), :].astype(bf)
    def quarter(q):
        blocks = []
        for j in range(4):
            at = (q % 2) * hhalf + 2 * j * 192 + (q // 2) * 192
            blocks.append(R.w[2][:, at : at + 192].astype(fl))
        return jnp.concatenate(blocks, axis=1)

    for k in (0, VEC, 1, 2, OUT, DOWN):
        if k != VEC:
            R.stage[k][...] = padded(shard_half(k, False))
        to_sibling(50 + k, R.stage[k], R.peer[k])
    for q in range(QUAD):
        R.stage[UP][q] = padded(quarter(q))
    for i, device, q in (
        (54, None, member + 1 - 2 * core),
        (25, across, member + 2 - 4 * x_at),
        (26, diagonal, 3 - member),
    ):
        to_sibling(i, R.stage[UP].at[q], R.peer[UP].at[member], device)
    for load in loads[:4]:
        load.wait()
    to_sibling(5, R.tokens, R.tok.at[own_rows])
    own_marks = jnp.concatenate(
        [R.doc[...].astype(fl), R.pad[...].astype(fl), jnp.zeros((6, rows), fl)], axis=0
    )
    R.marks[core] = own_marks
    to_sibling(6, R.marks.at[core], R.marks.at[core])
    R.tok[own_rows, :] = R.tokens[...]

    plan.now = 3.0
    piece_bytes = [2 * PIECE_ROWS[k] * PIECE_COLS[k] for k in range(COUNT)]
    done = [1] * COUNT

    def piece_at(k, r):
        n = PIECE_ROWS[k]
        place = pair_of(r) if PIECES[k] == PAIRS else quad_of(r)
        return pl.ds(pl.multiple_of(place * n, n), n)

    def gather_move(k, r, b):
        at = piece_at(k, r)
        slot = r | (1 << b)
        copy = pltpu.make_async_remote_copy(
            src_ref=R.whole[k].at[at],
            dst_ref=R.whole[k].at[at],
            send_sem=g_send.at[k, slot],
            recv_sem=g_recv.at[k, slot],
            device_id=(device_along(b),),
            device_id_type=MESH_IDS,
        )
        sent.append(copy)
        plan.ask(GATHER_FIRST[k], b, piece_bytes[k], (True, k, slot, b), copy.start)

    for k in (0, VEC, 1, 2, OUT, DOWN, UP):
        arrived(50 + k)
        if k == UP:
            R.peer[UP][member] = R.stage[UP][member]
            arrived(25)
            arrived(26)
            rows_in = [R.peer[UP][q].astype(fl)[: width // GROUP] for q in range(QUAD)]
        else:
            mine = R.vec32[pl.ds(0, 16), :] if k == VEC else shard_half(k, True)
            theirs = R.peer[k][...].astype(fl)[: mine.shape[0]]
            rows_in = [jnp.where(is_first, mine, theirs), jnp.where(is_first, theirs, mine)]
        R.whole[k][piece_at(k, 0), :] = jnp.concatenate(rows_in, axis=0).astype(bf)
        for b in GATHER_ORDERS[k]:
            gather_move(k, 0, b)
        plan.pump()

    def on_gather(k, r, b):
        here = R.whole[k].at[piece_at(k, r)]
        pltpu.make_async_remote_copy(
            src_ref=here,
            dst_ref=here,
            send_sem=g_send.at[k, r],
            recv_sem=g_recv.at[k, r],
            device_id=(device_along(b),),
            device_id_type=MESH_IDS,
        ).wait_recv()
        order = GATHER_ORDERS[k]
        for later in order[order.index(b) + 1 :]:
            gather_move(k, r, later)
        done[k] += 1

    slot_of = []
    for k in range(COUNT):
        table = {}
        for step in range(len(SCATTER_ORDERS[k])):
            for r in subsets(SCATTER_ORDERS[k], step):
                table[step, r] = len(table)
        slot_of.append(table)
    copies = {}

    def held(k, step, r):
        if step < 0:
            return R.part[k].at[piece_at(k, r)]
        return R.land[k].at[slot_of[k][step, r]]

    def scatter_move(k, step, r):
        b = SCATTER_ORDERS[k][step]
        low = r & ~(1 << b)
        slot = slot_of[k][step, low]
        copy = pltpu.make_async_remote_copy(
            src_ref=held(k, step - 1, r),
            dst_ref=R.land[k].at[slot],
            send_sem=s_send.at[k, slot],
            recv_sem=s_recv.at[k, slot],
            device_id=(device_along(b),),
            device_id_type=MESH_IDS,
        )
        sent.append(copy)
        copies[k, step, low] = copy
        plan.ask(SCATTER_FIRST[k], b, piece_bytes[k], (False, k, step, low), copy.start)

    def scatter_start(k):
        order = SCATTER_ORDERS[k]
        for r in subsets(order, 0):
            scatter_move(k, 0, r | (1 << order[0]))

    def finish(k):
        if k == VEC:
            R.gv[...] = R.fin[VEC][pl.ds(by_core(16), 16), :]
            stores[2].start()
            return
        if k == UP:
            at = pl.ds(pl.multiple_of(x_at * hhalf + core * hquarter, 128), hquarter)
            n = PIECE_ROWS[UP] // QUAD

            def share(q):
                return R.fin[UP].at[pl.ds(pl.multiple_of(q * n, n), n)]

            for i, device, q in (
                (22, None, member + 1 - 2 * core),
                (27, across, member + 2 - 4 * x_at),
                (28, diagonal, 3 - member),
            ):
                to_sibling(i, share(q), R.mixed.at[:, at], device)
            R.mixed[:, at] = share(member)[...]
            return
        n = PIECE_ROWS[k] // 2
        mine = R.fin[k].at[pl.ds(by_core(n), n)]
        theirs = R.fin[k].at[pl.ds(by_core(n, 1), n)]
        if k < 3:
            into, at = R.mixed_qkv, pl.ds(pl.multiple_of((3 * core + k) * 384, 384), 384)
        else:
            into, at = R.g[1 if k == OUT else 3], own_half
        to_sibling(18 + k, theirs, into.at[:, at])
        into[:, at] = mine[...]

    summed = set()
    early = {}

    def on_scatter(k, step, r):
        if step and (k, step - 1, r) not in summed:
            early[k, step - 1, r] = step
            return
        summed.add((k, step, r))
        plan.now += ADD_US[k]
        add_piece(k, step, r)
        if (k, step, r) in early:
            on_scatter(k, early[k, step, r], r)

    def add_piece(k, step, r):
        copies[k, step, r].wait_recv()
        order = SCATTER_ORDERS[k]
        before, now = held(k, step - 1, r), held(k, step, r)
        total = now[...].astype(fl) + before[...].astype(fl)
        if step == len(order) - 1:
            R.fin[k][...] = total
            finish(k)
            return
        now[...] = total.astype(bf)
        if r >> order[step + 1] & 1:
            scatter_move(k, step + 1, r)

    def column_of(n, period):
        return jnp.floor((n + 0.5) * (1.0 / period))

    def pick(count, period):
        n = lax.broadcasted_iota(jnp.int32, (128, count), 1).astype(fl)
        i = lax.broadcasted_iota(jnp.int32, (128, count), 0).astype(fl)
        return jnp.where(n - period * column_of(n, period) == i, 1.0, 0.0).astype(bf)

    def owner_is(count, period):
        n = lax.broadcasted_iota(jnp.int32, (GROUP, count), 1).astype(fl)
        d = lax.broadcasted_iota(jnp.int32, (GROUP, count), 0).astype(fl)
        return column_of(n, period) == d

    small, large = width // GROUP, hidden // GROUP

    def unit_owner():
        n = lax.broadcasted_iota(jnp.int32, (GROUP, hquarter), 1).astype(fl)
        d = lax.broadcasted_iota(jnp.int32, (GROUP, hquarter), 0).astype(fl)
        block = column_of(n, large)
        quad = column_of(block, 2)
        first = (16 * core + 2 * x_at).astype(fl)
        return first + 4.0 * quad + (block - 2.0 * quad) == d

    def task_vectors():
        R.vec32[...] = R.whole[VEC][...].astype(fl)
        chosen, owner = pick(width, small), owner_is(width, small)
        for j in range(8):
            v = R.vec32[pl.ds(j, GROUP, stride=16), :].astype(bf)
            R.vecs[j : j + 1, :] = jnp.sum(
                jnp.where(owner, dot(v, chosen), 0.0), axis=0, keepdims=True
            )
        v = R.vec32[pl.ds(8, GROUP, stride=16), :].astype(bf)
        R.upb[0:1, :] = jnp.sum(
            jnp.where(unit_owner(), dot(v, pick(hquarter, large)), 0.0),
            axis=0,
            keepdims=True,
        )

    def vec(j):
        return R.vecs[j : j + 1, :]

    def task_qkv(two):
        if two == 0:
            arrived(5)
            arrived(6)
        value = dot(R.tok[...], R.whole[two][...])
        for p in range(3):
            block = value[:, p * 128 : (p + 1) * 128]
            if p != 1:
                at = pl.ds(pl.multiple_of(core * half + two * 128, 128), 128)
                block = block + R.vecs[p // 2 : p // 2 + 1, at]
            R.qkv[:, two * 384 + p * 128 : two * 384 + (p + 1) * 128] = block.astype(bf)

    def seen(b):
        doc, pad = R.marks[b, 0:1, :], R.marks[b, 1:2, :]
        square = (rows, rows)
        wide = jnp.broadcast_to(doc, square)
        same = lax.broadcasted_iota(jnp.int32, square, 0) == lax.broadcasted_iota(
            jnp.int32, square, 1
        )
        return (wide.T == wide) & ((jnp.broadcast_to(pad, square) == 1.0) | same)

    def head_of(b, h):
        at = b * rows
        first = h // 2 * 384 + h % 2 * size
        return [
            R.qkv[at : at + rows, first + p * 128 : first + p * 128 + size] for p in range(3)
        ]

    def task_attention(b, two):
        visible = seen(b)
        found = []
        for h in (2 * two, 2 * two + 1):
            query, key_rows, value_rows = head_of(b, h)
            scores = jnp.where(visible, dot(query, key_rows, COLS_BOTH) * scale, -1e30)
            row_max = jnp.max(scores, axis=-1, keepdims=True)
            total = jnp.sum(jnp.exp(scores - row_max), axis=-1, keepdims=True)
            probs = jnp.exp(scores - (row_max + jnp.log(total)))
            R.probs[b * (HEADS // 2) + h] = probs
            found.append(dot(probs.astype(bf), value_rows))
        at = pl.ds(pl.multiple_of(core * half + two * 2 * size, 128), 2 * size)
        R.ctx[pl.ds(b * rows, rows), at] = jnp.concatenate(found, axis=1).astype(bf)
        if b == 1:
            to_sibling((7, 45, 46)[two], R.ctx.at[:, at], R.ctx.at[:, at])

    def task_project():
        arrived(7)
        arrived(45)
        arrived(46)
        R.proj_s[...] = dot(R.ctx[sib_rows, :], R.whole[OUT][...])
        to_sibling(8, R.proj_s, R.proj_r)
        R.proj_o[...] = dot(R.ctx[own_rows, :], R.whole[OUT][...])

    def norm(values):
        centred = values - jnp.mean(values, axis=-1, keepdims=True)
        inverse = lax.rsqrt(jnp.mean(centred * centred, axis=-1, keepdims=True) + norm_eps)
        return centred * inverse, inverse

    def task_norm_one():
        arrived(8)
        attn = (
            R.tokens[...].astype(fl)
            + side_by_side(R.proj_o[...], R.proj_r[...])
            + vec(2)
        )
        normed, inverse = norm(attn)
        hid = normed * vec(3) + vec(4)
        R.n1[...] = normed
        R.i1[...] = jnp.broadcast_to(inverse, (rows, 128))
        R.hid[...] = hid
        R.hb[quad_rows(0, 0), :] = hid.astype(bf)
        spread_rows(R.hb, 9, 29)

    tile = 384

    def spread_rows(ref, i, first):
        for skip in (0, 1):
            at = quad_rows(0, 0, rows // 2, skip * (rows // 2))
            to_sibling(first + skip, ref.at[at], ref.at[at], across)
        at = quad_rows(0, 0)
        to_sibling(i, ref.at[at], ref.at[at])

    def pass_on(ref, first):
        for skip in (0, 1):
            arrived(first + skip)
            at = quad_rows(1, 0, rows // 2, skip * (rows // 2))
            to_sibling(first + 2 + skip, ref.at[at], ref.at[at])

    def task_up(other):
        if other:
            arrived(31)
            arrived(32)
        else:
            arrived(9)
        to = chip_rows(other)

        def body(t, carry):
            at = pl.ds(pl.multiple_of(t * tile, tile), tile)
            pre = dot(R.hb[to, :], R.whole[UP][:, at]) + R.upb[0:1, at]
            cdf = 0.5 * (1.0 + lax.erf(pre * root_half))
            pdf = jnp.exp(-0.5 * pre * pre) * inv_root_two_pi
            R.fac[to, at] = cdf + pre * pdf
            R.act[to, pl.ds(pl.multiple_of(core * hquarter + t * tile, tile), tile)] = (
                pre * cdf
            ).astype(bf)
            return carry

        lax.fori_loop(0, hquarter // tile, body, 0)
        to_sibling(33 + other, R.act.at[to, own_hq], R.act.at[to, own_hq])

    def task_ffn():
        arrived(33)
        arrived(34)
        for i, other_core in ((35, 1), (36, 0)):
            at = pl.ds(by_core(rows, 1 if other_core else None), rows)
            R.ffn_xs[at, :] = dot(R.act[quad_rows(1, other_core), :], R.whole[DOWN][...]).astype(bf)
            to_sibling(i, R.ffn_xs.at[at], R.ffn_xr.at[at], across)
        R.ffn_o[...] = dot(R.act[chip_rows(0), :], R.whole[DOWN][...])

    def task_ffn_sum():
        arrived(35)
        R.ffn_s[...] = R.ffn_o[sib_rows, :] + R.ffn_xr[sib_rows, :].astype(fl)
        to_sibling(11, R.ffn_s, R.ffn_r)
        arrived(36)

    def back_of_norm(upstream, normed, inverse, gain):
        scaled = upstream * gain
        return inverse * (
            scaled
            - jnp.mean(scaled, axis=-1, keepdims=True)
            - normed * jnp.mean(scaled * normed, axis=-1, keepdims=True)
        )

    def add_sum(j, values):
        R.sums[j : j + 1, :] = jnp.sum(values, axis=0, keepdims=True)

    def task_norm_two():
        arrived(11)
        mine = R.ffn_o[own_rows, :] + R.ffn_xr[own_rows, :].astype(fl)
        total = R.hid[...] + side_by_side(mine, R.ffn_r[...]) + vec(5)
        normed, inverse = norm(total)
        R.layer_out[...] = (normed * vec(6) + vec(7)).astype(bf)
        stores[0].start()
        upstream = R.cotangent[...].astype(fl)
        d_ffn = back_of_norm(upstream, normed, inverse, vec(6))
        R.dff[...] = d_ffn
        R.dfb[quad_rows(0, 0), :] = d_ffn.astype(bf)
        spread_rows(R.dfb, 12, 37)
        add_sum(6, upstream * normed)
        add_sum(7, upstream)
        add_sum(5, d_ffn)

    def task_grad_down():
        arrived(39)
        arrived(40)

        def body(t, carry):
            at = pl.ds(pl.multiple_of(t * tile, tile), tile)
            R.part[DOWN][at, :] = dot(R.act[:, at], R.dfb[:, own_half], ROWS_BOTH).astype(bf)
            return carry

        lax.fori_loop(0, hhalf // tile, body, 0)
        scatter_start(DOWN)

    def task_d_act(other):
        if not other:
            arrived(12)
        at = chip_rows(other)
        right = R.dfb[at, own_half]
        R.dact_s[at, :] = dot(right, R.whole[DOWN][sib_hq, :], COLS_BOTH)
        to_sibling(41 + other, R.dact_s.at[at], R.dact_r.at[at])
        R.dact_o[at, :] = dot(right, R.whole[DOWN][own_hq, :], COLS_BOTH)

    def task_d_pre():
        arrived(41)
        arrived(42)

        def body(t, carry):
            at = pl.ds(pl.multiple_of(t * tile, tile), tile)
            value = (R.dact_o[:, at] + R.dact_r[:, at]) * R.fac[:, at]
            R.upsum[0:1, at] = jnp.sum(value, axis=0, keepdims=True)
            R.dpre[:, at] = value.astype(bf)
            return carry

        lax.fori_loop(0, hquarter // tile, body, 0)

    def task_d_hidden():
        for i, other_x in ((14, 1), (43, 0)):
            at = pl.ds(other_x * rows, rows)
            R.dhid_s[at, :] = dot(R.dpre[quad_rows(other_x, 1), :], R.whole[UP][...], COLS_BOTH)
            to_sibling(i, R.dhid_s.at[at], R.dhid_r.at[at])
        for other_x in (1, 0):
            R.dhid_o[pl.ds(other_x * rows, rows), :] = dot(
                R.dpre[quad_rows(other_x, 0), :], R.whole[UP][...], COLS_BOTH
            )

    def task_d_hidden_sum():
        arrived(14)
        at = pl.ds(rows, rows)
        R.dhid_xs[...] = (R.dhid_o[at, :] + R.dhid_r[at, :]).astype(bf)
        to_sibling(44, R.dhid_xs, R.dhid_xr, across)

    def task_grad_up():
        def body(t, carry):
            at = pl.ds(pl.multiple_of(t * tile, tile), tile)
            R.part[UP][:, at] = dot(R.hb[...], R.dpre[:, at], ROWS_BOTH).astype(bf)
            return carry

        lax.fori_loop(0, hquarter // tile, body, 0)
        scatter_start(UP)

    def task_norm_one_back():
        arrived(43)
        arrived(44)
        at = pl.ds(0, rows)
        d_hid = R.dff[...] + R.dhid_o[at, :] + R.dhid_r[at, :] + R.dhid_xr[...].astype(fl)
        normed = R.n1[...]
        d_attn = back_of_norm(d_hid, normed, R.i1[:, 0:1], vec(3))
        R.dat[...] = d_attn
        R.datb[own_rows, :] = d_attn.astype(bf)
        to_sibling(15, R.datb.at[own_rows], R.datb.at[own_rows])
        add_sum(3, d_hid * normed)
        add_sum(4, d_hid)
        add_sum(2, d_attn)

    def task_d_context():
        arrived(15)
        right = R.datb[:, own_half]
        R.dctx_s[...] = dot(right, R.whole[OUT][sib_half, :], COLS_BOTH)
        to_sibling(16, R.dctx_s, R.dctx_r)
        R.dctx_o[...] = dot(right, R.whole[OUT][own_half, :], COLS_BOTH)

    def task_grad_out():
        R.part[OUT][...] = dot(R.ctx[...], R.datb[:, own_half], ROWS_BOTH).astype(bf)
        scatter_start(OUT)

    def task_d_context_sum():
        arrived(16)
        R.dctx[...] = (R.dctx_o[...] + R.dctx_r[...]).astype(bf)

    bias_sums = {}

    def task_attention_back(b, two):
        found = []
        at = b * rows
        for h in (2 * two, 2 * two + 1):
            query, key_rows, value_rows = head_of(b, h)
            back = R.dctx[at : at + rows, h * size : (h + 1) * size]
            probs = R.probs[b * (HEADS // 2) + h]
            d_value = dot(probs.astype(bf), back, ROWS_BOTH)
            d_probs = dot(back, value_rows, COLS_BOTH)
            delta = jnp.sum(probs * d_probs, axis=-1, keepdims=True)
            d_scores = (probs * (d_probs - delta) * scale).astype(bf)
            found.append((dot(d_scores, key_rows), dot(d_scores, query, ROWS_BOTH), d_value))
        for p in range(3):
            block = jnp.concatenate([found[0][p], found[1][p]], axis=1)
            cols = two * 384 + p * 128
            R.dqkv[at : at + rows, cols : cols + 2 * size] = block.astype(bf)
            if p != 1:
                total = jnp.sum(block, axis=0, keepdims=True)
                if b == 0:
                    bias_sums[p, two] = total
                else:
                    to = pl.ds(pl.multiple_of(core * half + two * 2 * size, 128), 2 * size)
                    R.sums[p // 2 : p // 2 + 1, to] = total + bias_sums[p, two]

    def task_clear_sums():
        R.sums[...] = jnp.zeros(R.sums.shape, fl)

    def task_grad_qkv(two):
        at = pl.ds(two * 384, 384)
        R.part[two][...] = dot(R.tok[...], R.dqkv[:, at], ROWS_BOTH).astype(bf)
        scatter_start(two)

    def through_qkv(at):
        return sum(
            dot(R.dqkv[at, pl.ds(two * 384, 384)], R.whole[two][...], COLS_BOTH)
            for two in range(3)
        )

    def task_token_grad():
        R.tg_s[...] = through_qkv(sib_rows)
        to_sibling(17, R.tg_s, R.tg_r)
        R.tg_o[...] = R.dat[...] + through_qkv(own_rows)

    def task_sums():
        chosen, owner = pick(width, small), owner_is(width, small)
        R.vec32[...] = jnp.zeros(R.vec32.shape, fl)
        for j in range(8):
            spread = jnp.where(owner, R.sums[j : j + 1, :], 0.0).astype(bf)
            R.vec32[pl.ds(j, GROUP, stride=16), :] = dot(spread, chosen, COLS_BOTH)
        spread = jnp.where(unit_owner(), R.upsum[0:1, :], 0.0).astype(bf)
        R.vec32[pl.ds(8, GROUP, stride=16), :] = dot(spread, pick(hquarter, large), COLS_BOTH)
        R.stage_vec[...] = R.vec32[...].astype(bf)
        to_sibling(24, R.stage_vec, R.peer_vec)

    def task_sums_send():
        arrived(24)
        R.part[VEC][...] = (R.vec32[...] + R.peer_vec[...].astype(fl)).astype(bf)
        scatter_start(VEC)

    def task_token_grad_sum():
        arrived(17)
        R.token_grad[...] = R.tg_o[...] + R.tg_r[...]
        stores[1].start()

    call = functools.partial
    tasks = [(task_clear_sums, (), (), 0.1), (task_vectors, (VEC,), (), 0.6)]
    for two in range(3):
        tasks += [(call(task_qkv, two), (two,), (5, 6), 0.4)]
        tasks += [(call(task_attention, b, two), (), (), 0.9) for b in range(2)]
    tasks += [
        (task_project, (OUT,), (7, 45, 46), 1.0),
        (task_norm_one, (), (8,), 1.0),
        (call(task_up, 0), (UP,), (9,), 1.8),
        (call(pass_on, R.hb, 29), (), (29, 30), 0.2),
        (call(task_up, 1), (), (31, 32), 1.8),
        (task_ffn, (DOWN,), (33, 34), 1.5),
        (task_ffn_sum, (), (35, 36), 0.4),
        (task_norm_two, (), (11,), 1.2),
        (call(task_d_act, 0), (), (12,), 1.2),
        (call(pass_on, R.dfb, 37), (), (37, 38), 0.2),
        (task_grad_down, (), (39, 40), 1.7),
        (call(task_d_act, 1), (), (), 1.2),
        (task_d_pre, (), (41, 42), 0.6),
        (task_d_hidden, (), (), 1.5),
        (task_d_hidden_sum, (), (14,), 0.3),
        (task_grad_up, (), (), 1.0),
        (task_norm_one_back, (), (43, 44), 1.0),
        (task_d_context, (), (15,), 0.7),
        (task_grad_out, (), (), 0.5),
        (task_d_context_sum, (), (16,), 0.2),
    ]
    for two in range(3):
        tasks += [(call(task_attention_back, b, two), (), (), 0.75) for b in range(2)]
        tasks += [(call(task_grad_qkv, two), (), (), 0.4)]
    tasks += [
        (task_sums, (), (), 0.7),
        (task_token_grad, (), (), 1.0),
        (task_sums_send, (), (24,), 0.3),
        (task_token_grad_sum, (), (17,), 0.3),
    ]
    late, credit = [], 0
    while tasks or plan.pending or plan.waiting or late:
        plan.pump()
        while plan.pending and plan.pending[0][0] <= plan.now and not plan.pending[0][2][0]:
            key = heapq.heappop(plan.pending)[2]
            if key[0] is None:
                plan.here.add(key[1])
            else:
                late.append(key)
        ready = bool(tasks) and (
            all(done[k] == PIECES[k] for k in tasks[0][1]) and plan.here.issuperset(tasks[0][2])
        )
        if plan.pending and plan.pending[0][2][0] and plan.pending[0][0] <= plan.now:
            plan.now += 0.1
            on_gather(*heapq.heappop(plan.pending)[2][1:])
        elif late and (not ready or credit > 0):
            credit -= 1
            on_scatter(*late.pop(0)[1:])
        elif ready:
            task, _, _, cost = tasks.pop(0)
            plan.now += cost
            credit = ADDS_BETWEEN
            task()
        elif plan.pending:
            plan.now = max(plan.now, plan.pending[0][0])
        else:
            plan.now += 0.5
    for k, parts in ((3, (18 + DOWN,)), (2, (22, 27, 28)), (1, (18 + OUT,)), (0, (18, 19, 20))):
        for i in parts:
            arrived(i)
        if k == 2:
            for j in range(8):
                R.g[2][:, 2 * j * 192 : 2 * (j + 1) * 192] = jnp.concatenate(
                    [R.mixed[:, x * hhalf + j * 192 : x * hhalf + (j + 1) * 192] for x in (0, 1)],
                    axis=1,
                )
        if k == 0:
            for c in range(2):
                for two in range(3):
                    for p in range(3):
                        to = p * width + c * half + two * 128
                        at = (3 * c + two) * 384 + p * 128
                        R.g[0][:, to : to + 128] = R.mixed_qkv[:, at : at + 128]
        stores[3 + k].start()
    for store in stores:
        store.wait()
    for copy in sent:
        copy.wait_send()


def deliver_kernel(*refs):
    found, given, near = refs[:OUTPUTS], refs[OUTPUTS : 2 * OUTPUTS + 8], refs[2 * OUTPUTS + 8 :]
    singles, (in_sem, out_sem) = near[OUTPUTS:-2], near[-2:]
    loads = [pltpu.make_async_copy(f, n, in_sem.at[i]) for i, (f, n) in enumerate(zip(found, near))]
    for load in loads:
        load.start()
    stores = []

    def store(src, dst):
        copy = pltpu.make_async_copy(src, dst, out_sem.at[len(stores)])
        copy.start()
        stores.append(copy)

    loads[2].wait()
    for j, single in enumerate(singles):
        single[...] = near[2][j : j + 1, 0 : single.shape[1]]
        store(single, given[OUTPUTS - 1 + j])
    for i in (0, 4, 3, 1, 5, 6):
        loads[i].wait()
        store(near[i], given[i - (i > 2)])
    for copy in stores:
        copy.wait()


def fused(tokens, doc_ids, pad_mask, matrices, vectors, cotangent):
    rows, width = tokens.shape
    hidden = matrices[2].shape[1]
    fl = jnp.float32
    lists, named = scratch_of(rows, width, hidden)
    operands = (
        [tokens, doc_ids[None], pad_mask[None], cotangent]
        + list(matrices)
        + [v[None] for v in vectors]
    )
    results = [
        jax.ShapeDtypeStruct(tokens.shape, jnp.bfloat16),
        jax.ShapeDtypeStruct(tokens.shape, fl),
        jax.ShapeDtypeStruct((16, 128), fl),
    ] + [jax.ShapeDtypeStruct(m.shape, fl) for m in matrices]
    far = pl.BlockSpec(memory_space=pl.ANY)
    dma = pltpu.SemaphoreType.DMA
    found = pl.pallas_call(
        functools.partial(layer_kernel, tuple(named)),
        out_shape=results,
        in_specs=[far] * INPUTS,
        out_specs=[far] * OUTPUTS,
        scratch_shapes=[pltpu.VMEM(a.shape, a.dtype) for a in operands + results]
        + [pltpu.VMEM(shape, kind) for shape, kind in lists + list(named.values())]
        + [
            dma((SIBLING_COPIES,)),
            dma((SIBLING_COPIES,)),
            dma((COUNT, PAIRS)),
            dma((COUNT, PAIRS)),
            dma((COUNT, PAIRS)),
            dma((COUNT, PAIRS)),
            dma((INPUTS,)),
            dma((OUTPUTS,)),
        ],
        compiler_params=pltpu.CompilerParams(
            collective_id=0, has_side_effects=True, vmem_limit_bytes=FUSED_VMEM
        ),
        name="layer",
    )(*operands)
    singles = [jax.ShapeDtypeStruct((1, v.shape[0]), fl) for v in vectors]
    large = [r for i, r in enumerate(results) if i != 2]
    given = pl.pallas_call(
        deliver_kernel,
        out_shape=large + singles,
        in_specs=[far] * OUTPUTS,
        out_specs=[far] * (len(large) + len(singles)),
        scratch_shapes=[pltpu.VMEM(a.shape, a.dtype) for a in results + singles]
        + [dma((OUTPUTS,)), dma((OUTPUTS + len(singles),))],
        name="deliver",
    )(*found)
    layer_out, token_grad, g0, g1, g2, g3 = given[: len(large)]
    s = [v[0] for v in given[len(large) :]]
    return (
        layer_out,
        token_grad,
        g0,
        s[0],
        s[1],
        g1,
        s[2],
        s[3],
        s[4],
        g2,
        s[8],
        g3,
        s[5],
        s[6],
        s[7],
    )


def local(
    tokens,
    doc_ids,
    pad_mask,
    qkv_matrix,
    query_bias,
    value_bias,
    out_matrix,
    out_bias,
    attn_gain,
    attn_shift,
    up_matrix,
    up_bias,
    down_matrix,
    down_bias,
    ffn_gain,
    ffn_shift,
    cotangent,
):
    fl = jnp.float32
    if lax.axis_size(AXIS) == GROUP:
        return fused(
            tokens,
            doc_ids,
            pad_mask,
            (qkv_matrix, out_matrix, up_matrix, down_matrix),
            (
                query_bias,
                value_bias,
                out_bias,
                attn_gain,
                attn_shift,
                down_bias,
                ffn_gain,
                ffn_shift,
                up_bias,
            ),
            cotangent,
        )
    owned_vectors = (
        query_bias,
        value_bias,
        out_bias,
        attn_gain,
        attn_shift,
        down_bias,
        ffn_gain,
        ffn_shift,
        up_bias,
    )
    vectors = vector_rows([v[None] for v in owned_vectors])[0]
    wholes = [
        lax.all_gather(w, AXIS, axis=0, tiled=True)
        for w in (qkv_matrix, out_matrix, up_matrix, down_matrix, vectors)
    ]
    qkv_full, outm_full, upm_full, downm_full, vectors_full = wholes
    vectors_full = vectors_full.reshape((-1,) + vectors.shape)
    (
        qbias_full,
        vbias_full,
        outb_full,
        gain_one,
        shift_one,
        downb_full,
        gain_two,
        shift_two,
        upb_full,
    ) = (vectors_full[:, j, : v.shape[0]].reshape(-1) for j, v in enumerate(owned_vectors))
    qkv_back, outm_back, upm_back, downm_back = qkv_full, outm_full, upm_full, downm_full
    gain_one_back, gain_two_back = gain_one, gain_two
    row_count, model_width = tokens.shape
    head_size = model_width // HEADS
    score_scale = 1.0 / math.sqrt(head_size)
    hidden_width = upm_full.shape[1]
    ratio = hidden_width // model_width
    zero_part = jnp.zeros((model_width,), fl)
    qkv = jnp.dot(tokens, qkv_full, preferred_element_type=fl)
    qkv = (qkv + jnp.concatenate([qbias_full.astype(fl), zero_part, vbias_full.astype(fl)])).astype(
        jnp.bfloat16
    )
    query = qkv[:, :model_width].reshape(row_count, HEADS, head_size)
    key_rows = qkv[:, model_width : 2 * model_width].reshape(row_count, HEADS, head_size)
    value_rows = qkv[:, 2 * model_width :].reshape(row_count, HEADS, head_size)
    positions = jnp.arange(row_count)
    visible = (doc_ids[:, None] == doc_ids[None, :]) & (
        (pad_mask[None, :] == 1) | (positions[:, None] == positions[None, :])
    )
    scores = masked_scores(query, key_rows, visible, score_scale)
    row_max = jnp.max(scores, axis=-1, keepdims=True)
    log_total = row_max + jnp.log(jnp.sum(jnp.exp(scores - row_max), axis=-1, keepdims=True))
    probs_b = jnp.exp(scores - log_total).astype(jnp.bfloat16)
    context = jnp.einsum("hqk,khd->qhd", probs_b, value_rows, preferred_element_type=fl)
    context = context.reshape(row_count, model_width).astype(jnp.bfloat16)
    attn_sum = (
        tokens.astype(fl)
        + jnp.dot(context, outm_full, preferred_element_type=fl)
        + outb_full.astype(fl)
    )
    hidden, normed_one, inverse_one = layer_norm(
        attn_sum, gain_one.astype(fl), shift_one.astype(fl)
    )
    hidden_b = hidden.astype(jnp.bfloat16)
    pre_act = jnp.dot(hidden_b, upm_full, preferred_element_type=fl) + upb_full.astype(fl)
    cdf_part = 0.5 * (1.0 + jax.scipy.special.erf(pre_act * root_half))
    pdf_part = jnp.exp(-0.5 * pre_act * pre_act) * inv_root_two_pi
    activation = (pre_act * cdf_part).astype(jnp.bfloat16)
    ffn_sum = (
        hidden + jnp.dot(activation, downm_full, preferred_element_type=fl) + downb_full.astype(fl)
    )
    normed_out, normed_two, inverse_two = layer_norm(
        ffn_sum, gain_two.astype(fl), shift_two.astype(fl)
    )
    layer_out = normed_out.astype(jnp.bfloat16)
    upstream = cotangent.astype(fl)
    g_gain_two = jnp.sum(upstream * normed_two, axis=0)
    g_shift_two = jnp.sum(upstream, axis=0)
    d_ffn = norm_back(upstream, normed_two, inverse_two, gain_two_back.astype(fl))
    g_down_b = jnp.sum(d_ffn, axis=0)
    d_ffn_b = d_ffn.astype(jnp.bfloat16)
    d_act = jnp.einsum("rd,fd->rf", d_ffn_b, downm_back, preferred_element_type=fl)
    d_pre = d_act * (cdf_part + pre_act * pdf_part)
    g_up_b = jnp.sum(d_pre, axis=0)
    d_pre_b = d_pre.astype(jnp.bfloat16)
    d_hidden = d_ffn + jnp.einsum("rf,df->rd", d_pre_b, upm_back, preferred_element_type=fl)
    g_gain_one = jnp.sum(d_hidden * normed_one, axis=0)
    g_shift_one = jnp.sum(d_hidden, axis=0)
    d_attn = norm_back(d_hidden, normed_one, inverse_one, gain_one_back.astype(fl))
    g_out_b = jnp.sum(d_attn, axis=0)
    d_attn_b = d_attn.astype(jnp.bfloat16)
    d_context = jnp.einsum("re,de->rd", d_attn_b, outm_back, preferred_element_type=fl).astype(
        jnp.bfloat16
    )
    d_qkv, attn_sums = attention_back(qkv, d_context, doc_ids, pad_mask)
    g_qbias, g_vbias = attn_sums[0], attn_sums[1]
    token_grad = d_attn + jnp.einsum("re,de->rd", d_qkv, qkv_back, preferred_element_type=fl)
    sums = vector_rows(
        [
            g.reshape((lax.axis_size(AXIS), -1))
            for g in (
                g_qbias,
                g_vbias,
                g_out_b,
                g_gain_one,
                g_shift_one,
                g_down_b,
                g_gain_two,
                g_shift_two,
                g_up_b,
            )
        ]
    )
    pairs = ((tokens, d_qkv), (context, d_attn_b), (hidden_b, d_pre_b), (activation, d_ffn_b))
    owned = [
        lax.psum_scatter(p, AXIS, scatter_dimension=0, tiled=True)
        for p in [grad_rows(left, right) for left, right in pairs]
        + [sums.reshape((-1, sums.shape[2]))]
    ]
    grad_qkv, grad_outmat, grad_upmat, grad_downmat, vec = owned
    owned_sums = [vec[j, : v.shape[0]] for j, v in enumerate(owned_vectors)]
    return (
        layer_out,
        token_grad,
        grad_qkv,
        owned_sums[0],
        owned_sums[1],
        grad_outmat,
        owned_sums[2],
        owned_sums[3],
        owned_sums[4],
        grad_upmat,
        owned_sums[8],
        grad_downmat,
        owned_sums[5],
        owned_sums[6],
        owned_sums[7],
    )


def solution(mesh):
    placed = (
        P("fsdp", None),
        P("fsdp"),
        P("fsdp"),
        P("fsdp", None),
        P("fsdp"),
        P("fsdp"),
        P("fsdp", None),
        P("fsdp"),
        P("fsdp"),
        P("fsdp"),
        P("fsdp", None),
        P("fsdp"),
        P("fsdp", None),
        P("fsdp"),
        P("fsdp"),
        P("fsdp"),
        P("fsdp", None),
    )
    return jax.shard_map(
        local,
        mesh=mesh,
        in_specs=placed,
        out_specs=(
            P("fsdp", None),
            P("fsdp", None),
            P("fsdp", None),
            P("fsdp"),
            P("fsdp"),
            P("fsdp", None),
            P("fsdp"),
            P("fsdp"),
            P("fsdp"),
            P("fsdp", None),
            P("fsdp"),
            P("fsdp", None),
            P("fsdp"),
            P("fsdp"),
            P("fsdp"),
        ),
        check_vma=False,
    )
```

```python
import functools
import heapq
import math
import types

import jax
import jax.numpy as jnp
from jax import lax
from jax.experimental import pallas as pl
from jax.experimental.pallas import tpu as pltpu
from jax.sharding import PartitionSpec as P

HEADS = 12
AXIS = "fsdp"
MESH_IDS = pl.DeviceIdType.MESH
GROUP = 32


norm_eps = 1e-06
root_half = 0.7071067811865476
inv_root_two_pi = 0.3989422804014327


def layer_norm(values, gain, shift):
    centred = values - jnp.mean(values, axis=-1, keepdims=True)
    inverse = lax.rsqrt(jnp.mean(centred * centred, axis=-1, keepdims=True) + norm_eps)
    normed = centred * inverse
    return (normed * gain + shift, normed, inverse)


def norm_back(upstream, normed, inverse, gain):
    scaled = upstream * gain
    return inverse * (
        scaled
        - jnp.mean(scaled, axis=-1, keepdims=True)
        - normed * jnp.mean(scaled * normed, axis=-1, keepdims=True)
    )


def masked_scores(query, key_rows, visible, score_scale):
    scores = (
        jnp.einsum("qhd,khd->hqk", query, key_rows, preferred_element_type=jnp.float32)
        * score_scale
    )
    return jnp.where(visible[None], scores, -1e30)


def vector_rows(vectors):
    rows = [jnp.pad(v, ((0, 0), (0, 128 - v.shape[1]))) for v in vectors]
    rows = rows + [jnp.zeros_like(rows[0])] * (16 - len(rows))
    return jnp.stack(rows, axis=1)


def attention_back_kernel(
    scale, qkv_ref, back_ref, doc_col, doc_row, pad_row, d_qkv_ref, sums_ref
):
    fl = jnp.float32
    rows, width = back_ref.shape
    size = width // HEADS
    across, down, both = ((1,), (0,)), ((0,), (0,)), ((1,), (1,))

    def dot(a, b, over):
        return lax.dot_general(a, b, (over, ((), ())), preferred_element_type=fl)

    square = (rows, rows)
    same = lax.broadcasted_iota(jnp.int32, square, 0) == lax.broadcasted_iota(
        jnp.int32, square, 1
    )
    visible = (doc_col[...] == doc_row[...]) & ((pad_row[...] == 1) | same)
    for pair in range(HEADS // 2):
        results = []
        for h in (2 * pair, 2 * pair + 1):
            query, key_rows, value_rows = (
                qkv_ref[:, part * width + h * size : part * width + (h + 1) * size]
                for part in range(3)
            )
            back = back_ref[:, h * size : (h + 1) * size]
            scores = jnp.where(visible, dot(query, key_rows, both) * scale, -1e30)
            row_max = jnp.max(scores, axis=-1, keepdims=True)
            total = jnp.sum(jnp.exp(scores - row_max), axis=-1, keepdims=True)
            probs = jnp.exp(scores - (row_max + jnp.log(total)))
            d_value = dot(probs.astype(jnp.bfloat16), back, down)
            d_probs = dot(back, value_rows, both)
            delta = jnp.sum(probs * d_probs, axis=-1, keepdims=True)
            d_scores = (probs * (d_probs - delta) * scale).astype(jnp.bfloat16)
            results.append(
                (dot(d_scores, key_rows, across), dot(d_scores, query, down), d_value)
            )
        for part in range(3):
            block = jnp.concatenate([results[0][part], results[1][part]], axis=1)
            at = pair * 2 * size
            d_qkv_ref[:, part * width + at : part * width + at + 2 * size] = block.astype(
                jnp.bfloat16
            )
            if part != 1:
                row = part // 2
                sums_ref[row : row + 1, at : at + 2 * size] = jnp.sum(
                    block, axis=0, keepdims=True
                )


def attention_back(qkv, d_context, doc_ids, pad_mask):
    rows, width = d_context.shape
    return pl.pallas_call(
        functools.partial(attention_back_kernel, 1.0 / math.sqrt(width // HEADS)),
        out_shape=(
            jax.ShapeDtypeStruct(qkv.shape, jnp.bfloat16),
            jax.ShapeDtypeStruct((2, width), jnp.float32),
        ),
        compiler_params=pltpu.CompilerParams(vmem_limit_bytes=24 * 1024 * 1024),
        name="attention_back",
    )(qkv, d_context, doc_ids[:, None], doc_ids[None], pad_mask[None])


def grad_rows(left, right):
    return jnp.einsum("ra,rb->ab", left, right, preferred_element_type=jnp.float32)


X, Y, Z1, Z2 = 0, 1, 2, 3
GATHER_ORDERS = (
    (Z2, Z1, X, Y),
    (Z2, Z1, Y, X),
    (Y, Z2, Z1, X),
    (Z2, Z1, Y, X),
    (Z2, Z1, Y),
    (Z2, Z1, Y),
    (Z2, Z1, Y),
    (Y, Z2, Z1),
    (Y, Z2, Z1, X),
)
SCATTER_ORDERS = (
    (X, Z1, Z2, Y),
    (Y, X, Z1, Z2),
    (Y, X, Z1, Z2),
    (Y, X, Z1, Z2),
    (Y, Z1, Z2),
    (Y, Z1, Z2),
    (Y, Z1, Z2),
    (Z1, Z2, Y),
    (X, Z1, Z2, Y),
)
GATHER_FIRST = (0, 1, 2, 3, 4, 4, 5, 5, 0)
SCATTER_FIRST = (3, 0, 0, 1, 1, 2, 3, 2, 3)
ADDS_BETWEEN = 1
ADD_US = (0.225, 0.225, 0.225, 0.225, 0.3, 0.3, 0.3, 0.3, 0.12)
PAIRS = 16
PIECES = (16, 16, 16, 16, 8, 8, 8, 8, 16)
PIECE_ROWS = (48, 48, 48, 48, 96, 96, 96, 96, 32)
PIECE_COLS = (384, 384, 384, 384, 384, 384, 384, 384, 128)
TRAVELLERS = 9
BUFFER = (0, 1, 2, 3, 4, 4, 5, 5, 6)
PLACE_ROWS = (48, 48, 48, 48, 96, 192, 32)
PLACE_COLS = (384, 384, 384, 384, 768, 384, 128)
PLACES = (16, 16, 16, 16, 8, 8, 16)
OUT, UP, DOWN, VEC = 3, 4, 5, 6
QUAD = 4
COUNT = 7
HOPS = {X: ((0, 1),), Y: ((1, 1),), Z1: ((2, 1),), Z2: ((2, 1), (3, 2))}
LINK_BYTES_PER_US = 44e3
HOP_US = 1.5
CORE_BYTES_PER_US = 600e3
BACKLOG_US = 1.5
FUSED_VMEM = 58 * 1024 * 1024


class Plan:
    def __init__(self):
        self.now = 0.0
        self.free = {}
        self.pending = []
        self.waiting = []
        self.here = set()
        self.seq = 0

    def travel(self, dim, size, key):
        if dim is None:
            us, hops = size / CORE_BYTES_PER_US, ((4, 1),)
        else:
            us, hops = size / LINK_BYTES_PER_US, HOPS[dim]
        begin = max([self.now] + [self.free.get(link, 0.0) for link, _ in hops])
        end = begin
        for link, cost in hops:
            self.free[link] = begin + cost * us
            end = max(end, begin + cost * us)
        self.seq += 1
        heapq.heappush(self.pending, (end + HOP_US, self.seq, key))

    def ask(self, first, dim, size, key, start):
        self.seq += 1
        self.waiting.append((first, self.seq, dim, size, key, start))
        self.waiting.sort(key=lambda entry: entry[:2])

    def pump(self):
        left = []
        for entry in self.waiting:
            _, _, dim, size, key, start = entry
            if max(self.free.get(link, 0.0) for link, _ in HOPS[dim]) - self.now < BACKLOG_US:
                start()
                self.travel(dim, size, key)
            else:
                left.append(entry)
        self.waiting = left


def subsets(order, step):
    blocks = [0]
    for b in reversed(order[step + 1 :]):
        blocks = [r | (1 << b) for r in blocks] + blocks
    return blocks


def dot(a, b, over=((1,), (0,))):
    return lax.dot_general(a, b, (over, ((), ())), preferred_element_type=jnp.float32)


ROWS_BOTH, COLS_BOTH = ((0,), (0,)), ((1,), (1,))

SIBLING_COPIES = 58
INPUTS, OUTPUTS = 17, 7


def stage_shape(k):
    if k == UP:
        return ((QUAD, 32, PLACE_COLS[k]), jnp.bfloat16)
    return (((PLACE_ROWS[k] // 2 + 15) // 16 * 16, PLACE_COLS[k]), jnp.bfloat16)


def scratch_of(rows, width, hidden):
    fl, bf = jnp.float32, jnp.bfloat16
    both, half, quad = 2 * rows, width // 2, QUAD * rows
    hhalf, hquarter = hidden // 2, hidden // 4
    lists = []
    for shape_of in (
        lambda k: ((PLACES[k] * PLACE_ROWS[k], PLACE_COLS[k]), bf),
        lambda k: ((PLACES[k] * PLACE_ROWS[k], PLACE_COLS[k]), bf),
        stage_shape,
        stage_shape,
        lambda k: ((PLACE_ROWS[k], PLACE_COLS[k]), fl),
    ):
        lists += [shape_of(k) for k in range(COUNT)]
    lists += [((PIECES[k] - 1, PIECE_ROWS[k], PIECE_COLS[k]), bf) for k in range(TRAVELLERS)]
    named = dict(
        peer_vec=((PAIRS * PLACE_ROWS[VEC], PLACE_COLS[VEC]), bf),
        stage_vec=((PAIRS * PLACE_ROWS[VEC], PLACE_COLS[VEC]), bf),
        tok=((both, width), bf),
        marks=((2, 8, rows), fl),
        vec32=((PAIRS * 32, 128), fl),
        vecs=((16, width), fl),
        upb=((8, hquarter), fl),
        qkv=((both, 3 * half), bf),
        probs=((HEADS, rows, rows), fl),
        ctx=((both, width), bf),
        proj_s=((both, half), fl),
        proj_r=((rows, half), fl),
        hid=((rows, width), fl),
        n1=((rows, width), fl),
        i1=((rows, 128), fl),
        hb=((quad, width), bf),
        act=((quad, hhalf), bf),
        fac=((quad, hquarter), fl),
        ffn_s=((rows, half), fl),
        ffn_r=((rows, half), fl),
        ffn_o=((both, half), fl),
        ffn_xs=((both, half), bf),
        ffn_xr=((both, half), bf),
        dff=((rows, width), fl),
        dfb=((quad, width), bf),
        dact_s=((quad, hquarter), fl),
        dact_r=((quad, hquarter), fl),
        dact_o=((quad, hquarter), fl),
        dpre=((quad, hquarter), bf),
        dhid_s=((both, width), fl),
        dhid_r=((both, width), fl),
        dhid_o=((both, width), fl),
        dhid_xs=((rows, width), bf),
        dhid_xr=((rows, width), bf),
        dat=((rows, width), fl),
        datb=((both, width), bf),
        dctx_s=((both, half), fl),
        dctx_r=((both, half), fl),
        dctx_o=((both, half), fl),
        dctx=((both, half), bf),
        dqkv=((both, 3 * half), bf),
        tg_s=((both, width), fl),
        tg_r=((rows, width), fl),
        sums=((16, width), fl),
        upsum=((8, hquarter), fl),
        mixed=((width // GROUP, hidden), fl),
        mixed_qkv=((width // GROUP, 3 * width), fl),
    )
    return lists, named


def layer_kernel(names, *refs):
    refs = list(refs)

    def take(count):
        taken, refs[:count] = refs[:count], []
        return taken

    R = types.SimpleNamespace()
    far_in, far_out, near_in, near_out = take(INPUTS), take(OUTPUTS), take(INPUTS), take(OUTPUTS)
    R.tokens, R.doc, R.pad, R.cotangent = near_in[:4]
    R.w, R.v = near_in[4:8], near_in[8:]
    R.layer_out, R.token_grad, R.gv = near_out[:3]
    R.g = near_out[3:]
    R.whole, R.part, R.stage, R.peer, R.fin = (take(COUNT) for _ in range(5))
    R.land = take(TRAVELLERS)
    vars(R).update(zip(names, take(len(names))))
    sib_send, sib_recv, g_send, g_recv, s_send, s_recv, in_sem, out_sem = refs
    loads = [
        pltpu.make_async_copy(far, near, in_sem.at[i])
        for i, (far, near) in enumerate(zip(far_in, near_in))
    ]
    for i in (4, *range(8, 17), 5, 6, 7, 0, 1, 2, 3):
        loads[i].start()
    stores = [
        pltpu.make_async_copy(near, far, out_sem.at[i])
        for i, (far, near) in enumerate(zip(far_out, near_out))
    ]
    fl, bf = jnp.float32, jnp.bfloat16
    rows, width = R.tokens.shape
    hidden = R.w[2].shape[1]
    half, hhalf, hquarter = width // 2, hidden // 2, hidden // 4
    size = width // HEADS
    scale = 1.0 / math.sqrt(size)
    me = lax.axis_index(AXIS)
    core = lax.rem(me, 2)
    pair = lax.div(me, 2)
    bits = [lax.rem(lax.div(pair, 1 << b), 2) for b in range(4)]
    sibling = me + 1 - 2 * core
    is_first = core == 0

    def pair_of(r):
        p = pair
        for b in range(4):
            if r >> b & 1:
                p = p + (1 << b) * (1 - 2 * bits[b])
        return p

    def quad_of(r):
        q = lax.div(pair, 2)
        for b in range(1, 4):
            if r >> b & 1:
                q = q + (1 << (b - 1)) * (1 - 2 * bits[b])
        return q

    def device_along(b):
        return me + (2 << b) * (1 - 2 * bits[b])

    def by_core(step, which=None):
        at = core if which is None else 1 - core
        return pl.multiple_of(at * step, step)

    own_rows, sib_rows = pl.ds(by_core(rows), rows), pl.ds(by_core(rows, 1), rows)
    own_half, sib_half = pl.ds(by_core(half), half), pl.ds(by_core(half, 1), half)
    own_hq, sib_hq = pl.ds(by_core(hquarter), hquarter), pl.ds(by_core(hquarter, 1), hquarter)
    x_at = bits[X]
    across = device_along(X)
    diagonal = across + 1 - 2 * core
    member = 2 * x_at + core

    def quad_rows(other_x, other_core, count=rows, skip=0):
        at = 2 * (1 - x_at if other_x else x_at) + (1 - core if other_core else core)
        return pl.ds(pl.multiple_of(at * rows + skip, 64), count)

    def chip_rows(other_x):
        return pl.ds(pl.multiple_of((1 - x_at if other_x else x_at) * 2 * rows, 128), 2 * rows)


    barrier = pltpu.get_barrier_semaphore()
    for other in [sibling, diagonal] + [device_along(b) for b in range(4)]:
        pl.semaphore_signal(barrier, inc=1, device_id=(other,), device_id_type=MESH_IDS)
    pl.semaphore_wait(barrier, 6)

    plan = Plan()
    sib = {}
    sent = []

    def to_sibling(i, src, dst, device=None):
        copy = pltpu.make_async_remote_copy(
            src_ref=src,
            dst_ref=dst,
            send_sem=sib_send.at[i],
            recv_sem=sib_recv.at[i],
            device_id=(sibling if device is None else device,),
            device_id_type=MESH_IDS,
        )
        copy.start()
        sib[i] = copy
        sent.append(copy)
        plan.travel(None if device is None else X, math.prod(src.shape) * src.dtype.itemsize, (None, i))

    def arrived(i):
        sib.pop(i).wait_recv()

    def side_by_side(own, other):
        return jnp.concatenate(
            [jnp.where(is_first, own, other), jnp.where(is_first, other, own)], axis=1
        )

    def shard_half(k, mine):
        which = core if mine else 1 - core
        if k < 3:
            cols = [
                R.w[0][:, pl.ds(pl.multiple_of(p * width + which * half + k * 128, 128), 128)]
                for p in range(3)
            ]
            return jnp.concatenate([c.astype(fl) for c in cols], axis=1)
        cols = PLACE_COLS[k]
        ref = R.w[1] if k == OUT else R.w[3]
        return ref[:, pl.ds(by_core(cols, None if mine else 1), cols)].astype(fl)

    def padded(value):
        short = -value.shape[0] % 16
        if short:
            value = jnp.concatenate([value, jnp.zeros((short, value.shape[1]), fl)], axis=0)
        return value.astype(bf)

    for load in loads[4:]:
        load.wait()
    R.vec32[pl.ds(0, 16), :] = jnp.zeros((16, 128), fl)
    for j in range(9):
        v = R.v[j]
        R.vec32[j : j + 1, 0 : v.shape[1]] = v[...].astype(fl)
    R.stage[VEC][...] = R.vec32[pl.ds(0, 16), :].astype(bf)
    def quarter(q):
        blocks = []
        for j in range(4):
            at = (q % 2) * hhalf + 2 * j * 192 + (q // 2) * 192
            blocks.append(R.w[2][:, at : at + 192].astype(fl))
        return jnp.concatenate(blocks, axis=1)

    for k in (0, VEC, 1, 2, OUT, DOWN):
        if k != VEC:
            R.stage[k][...] = padded(shard_half(k, False))
        to_sibling(50 + k, R.stage[k], R.peer[k])
    for q in range(QUAD):
        R.stage[UP][q] = padded(quarter(q))
    for i, device, q in (
        (54, None, member + 1 - 2 * core),
        (25, across, member + 2 - 4 * x_at),
        (26, diagonal, 3 - member),
    ):
        to_sibling(i, R.stage[UP].at[q], R.peer[UP].at[member], device)
    for load in loads[:4]:
        load.wait()
    to_sibling(5, R.tokens, R.tok.at[own_rows])
    own_marks = jnp.concatenate(
        [R.doc[...].astype(fl), R.pad[...].astype(fl), jnp.zeros((6, rows), fl)], axis=0
    )
    R.marks[core] = own_marks
    to_sibling(6, R.marks.at[core], R.marks.at[core])
    R.tok[own_rows, :] = R.tokens[...]

    plan.now = 3.0
    piece_bytes = [2 * PIECE_ROWS[k] * PIECE_COLS[k] for k in range(TRAVELLERS)]
    done = [1] * TRAVELLERS

    def place_at(k, r):
        n = PLACE_ROWS[k]
        place = pair_of(r) if PLACES[k] == PAIRS else quad_of(r)
        return pl.multiple_of(place * n, n)

    def piece_of(refs, k, r):
        to = BUFFER[k]
        row, col = place_at(to, r), 0
        if k > 0 and BUFFER[k - 1] == to:
            if to == UP:
                col = PIECE_COLS[k]
            else:
                row = pl.multiple_of(row + PIECE_ROWS[k], PIECE_ROWS[k])
        return refs[to].at[pl.ds(row, PIECE_ROWS[k]), pl.ds(col, PIECE_COLS[k])]

    def gather_move(k, r, b):
        slot = r | (1 << b)
        copy = pltpu.make_async_remote_copy(
            src_ref=piece_of(R.whole, k, r),
            dst_ref=piece_of(R.whole, k, r),
            send_sem=g_send.at[k, slot],
            recv_sem=g_recv.at[k, slot],
            device_id=(device_along(b),),
            device_id_type=MESH_IDS,
        )
        sent.append(copy)
        plan.ask(GATHER_FIRST[k], b, piece_bytes[k], (True, k, slot, b), copy.start)

    for k in (0, VEC, 1, 2, OUT, DOWN, UP):
        arrived(50 + k)
        if k == UP:
            R.peer[UP][member] = R.stage[UP][member]
            arrived(25)
            arrived(26)
            rows_in = [R.peer[UP][q].astype(fl)[: width // GROUP] for q in range(QUAD)]
        else:
            mine = R.vec32[pl.ds(0, 16), :] if k == VEC else shard_half(k, True)
            theirs = R.peer[k][...].astype(fl)[: mine.shape[0]]
            rows_in = [jnp.where(is_first, mine, theirs), jnp.where(is_first, theirs, mine)]
        R.whole[k][pl.ds(place_at(k, 0), PLACE_ROWS[k]), :] = jnp.concatenate(
            rows_in, axis=0
        ).astype(bf)
        for j in range(TRAVELLERS):
            if BUFFER[j] == k:
                for b in GATHER_ORDERS[j]:
                    gather_move(j, 0, b)
        plan.pump()

    def on_gather(k, r, b):
        here = piece_of(R.whole, k, r)
        pltpu.make_async_remote_copy(
            src_ref=here,
            dst_ref=here,
            send_sem=g_send.at[k, r],
            recv_sem=g_recv.at[k, r],
            device_id=(device_along(b),),
            device_id_type=MESH_IDS,
        ).wait_recv()
        order = GATHER_ORDERS[k]
        for later in order[order.index(b) + 1 :]:
            gather_move(k, r, later)
        done[k] += 1

    slot_of = []
    for k in range(TRAVELLERS):
        table = {}
        for step in range(len(SCATTER_ORDERS[k])):
            for r in subsets(SCATTER_ORDERS[k], step):
                table[step, r] = len(table)
        slot_of.append(table)
    copies = {}

    def held(k, step, r):
        if step < 0:
            return piece_of(R.part, k, r)
        return R.land[k].at[slot_of[k][step, r]]

    def scatter_move(k, step, r):
        b = SCATTER_ORDERS[k][step]
        low = r & ~(1 << b)
        slot = slot_of[k][step, low]
        copy = pltpu.make_async_remote_copy(
            src_ref=held(k, step - 1, r),
            dst_ref=R.land[k].at[slot],
            send_sem=s_send.at[k, slot],
            recv_sem=s_recv.at[k, slot],
            device_id=(device_along(b),),
            device_id_type=MESH_IDS,
        )
        sent.append(copy)
        copies[k, step, low] = copy
        plan.ask(SCATTER_FIRST[k], b, piece_bytes[k], (False, k, step, low), copy.start)

    def scatter_start(k):
        order = SCATTER_ORDERS[k]
        for r in subsets(order, 0):
            scatter_move(k, 0, r | (1 << order[0]))

    def finish(k):
        if k == VEC:
            R.gv[...] = R.fin[VEC][pl.ds(by_core(16), 16), :]
            stores[2].start()
            return
        if k == UP:
            at = pl.ds(pl.multiple_of(x_at * hhalf + core * hquarter, 128), hquarter)
            n = PLACE_ROWS[UP] // QUAD

            def share(q):
                return R.fin[UP].at[pl.ds(pl.multiple_of(q * n, n), n)]

            for i, device, q in (
                (22, None, member + 1 - 2 * core),
                (27, across, member + 2 - 4 * x_at),
                (28, diagonal, 3 - member),
            ):
                to_sibling(i, share(q), R.mixed.at[:, at], device)
            R.mixed[:, at] = share(member)[...]
            return
        n = PLACE_ROWS[k] // 2
        mine = R.fin[k].at[pl.ds(by_core(n), n)]
        theirs = R.fin[k].at[pl.ds(by_core(n, 1), n)]
        if k < 3:
            into, at = R.mixed_qkv, pl.ds(pl.multiple_of((3 * core + k) * 384, 384), 384)
        else:
            into, at = R.g[1 if k == OUT else 3], own_half
        to_sibling(18 + k, theirs, into.at[:, at])
        into[:, at] = mine[...]

    unfinished = [BUFFER.count(k) for k in range(COUNT)]
    summed = set()
    early = {}

    def on_scatter(k, step, r):
        if step and (k, step - 1, r) not in summed:
            early[k, step - 1, r] = step
            return
        summed.add((k, step, r))
        plan.now += ADD_US[k]
        add_piece(k, step, r)
        if (k, step, r) in early:
            on_scatter(k, early[k, step, r], r)

    def add_piece(k, step, r):
        copies[k, step, r].wait_recv()
        order = SCATTER_ORDERS[k]
        before, now = held(k, step - 1, r), held(k, step, r)
        if step == len(order) - 1:
            to = BUFFER[k]
            row, col = 0, 0
            if k > 0 and BUFFER[k - 1] == to:
                row, col = (0, PIECE_COLS[k]) if to == UP else (PIECE_ROWS[k], 0)
            R.fin[to][row : row + PIECE_ROWS[k], col : col + PIECE_COLS[k]] = now[...].astype(
                fl
            ) + before[...].astype(fl)
            unfinished[to] -= 1
            if not unfinished[to]:
                finish(to)
            return
        now[...] = now[...] + before[...]
        if r >> order[step + 1] & 1:
            scatter_move(k, step + 1, r)

    def column_of(n, period):
        return jnp.floor((n + 0.5) * (1.0 / period))

    def pick(count, period):
        n = lax.broadcasted_iota(jnp.int32, (128, count), 1).astype(fl)
        i = lax.broadcasted_iota(jnp.int32, (128, count), 0).astype(fl)
        return jnp.where(n - period * column_of(n, period) == i, 1.0, 0.0).astype(bf)

    def owner_is(count, period):
        n = lax.broadcasted_iota(jnp.int32, (GROUP, count), 1).astype(fl)
        d = lax.broadcasted_iota(jnp.int32, (GROUP, count), 0).astype(fl)
        return column_of(n, period) == d

    small, large = width // GROUP, hidden // GROUP

    def unit_owner():
        n = lax.broadcasted_iota(jnp.int32, (GROUP, hquarter), 1).astype(fl)
        d = lax.broadcasted_iota(jnp.int32, (GROUP, hquarter), 0).astype(fl)
        block = column_of(n, large)
        quad = column_of(block, 2)
        first = (16 * core + 2 * x_at).astype(fl)
        return first + 4.0 * quad + (block - 2.0 * quad) == d

    def task_vectors():
        R.vec32[...] = R.whole[VEC][...].astype(fl)
        chosen, owner = pick(width, small), owner_is(width, small)
        for j in range(8):
            v = R.vec32[pl.ds(j, GROUP, stride=16), :].astype(bf)
            R.vecs[j : j + 1, :] = jnp.sum(
                jnp.where(owner, dot(v, chosen), 0.0), axis=0, keepdims=True
            )
        v = R.vec32[pl.ds(8, GROUP, stride=16), :].astype(bf)
        R.upb[0:1, :] = jnp.sum(
            jnp.where(unit_owner(), dot(v, pick(hquarter, large)), 0.0),
            axis=0,
            keepdims=True,
        )

    def vec(j):
        return R.vecs[j : j + 1, :]

    def task_qkv(two):
        if two == 0:
            arrived(5)
            arrived(6)
        value = dot(R.tok[...], R.whole[two][...])
        for p in range(3):
            block = value[:, p * 128 : (p + 1) * 128]
            if p != 1:
                at = pl.ds(pl.multiple_of(core * half + two * 128, 128), 128)
                block = block + R.vecs[p // 2 : p // 2 + 1, at]
            R.qkv[:, two * 384 + p * 128 : two * 384 + (p + 1) * 128] = block.astype(bf)

    def seen(b):
        doc, pad = R.marks[b, 0:1, :], R.marks[b, 1:2, :]
        square = (rows, rows)
        wide = jnp.broadcast_to(doc, square)
        same = lax.broadcasted_iota(jnp.int32, square, 0) == lax.broadcasted_iota(
            jnp.int32, square, 1
        )
        return (wide.T == wide) & ((jnp.broadcast_to(pad, square) == 1.0) | same)

    def head_of(b, h):
        at = b * rows
        first = h // 2 * 384 + h % 2 * size
        return [
            R.qkv[at : at + rows, first + p * 128 : first + p * 128 + size] for p in range(3)
        ]

    def task_attention(b, two):
        visible = seen(b)
        found = []
        for h in (2 * two, 2 * two + 1):
            query, key_rows, value_rows = head_of(b, h)
            scores = jnp.where(visible, dot(query, key_rows, COLS_BOTH) * scale, -1e30)
            row_max = jnp.max(scores, axis=-1, keepdims=True)
            total = jnp.sum(jnp.exp(scores - row_max), axis=-1, keepdims=True)
            probs = jnp.exp(scores - (row_max + jnp.log(total)))
            R.probs[b * (HEADS // 2) + h] = probs
            found.append(dot(probs.astype(bf), value_rows))
        at = pl.ds(pl.multiple_of(core * half + two * 2 * size, 128), 2 * size)
        R.ctx[pl.ds(b * rows, rows), at] = jnp.concatenate(found, axis=1).astype(bf)
        if b == 1:
            to_sibling((7, 45, 46)[two], R.ctx.at[:, at], R.ctx.at[:, at])

    def task_project():
        arrived(7)
        arrived(45)
        arrived(46)
        R.proj_s[...] = dot(R.ctx[...], R.whole[OUT][...])
        to_sibling(8, R.proj_s.at[sib_rows], R.proj_r)

    def norm(values):
        centred = values - jnp.mean(values, axis=-1, keepdims=True)
        inverse = lax.rsqrt(jnp.mean(centred * centred, axis=-1, keepdims=True) + norm_eps)
        return centred * inverse, inverse

    def task_norm_one():
        arrived(8)
        attn = (
            R.tokens[...].astype(fl)
            + side_by_side(R.proj_s[own_rows, :], R.proj_r[...])
            + vec(2)
        )
        normed, inverse = norm(attn)
        hid = normed * vec(3) + vec(4)
        R.n1[...] = normed
        R.i1[...] = jnp.broadcast_to(inverse, (rows, 128))
        R.hid[...] = hid
        R.hb[quad_rows(0, 0), :] = hid.astype(bf)
        spread_rows(R.hb, 9, 29)

    tile = 384

    def spread_rows(ref, i, first):
        for skip in (0, 1):
            at = quad_rows(0, 0, rows // 2, skip * (rows // 2))
            to_sibling(first + skip, ref.at[at], ref.at[at], across)
        at = quad_rows(0, 0)
        to_sibling(i, ref.at[at], ref.at[at])

    def pass_on(ref, first):
        for skip in (0, 1):
            arrived(first + skip)
            at = quad_rows(1, 0, rows // 2, skip * (rows // 2))
            to_sibling(first + 2 + skip, ref.at[at], ref.at[at])

    def task_up(other):
        if other:
            arrived(31)
            arrived(32)
        else:
            arrived(9)
        to = chip_rows(other)

        def body(t, carry):
            at = pl.ds(pl.multiple_of(t * tile, tile), tile)
            pre = dot(R.hb[to, :], R.whole[UP][:, at]) + R.upb[0:1, at]
            cdf = 0.5 * (1.0 + lax.erf(pre * root_half))
            pdf = jnp.exp(-0.5 * pre * pre) * inv_root_two_pi
            R.fac[to, at] = cdf + pre * pdf
            R.act[to, pl.ds(pl.multiple_of(core * hquarter + t * tile, tile), tile)] = (
                pre * cdf
            ).astype(bf)
            return carry

        lax.fori_loop(0, hquarter // tile, body, 0)
        to_sibling(33 + other, R.act.at[to, own_hq], R.act.at[to, own_hq])

    def task_ffn():
        arrived(33)
        arrived(34)
        R.ffn_xs[...] = dot(R.act[chip_rows(1), :], R.whole[DOWN][...]).astype(bf)
        for part, ids in ((0, (35, 36)), (1, (47, 48))):
            for i, other_core in zip(ids, (1, 0)):
                at = local_rows(other_core, part)
                to_sibling(i, R.ffn_xs.at[at], R.ffn_xr.at[at], across)
        R.ffn_o[...] = dot(R.act[chip_rows(0), :], R.whole[DOWN][...])

    def local_rows(other_core, part):
        at = (1 - core if other_core else core) * rows + part * (rows // 2)
        return pl.ds(pl.multiple_of(at, 64), rows // 2)

    def task_ffn_sum(part):
        arrived((35, 47)[part])
        at, to = local_rows(1, part), pl.ds(part * (rows // 2), rows // 2)
        R.ffn_s[to, :] = R.ffn_o[at, :] + R.ffn_xr[at, :].astype(fl)
        to_sibling((11, 49)[part], R.ffn_s.at[to], R.ffn_r.at[to])
        arrived((36, 48)[part])

    def back_of_norm(upstream, normed, inverse, gain):
        scaled = upstream * gain
        return inverse * (
            scaled
            - jnp.mean(scaled, axis=-1, keepdims=True)
            - normed * jnp.mean(scaled * normed, axis=-1, keepdims=True)
        )

    def add_sum(j, values, more=False):
        total = jnp.sum(values, axis=0, keepdims=True)
        R.sums[j : j + 1, :] = R.sums[j : j + 1, :] + total if more else total

    def task_norm_two(part):
        arrived((11, 49)[part])
        at, to = local_rows(0, part), pl.ds(part * (rows // 2), rows // 2)
        mine = R.ffn_o[at, :] + R.ffn_xr[at, :].astype(fl)
        total = R.hid[to, :] + side_by_side(mine, R.ffn_r[to, :]) + vec(5)
        normed, inverse = norm(total)
        R.layer_out[to, :] = (normed * vec(6) + vec(7)).astype(bf)
        upstream = R.cotangent[to, :].astype(fl)
        d_ffn = back_of_norm(upstream, normed, inverse, vec(6))
        R.dff[to, :] = d_ffn
        rows_at = quad_rows(0, 0, rows // 2, part * (rows // 2))
        R.dfb[rows_at, :] = d_ffn.astype(bf)
        to_sibling(37 + part, R.dfb.at[rows_at], R.dfb.at[rows_at], across)
        add_sum(6, upstream * normed, part)
        add_sum(7, upstream, part)
        add_sum(5, d_ffn, part)
        if part:
            stores[0].start()
            rows_at = quad_rows(0, 0)
            to_sibling(12, R.dfb.at[rows_at], R.dfb.at[rows_at])

    def pass_half(ref, first, part):
        arrived(first + part)
        at = quad_rows(1, 0, rows // 2, part * (rows // 2))
        to_sibling(first + 2 + part, ref.at[at], ref.at[at])

    def task_grad_down():
        def body(t, carry):
            at = pl.ds(pl.multiple_of(t * tile, tile), tile)
            R.part[DOWN][at, :] = dot(R.act[:, at], R.dfb[:, own_half], ROWS_BOTH).astype(bf)
            return carry

        lax.fori_loop(0, hhalf // tile, body, 0)
        scatter_start(6)
        scatter_start(7)

    def task_d_act(other):
        if other:
            arrived(39)
            arrived(40)
        else:
            arrived(12)
        at = chip_rows(other)
        right = R.dfb[at, own_half]
        R.dact_s[at, :] = dot(right, R.whole[DOWN][sib_hq, :], COLS_BOTH)
        to_sibling(41 + other, R.dact_s.at[at], R.dact_r.at[at])
        R.dact_o[at, :] = dot(right, R.whole[DOWN][own_hq, :], COLS_BOTH)

    def task_d_pre():
        arrived(41)
        arrived(42)

        def body(t, carry):
            at = pl.ds(pl.multiple_of(t * tile, tile), tile)
            value = (R.dact_o[:, at] + R.dact_r[:, at]) * R.fac[:, at]
            R.upsum[0:1, at] = jnp.sum(value, axis=0, keepdims=True)
            R.dpre[:, at] = value.astype(bf)
            return carry

        lax.fori_loop(0, hquarter // tile, body, 0)

    def task_d_hidden():
        for other_core, into in ((1, R.dhid_s), (0, R.dhid_o)):
            left = jnp.concatenate(
                [R.dpre[quad_rows(other_x, other_core), :] for other_x in (0, 1)], axis=0
            )
            into[...] = dot(left, R.whole[UP][...], COLS_BOTH)
            if other_core:
                for i, other_x in ((14, 1), (43, 0)):
                    at = pl.ds(other_x * rows, rows)
                    to_sibling(i, R.dhid_s.at[at], R.dhid_r.at[at])

    def task_d_hidden_sum():
        arrived(14)
        at = pl.ds(rows, rows)
        R.dhid_xs[...] = (R.dhid_o[at, :] + R.dhid_r[at, :]).astype(bf)
        to_sibling(44, R.dhid_xs, R.dhid_xr, across)

    def task_grad_up():
        for t in range(2):
            at = pl.ds(t * tile, tile)
            R.part[UP][:, at] = dot(R.hb[...], R.dpre[:, at], ROWS_BOTH).astype(bf)
            scatter_start(4 + t)

    def task_norm_one_back():
        arrived(43)
        arrived(44)
        at = pl.ds(0, rows)
        d_hid = R.dff[...] + R.dhid_o[at, :] + R.dhid_r[at, :] + R.dhid_xr[...].astype(fl)
        normed = R.n1[...]
        d_attn = back_of_norm(d_hid, normed, R.i1[:, 0:1], vec(3))
        R.dat[...] = d_attn
        R.datb[own_rows, :] = d_attn.astype(bf)
        to_sibling(15, R.datb.at[own_rows], R.datb.at[own_rows])
        add_sum(3, d_hid * normed)
        add_sum(4, d_hid)
        add_sum(2, d_attn)

    def task_d_context():
        arrived(15)
        right = R.datb[:, own_half]
        R.dctx_s[...] = dot(right, R.whole[OUT][sib_half, :], COLS_BOTH)
        to_sibling(16, R.dctx_s, R.dctx_r)
        R.dctx_o[...] = dot(right, R.whole[OUT][own_half, :], COLS_BOTH)

    def task_grad_out():
        R.part[OUT][...] = dot(R.ctx[...], R.datb[:, own_half], ROWS_BOTH).astype(bf)
        scatter_start(OUT)

    def task_d_context_sum():
        arrived(16)
        R.dctx[...] = (R.dctx_o[...] + R.dctx_r[...]).astype(bf)

    bias_sums = {}

    def task_attention_back(b, two):
        found = []
        at = b * rows
        for h in (2 * two, 2 * two + 1):
            query, key_rows, value_rows = head_of(b, h)
            back = R.dctx[at : at + rows, h * size : (h + 1) * size]
            probs = R.probs[b * (HEADS // 2) + h]
            d_value = dot(probs.astype(bf), back, ROWS_BOTH)
            d_probs = dot(back, value_rows, COLS_BOTH)
            delta = jnp.sum(probs * d_probs, axis=-1, keepdims=True)
            d_scores = (probs * (d_probs - delta) * scale).astype(bf)
            found.append((dot(d_scores, key_rows), dot(d_scores, query, ROWS_BOTH), d_value))
        for p in range(3):
            block = jnp.concatenate([found[0][p], found[1][p]], axis=1)
            cols = two * 384 + p * 128
            R.dqkv[at : at + rows, cols : cols + 2 * size] = block.astype(bf)
            if p != 1:
                total = jnp.sum(block, axis=0, keepdims=True)
                if b == 0:
                    bias_sums[p, two] = total
                else:
                    to = pl.ds(pl.multiple_of(core * half + two * 2 * size, 128), 2 * size)
                    R.sums[p // 2 : p // 2 + 1, to] = total + bias_sums[p, two]

    def task_clear_sums():
        R.sums[...] = jnp.zeros(R.sums.shape, fl)

    def task_grad_qkv(two):
        at = pl.ds(two * 384, 384)
        R.part[two][...] = dot(R.tok[...], R.dqkv[:, at], ROWS_BOTH).astype(bf)
        scatter_start(two)

    def task_token_grad():
        R.tg_s[...] = sum(
            dot(R.dqkv[:, pl.ds(two * 384, 384)], R.whole[two][...], COLS_BOTH)
            for two in range(3)
        )
        to_sibling(17, R.tg_s.at[sib_rows], R.tg_r)

    def task_sums():
        chosen, owner = pick(width, small), owner_is(width, small)
        R.vec32[...] = jnp.zeros(R.vec32.shape, fl)
        for j in range(8):
            spread = jnp.where(owner, R.sums[j : j + 1, :], 0.0).astype(bf)
            R.vec32[pl.ds(j, GROUP, stride=16), :] = dot(spread, chosen, COLS_BOTH)
        spread = jnp.where(unit_owner(), R.upsum[0:1, :], 0.0).astype(bf)
        R.vec32[pl.ds(8, GROUP, stride=16), :] = dot(spread, pick(hquarter, large), COLS_BOTH)
        R.stage_vec[...] = R.vec32[...].astype(bf)
        to_sibling(24, R.stage_vec, R.peer_vec)

    def task_sums_send():
        arrived(24)
        R.part[VEC][...] = (R.vec32[...] + R.peer_vec[...].astype(fl)).astype(bf)
        scatter_start(8)

    def task_token_grad_sum():
        arrived(17)
        R.token_grad[...] = R.dat[...] + R.tg_s[own_rows, :] + R.tg_r[...]
        stores[1].start()

    call = functools.partial
    tasks = [(task_clear_sums, (), (), 0.1), (task_vectors, (8,), (), 0.6)]
    for two in range(3):
        tasks += [(call(task_qkv, two), (two,), (5, 6), 0.4)]
        tasks += [(call(task_attention, b, two), (), (), 0.9) for b in range(2)]
    tasks += [
        (task_project, (OUT,), (7, 45, 46), 1.0),
        (task_norm_one, (), (8,), 1.0),
        (call(task_up, 0), (4, 5), (9,), 1.8),
        (call(pass_on, R.hb, 29), (), (29, 30), 0.2),
        (call(task_up, 1), (), (31, 32), 1.8),
        (task_ffn, (6, 7), (33, 34), 1.5),
        (call(task_ffn_sum, 0), (), (35, 36), 0.2),
        (call(task_norm_two, 0), (), (11,), 0.7),
        (call(task_ffn_sum, 1), (), (47, 48), 0.2),
        (call(task_norm_two, 1), (), (49,), 0.7),
        (call(task_d_act, 0), (), (12,), 1.2),
        (call(pass_half, R.dfb, 37, 0), (), (37,), 0.1),
        (call(pass_half, R.dfb, 37, 1), (), (38,), 0.1),
        (call(task_d_act, 1), (), (39, 40), 1.2),
        (task_grad_down, (), (), 1.7),
        (task_d_pre, (), (41, 42), 0.6),
        (task_d_hidden, (), (), 1.5),
        (task_d_hidden_sum, (), (14,), 0.3),
        (task_grad_up, (), (), 1.0),
        (task_norm_one_back, (), (43, 44), 1.0),
        (task_d_context, (), (15,), 0.7),
        (task_grad_out, (), (), 0.5),
        (task_d_context_sum, (), (16,), 0.2),
    ]
    for two in range(3):
        tasks += [(call(task_attention_back, b, two), (), (), 0.75) for b in range(2)]
        tasks += [(call(task_grad_qkv, two), (), (), 0.4)]
    tasks += [
        (task_sums, (), (), 0.7),
        (task_token_grad, (), (), 1.0),
        (task_sums_send, (), (24,), 0.3),
        (task_token_grad_sum, (), (17,), 0.3),
    ]
    late, credit = [], 0
    while tasks or plan.pending or plan.waiting or late:
        plan.pump()
        while plan.pending and plan.pending[0][0] <= plan.now and not plan.pending[0][2][0]:
            key = heapq.heappop(plan.pending)[2]
            if key[0] is None:
                plan.here.add(key[1])
            else:
                late.append(key)
        ready = bool(tasks) and (
            all(done[k] == PIECES[k] for k in tasks[0][1]) and plan.here.issuperset(tasks[0][2])
        )
        if plan.pending and plan.pending[0][2][0] and plan.pending[0][0] <= plan.now:
            plan.now += 0.1
            on_gather(*heapq.heappop(plan.pending)[2][1:])
        elif late and (not ready or credit > 0):
            credit -= 1
            on_scatter(*late.pop(0)[1:])
        elif ready:
            task, _, _, cost = tasks.pop(0)
            plan.now += cost
            credit = ADDS_BETWEEN
            task()
        elif plan.pending:
            plan.now = max(plan.now, plan.pending[0][0])
        else:
            plan.now += 0.5
    for k, parts in ((3, (18 + DOWN,)), (2, (22, 27, 28)), (1, (18 + OUT,)), (0, (18, 19, 20))):
        for i in parts:
            arrived(i)
        if k == 2:
            for j in range(8):
                R.g[2][:, 2 * j * 192 : 2 * (j + 1) * 192] = jnp.concatenate(
                    [R.mixed[:, x * hhalf + j * 192 : x * hhalf + (j + 1) * 192] for x in (0, 1)],
                    axis=1,
                )
        if k == 0:
            for c in range(2):
                for two in range(3):
                    for p in range(3):
                        to = p * width + c * half + two * 128
                        at = (3 * c + two) * 384 + p * 128
                        R.g[0][:, to : to + 128] = R.mixed_qkv[:, at : at + 128]
        stores[3 + k].start()
    for store in stores:
        store.wait()
    for copy in sent:
        copy.wait_send()


def deliver_kernel(*refs):
    found, given, near = refs[:OUTPUTS], refs[OUTPUTS : 2 * OUTPUTS + 8], refs[2 * OUTPUTS + 8 :]
    singles, (in_sem, out_sem) = near[OUTPUTS:-2], near[-2:]
    loads = [pltpu.make_async_copy(f, n, in_sem.at[i]) for i, (f, n) in enumerate(zip(found, near))]
    for load in loads:
        load.start()
    stores = []

    def store(src, dst):
        copy = pltpu.make_async_copy(src, dst, out_sem.at[len(stores)])
        copy.start()
        stores.append(copy)

    loads[2].wait()
    for j, single in enumerate(singles):
        single[...] = near[2][j : j + 1, 0 : single.shape[1]]
        store(single, given[OUTPUTS - 1 + j])
    for i in (0, 4, 3, 1, 5, 6):
        loads[i].wait()
        store(near[i], given[i - (i > 2)])
    for copy in stores:
        copy.wait()


def fused(tokens, doc_ids, pad_mask, matrices, vectors, cotangent):
    rows, width = tokens.shape
    hidden = matrices[2].shape[1]
    fl = jnp.float32
    lists, named = scratch_of(rows, width, hidden)
    operands = (
        [tokens, doc_ids[None], pad_mask[None], cotangent]
        + list(matrices)
        + [v[None] for v in vectors]
    )
    results = [
        jax.ShapeDtypeStruct(tokens.shape, jnp.bfloat16),
        jax.ShapeDtypeStruct(tokens.shape, fl),
        jax.ShapeDtypeStruct((16, 128), fl),
    ] + [jax.ShapeDtypeStruct(m.shape, fl) for m in matrices]
    far = pl.BlockSpec(memory_space=pl.ANY)
    dma = pltpu.SemaphoreType.DMA
    found = pl.pallas_call(
        functools.partial(layer_kernel, tuple(named)),
        out_shape=results,
        in_specs=[far] * INPUTS,
        out_specs=[far] * OUTPUTS,
        scratch_shapes=[pltpu.VMEM(a.shape, a.dtype) for a in operands + results]
        + [pltpu.VMEM(shape, kind) for shape, kind in lists + list(named.values())]
        + [
            dma((SIBLING_COPIES,)),
            dma((SIBLING_COPIES,)),
            dma((TRAVELLERS, PAIRS)),
            dma((TRAVELLERS, PAIRS)),
            dma((TRAVELLERS, PAIRS)),
            dma((TRAVELLERS, PAIRS)),
            dma((INPUTS,)),
            dma((OUTPUTS,)),
        ],
        compiler_params=pltpu.CompilerParams(
            collective_id=0, has_side_effects=True, vmem_limit_bytes=FUSED_VMEM
        ),
        name="layer",
    )(*operands)
    singles = [jax.ShapeDtypeStruct((1, v.shape[0]), fl) for v in vectors]
    large = [r for i, r in enumerate(results) if i != 2]
    given = pl.pallas_call(
        deliver_kernel,
        out_shape=large + singles,
        in_specs=[far] * OUTPUTS,
        out_specs=[far] * (len(large) + len(singles)),
        scratch_shapes=[pltpu.VMEM(a.shape, a.dtype) for a in results + singles]
        + [dma((OUTPUTS,)), dma((OUTPUTS + len(singles),))],
        name="deliver",
    )(*found)
    layer_out, token_grad, g0, g1, g2, g3 = given[: len(large)]
    s = [v[0] for v in given[len(large) :]]
    return (
        layer_out,
        token_grad,
        g0,
        s[0],
        s[1],
        g1,
        s[2],
        s[3],
        s[4],
        g2,
        s[8],
        g3,
        s[5],
        s[6],
        s[7],
    )


def local(
    tokens,
    doc_ids,
    pad_mask,
    qkv_matrix,
    query_bias,
    value_bias,
    out_matrix,
    out_bias,
    attn_gain,
    attn_shift,
    up_matrix,
    up_bias,
    down_matrix,
    down_bias,
    ffn_gain,
    ffn_shift,
    cotangent,
):
    fl = jnp.float32
    if lax.axis_size(AXIS) == GROUP:
        return fused(
            tokens,
            doc_ids,
            pad_mask,
            (qkv_matrix, out_matrix, up_matrix, down_matrix),
            (
                query_bias,
                value_bias,
                out_bias,
                attn_gain,
                attn_shift,
                down_bias,
                ffn_gain,
                ffn_shift,
                up_bias,
            ),
            cotangent,
        )
    owned_vectors = (
        query_bias,
        value_bias,
        out_bias,
        attn_gain,
        attn_shift,
        down_bias,
        ffn_gain,
        ffn_shift,
        up_bias,
    )
    vectors = vector_rows([v[None] for v in owned_vectors])[0]
    wholes = [
        lax.all_gather(w, AXIS, axis=0, tiled=True)
        for w in (qkv_matrix, out_matrix, up_matrix, down_matrix, vectors)
    ]
    qkv_full, outm_full, upm_full, downm_full, vectors_full = wholes
    vectors_full = vectors_full.reshape((-1,) + vectors.shape)
    (
        qbias_full,
        vbias_full,
        outb_full,
        gain_one,
        shift_one,
        downb_full,
        gain_two,
        shift_two,
        upb_full,
    ) = (vectors_full[:, j, : v.shape[0]].reshape(-1) for j, v in enumerate(owned_vectors))
    qkv_back, outm_back, upm_back, downm_back = qkv_full, outm_full, upm_full, downm_full
    gain_one_back, gain_two_back = gain_one, gain_two
    row_count, model_width = tokens.shape
    head_size = model_width // HEADS
    score_scale = 1.0 / math.sqrt(head_size)
    hidden_width = upm_full.shape[1]
    ratio = hidden_width // model_width
    zero_part = jnp.zeros((model_width,), fl)
    qkv = jnp.dot(tokens, qkv_full, preferred_element_type=fl)
    qkv = (qkv + jnp.concatenate([qbias_full.astype(fl), zero_part, vbias_full.astype(fl)])).astype(
        jnp.bfloat16
    )
    query = qkv[:, :model_width].reshape(row_count, HEADS, head_size)
    key_rows = qkv[:, model_width : 2 * model_width].reshape(row_count, HEADS, head_size)
    value_rows = qkv[:, 2 * model_width :].reshape(row_count, HEADS, head_size)
    positions = jnp.arange(row_count)
    visible = (doc_ids[:, None] == doc_ids[None, :]) & (
        (pad_mask[None, :] == 1) | (positions[:, None] == positions[None, :])
    )
    scores = masked_scores(query, key_rows, visible, score_scale)
    row_max = jnp.max(scores, axis=-1, keepdims=True)
    log_total = row_max + jnp.log(jnp.sum(jnp.exp(scores - row_max), axis=-1, keepdims=True))
    probs_b = jnp.exp(scores - log_total).astype(jnp.bfloat16)
    context = jnp.einsum("hqk,khd->qhd", probs_b, value_rows, preferred_element_type=fl)
    context = context.reshape(row_count, model_width).astype(jnp.bfloat16)
    attn_sum = (
        tokens.astype(fl)
        + jnp.dot(context, outm_full, preferred_element_type=fl)
        + outb_full.astype(fl)
    )
    hidden, normed_one, inverse_one = layer_norm(
        attn_sum, gain_one.astype(fl), shift_one.astype(fl)
    )
    hidden_b = hidden.astype(jnp.bfloat16)
    pre_act = jnp.dot(hidden_b, upm_full, preferred_element_type=fl) + upb_full.astype(fl)
    cdf_part = 0.5 * (1.0 + jax.scipy.special.erf(pre_act * root_half))
    pdf_part = jnp.exp(-0.5 * pre_act * pre_act) * inv_root_two_pi
    activation = (pre_act * cdf_part).astype(jnp.bfloat16)
    ffn_sum = (
        hidden + jnp.dot(activation, downm_full, preferred_element_type=fl) + downb_full.astype(fl)
    )
    normed_out, normed_two, inverse_two = layer_norm(
        ffn_sum, gain_two.astype(fl), shift_two.astype(fl)
    )
    layer_out = normed_out.astype(jnp.bfloat16)
    upstream = cotangent.astype(fl)
    g_gain_two = jnp.sum(upstream * normed_two, axis=0)
    g_shift_two = jnp.sum(upstream, axis=0)
    d_ffn = norm_back(upstream, normed_two, inverse_two, gain_two_back.astype(fl))
    g_down_b = jnp.sum(d_ffn, axis=0)
    d_ffn_b = d_ffn.astype(jnp.bfloat16)
    d_act = jnp.einsum("rd,fd->rf", d_ffn_b, downm_back, preferred_element_type=fl)
    d_pre = d_act * (cdf_part + pre_act * pdf_part)
    g_up_b = jnp.sum(d_pre, axis=0)
    d_pre_b = d_pre.astype(jnp.bfloat16)
    d_hidden = d_ffn + jnp.einsum("rf,df->rd", d_pre_b, upm_back, preferred_element_type=fl)
    g_gain_one = jnp.sum(d_hidden * normed_one, axis=0)
    g_shift_one = jnp.sum(d_hidden, axis=0)
    d_attn = norm_back(d_hidden, normed_one, inverse_one, gain_one_back.astype(fl))
    g_out_b = jnp.sum(d_attn, axis=0)
    d_attn_b = d_attn.astype(jnp.bfloat16)
    d_context = jnp.einsum("re,de->rd", d_attn_b, outm_back, preferred_element_type=fl).astype(
        jnp.bfloat16
    )
    d_qkv, attn_sums = attention_back(qkv, d_context, doc_ids, pad_mask)
    g_qbias, g_vbias = attn_sums[0], attn_sums[1]
    token_grad = d_attn + jnp.einsum("re,de->rd", d_qkv, qkv_back, preferred_element_type=fl)
    sums = vector_rows(
        [
            g.reshape((lax.axis_size(AXIS), -1))
            for g in (
                g_qbias,
                g_vbias,
                g_out_b,
                g_gain_one,
                g_shift_one,
                g_down_b,
                g_gain_two,
                g_shift_two,
                g_up_b,
            )
        ]
    )
    pairs = ((tokens, d_qkv), (context, d_attn_b), (hidden_b, d_pre_b), (activation, d_ffn_b))
    owned = [
        lax.psum_scatter(p, AXIS, scatter_dimension=0, tiled=True)
        for p in [grad_rows(left, right) for left, right in pairs]
        + [sums.reshape((-1, sums.shape[2]))]
    ]
    grad_qkv, grad_outmat, grad_upmat, grad_downmat, vec = owned
    owned_sums = [vec[j, : v.shape[0]] for j, v in enumerate(owned_vectors)]
    return (
        layer_out,
        token_grad,
        grad_qkv,
        owned_sums[0],
        owned_sums[1],
        grad_outmat,
        owned_sums[2],
        owned_sums[3],
        owned_sums[4],
        grad_upmat,
        owned_sums[8],
        grad_downmat,
        owned_sums[5],
        owned_sums[6],
        owned_sums[7],
    )


def solution(mesh):
    placed = (
        P("fsdp", None),
        P("fsdp"),
        P("fsdp"),
        P("fsdp", None),
        P("fsdp"),
        P("fsdp"),
        P("fsdp", None),
        P("fsdp"),
        P("fsdp"),
        P("fsdp"),
        P("fsdp", None),
        P("fsdp"),
        P("fsdp", None),
        P("fsdp"),
        P("fsdp"),
        P("fsdp"),
        P("fsdp", None),
    )
    return jax.shard_map(
        local,
        mesh=mesh,
        in_specs=placed,
        out_specs=(
            P("fsdp", None),
            P("fsdp", None),
            P("fsdp", None),
            P("fsdp"),
            P("fsdp"),
            P("fsdp", None),
            P("fsdp"),
            P("fsdp"),
            P("fsdp"),
            P("fsdp", None),
            P("fsdp"),
            P("fsdp", None),
            P("fsdp"),
            P("fsdp"),
            P("fsdp"),
        ),
        check_vma=False,
    )
```

```python
import functools
import heapq
import math
import types

import jax
import jax.numpy as jnp
from jax import lax
from jax.experimental import pallas as pl
from jax.experimental.pallas import tpu as pltpu
from jax.sharding import PartitionSpec as P

HEADS = 12
AXIS = "fsdp"
MESH_IDS = pl.DeviceIdType.MESH
GROUP = 32


norm_eps = 1e-06
root_half = 0.7071067811865476
inv_root_two_pi = 0.3989422804014327


def layer_norm(values, gain, shift):
    centred = values - jnp.mean(values, axis=-1, keepdims=True)
    inverse = lax.rsqrt(jnp.mean(centred * centred, axis=-1, keepdims=True) + norm_eps)
    normed = centred * inverse
    return (normed * gain + shift, normed, inverse)


def norm_back(upstream, normed, inverse, gain):
    scaled = upstream * gain
    return inverse * (
        scaled
        - jnp.mean(scaled, axis=-1, keepdims=True)
        - normed * jnp.mean(scaled * normed, axis=-1, keepdims=True)
    )


def masked_scores(query, key_rows, visible, score_scale):
    scores = (
        jnp.einsum("qhd,khd->hqk", query, key_rows, preferred_element_type=jnp.float32)
        * score_scale
    )
    return jnp.where(visible[None], scores, -1e30)


def vector_rows(vectors):
    rows = [jnp.pad(v, ((0, 0), (0, 128 - v.shape[1]))) for v in vectors]
    rows = rows + [jnp.zeros_like(rows[0])] * (16 - len(rows))
    return jnp.stack(rows, axis=1)


def attention_back_kernel(
    scale, qkv_ref, back_ref, doc_col, doc_row, pad_row, d_qkv_ref, sums_ref
):
    fl = jnp.float32
    rows, width = back_ref.shape
    size = width // HEADS
    across, down, both = ((1,), (0,)), ((0,), (0,)), ((1,), (1,))

    def dot(a, b, over):
        return lax.dot_general(a, b, (over, ((), ())), preferred_element_type=fl)

    square = (rows, rows)
    same = lax.broadcasted_iota(jnp.int32, square, 0) == lax.broadcasted_iota(
        jnp.int32, square, 1
    )
    visible = (doc_col[...] == doc_row[...]) & ((pad_row[...] == 1) | same)
    for pair in range(HEADS // 2):
        results = []
        for h in (2 * pair, 2 * pair + 1):
            query, key_rows, value_rows = (
                qkv_ref[:, part * width + h * size : part * width + (h + 1) * size]
                for part in range(3)
            )
            back = back_ref[:, h * size : (h + 1) * size]
            scores = jnp.where(visible, dot(query, key_rows, both) * scale, -1e30)
            row_max = jnp.max(scores, axis=-1, keepdims=True)
            total = jnp.sum(jnp.exp(scores - row_max), axis=-1, keepdims=True)
            probs = jnp.exp(scores - (row_max + jnp.log(total)))
            d_value = dot(probs.astype(jnp.bfloat16), back, down)
            d_probs = dot(back, value_rows, both)
            delta = jnp.sum(probs * d_probs, axis=-1, keepdims=True)
            d_scores = (probs * (d_probs - delta) * scale).astype(jnp.bfloat16)
            results.append(
                (dot(d_scores, key_rows, across), dot(d_scores, query, down), d_value)
            )
        for part in range(3):
            block = jnp.concatenate([results[0][part], results[1][part]], axis=1)
            at = pair * 2 * size
            d_qkv_ref[:, part * width + at : part * width + at + 2 * size] = block.astype(
                jnp.bfloat16
            )
            if part != 1:
                row = part // 2
                sums_ref[row : row + 1, at : at + 2 * size] = jnp.sum(
                    block, axis=0, keepdims=True
                )


def attention_back(qkv, d_context, doc_ids, pad_mask):
    rows, width = d_context.shape
    return pl.pallas_call(
        functools.partial(attention_back_kernel, 1.0 / math.sqrt(width // HEADS)),
        out_shape=(
            jax.ShapeDtypeStruct(qkv.shape, jnp.bfloat16),
            jax.ShapeDtypeStruct((2, width), jnp.float32),
        ),
        compiler_params=pltpu.CompilerParams(vmem_limit_bytes=24 * 1024 * 1024),
        name="attention_back",
    )(qkv, d_context, doc_ids[:, None], doc_ids[None], pad_mask[None])


def grad_rows(left, right):
    return jnp.einsum("ra,rb->ab", left, right, preferred_element_type=jnp.float32)


X, Y, Z1, Z2 = 0, 1, 2, 3
GATHER_ORDERS = (
    (Z2, Z1, X, Y),
    (Z2, Z1, Y, X),
    (Y, Z2, Z1, X),
    (Z2, Z1, Y, X),
    (Z2, Z1, Y),
    (Z2, Z1, Y),
    (Z2, Z1, Y),
    (Y, Z2, Z1),
    (Y, Z2, Z1, X),
)
SCATTER_ORDERS = (
    (X, Z1, Z2, Y),
    (Y, X, Z1, Z2),
    (Y, X, Z1, Z2),
    (Y, X, Z1, Z2),
    (Y, Z1, Z2),
    (Y, Z1, Z2),
    (Y, Z1, Z2),
    (Z1, Z2, Y),
    (X, Z1, Z2, Y),
)
GATHER_FIRST = (0, 1, 2, 3, 4, 4, 5, 5, 0)
SCATTER_FIRST = (3, 0, 0, 1, 1, 2, 3, 1, 3)
ADDS_BETWEEN = 1
ADD_US = (0.225, 0.225, 0.225, 0.225, 0.3, 0.3, 0.3, 0.3, 0.12)
PAIRS = 16
PIECES = (16, 16, 16, 16, 8, 8, 8, 8, 16)
PIECE_ROWS = (48, 48, 48, 48, 96, 96, 96, 96, 32)
PIECE_COLS = (384, 384, 384, 384, 384, 384, 384, 384, 128)
TRAVELLERS = 9
BUFFER = (0, 1, 2, 3, 4, 4, 5, 5, 6)
PLACE_ROWS = (48, 48, 48, 48, 96, 192, 32)
PLACE_COLS = (384, 384, 384, 384, 768, 384, 128)
PLACES = (16, 16, 16, 16, 8, 8, 16)
OUT, UP, DOWN, VEC = 3, 4, 5, 6
QUAD = 4
COUNT = 7
HOPS = {X: ((0, 1),), Y: ((1, 1),), Z1: ((2, 1),), Z2: ((2, 1), (3, 2))}
LINK_BYTES_PER_US = 44e3
HOP_US = 1.5
CORE_BYTES_PER_US = 600e3
BACKLOG_US = 1.5
FUSED_VMEM = 58 * 1024 * 1024


class Plan:
    def __init__(self):
        self.now = 0.0
        self.free = {}
        self.pending = []
        self.waiting = []
        self.here = set()
        self.seq = 0

    def travel(self, dim, size, key):
        if dim is None:
            us, hops = size / CORE_BYTES_PER_US, ((4, 1),)
        else:
            us, hops = size / LINK_BYTES_PER_US, HOPS[dim]
        begin = max([self.now] + [self.free.get(link, 0.0) for link, _ in hops])
        end = begin
        for link, cost in hops:
            self.free[link] = begin + cost * us
            end = max(end, begin + cost * us)
        self.seq += 1
        heapq.heappush(self.pending, (end + HOP_US, self.seq, key))

    def ask(self, first, dim, size, key, start):
        self.seq += 1
        self.waiting.append((first, self.seq, dim, size, key, start))
        self.waiting.sort(key=lambda entry: entry[:2])

    def pump(self):
        left = []
        for entry in self.waiting:
            _, _, dim, size, key, start = entry
            if max(self.free.get(link, 0.0) for link, _ in HOPS[dim]) - self.now < BACKLOG_US:
                start()
                self.travel(dim, size, key)
            else:
                left.append(entry)
        self.waiting = left


def subsets(order, step):
    blocks = [0]
    for b in reversed(order[step + 1 :]):
        blocks = [r | (1 << b) for r in blocks] + blocks
    return blocks


def dot(a, b, over=((1,), (0,))):
    return lax.dot_general(a, b, (over, ((), ())), preferred_element_type=jnp.float32)


ROWS_BOTH, COLS_BOTH = ((0,), (0,)), ((1,), (1,))

SIBLING_COPIES = 58
INPUTS, OUTPUTS = 17, 7


def stage_shape(k):
    if k == UP:
        return ((QUAD, 32, PLACE_COLS[k]), jnp.bfloat16)
    return (((PLACE_ROWS[k] // 2 + 15) // 16 * 16, PLACE_COLS[k]), jnp.bfloat16)


def scratch_of(rows, width, hidden):
    fl, bf = jnp.float32, jnp.bfloat16
    both, half, quad = 2 * rows, width // 2, QUAD * rows
    hhalf, hquarter = hidden // 2, hidden // 4
    lists = []
    for shape_of in (
        lambda k: ((PLACES[k] * PLACE_ROWS[k], PLACE_COLS[k]), bf),
        lambda k: ((PLACES[k] * PLACE_ROWS[k], PLACE_COLS[k]), bf),
        stage_shape,
        stage_shape,
        lambda k: ((PLACE_ROWS[k], PLACE_COLS[k]), fl),
    ):
        lists += [shape_of(k) for k in range(COUNT)]
    lists += [((PIECES[k] - 1, PIECE_ROWS[k], PIECE_COLS[k]), bf) for k in range(TRAVELLERS)]
    named = dict(
        peer_vec=((PAIRS * PLACE_ROWS[VEC], PLACE_COLS[VEC]), bf),
        stage_vec=((PAIRS * PLACE_ROWS[VEC], PLACE_COLS[VEC]), bf),
        tok=((both, width), bf),
        marks=((2, 8, rows), fl),
        vec32=((PAIRS * 32, 128), fl),
        vecs=((16, width), fl),
        upb=((8, hquarter), fl),
        qkv=((both, 3 * half), bf),
        probs=((HEADS, rows, rows), fl),
        ctx=((both, width), bf),
        proj_s=((both, half), fl),
        proj_r=((rows, half), fl),
        hid=((rows, width), fl),
        n1=((rows, width), fl),
        i1=((rows, 128), fl),
        hb=((quad, width), bf),
        act=((quad, hhalf), bf),
        fac=((quad, hquarter), fl),
        ffn_s=((rows, half), fl),
        ffn_r=((rows, half), fl),
        ffn_o=((both, half), fl),
        ffn_xs=((both, half), bf),
        ffn_xr=((both, half), bf),
        dff=((rows, width), fl),
        dfb=((quad, width), bf),
        dact_s=((quad, hquarter), fl),
        dact_r=((quad, hquarter), fl),
        dact_o=((quad, hquarter), fl),
        dpre=((quad, hquarter), bf),
        dhid_s=((both, width), fl),
        dhid_r=((both, width), fl),
        dhid_o=((both, width), fl),
        dhid_xs=((rows, width), bf),
        dhid_xr=((rows, width), bf),
        dat=((rows, width), fl),
        datb=((both, width), bf),
        dctx_s=((both, half), fl),
        dctx_r=((both, half), fl),
        dctx_o=((both, half), fl),
        dctx=((both, half), bf),
        dqkv=((both, 3 * half), bf),
        tg_s=((both, width), fl),
        tg_r=((rows, width), fl),
        sums=((16, width), fl),
        upsum=((8, hquarter), fl),
        mixed=((width // GROUP, hidden), fl),
        mixed_qkv=((width // GROUP, 3 * width), fl),
    )
    return lists, named


def layer_kernel(names, *refs):
    refs = list(refs)

    def take(count):
        taken, refs[:count] = refs[:count], []
        return taken

    R = types.SimpleNamespace()
    far_in, far_out, near_in, near_out = take(INPUTS), take(OUTPUTS), take(INPUTS), take(OUTPUTS)
    R.tokens, R.doc, R.pad, R.cotangent = near_in[:4]
    R.w, R.v = near_in[4:8], near_in[8:]
    R.layer_out, R.token_grad, R.gv = near_out[:3]
    R.g = near_out[3:]
    R.whole, R.part, R.stage, R.peer, R.fin = (take(COUNT) for _ in range(5))
    R.land = take(TRAVELLERS)
    vars(R).update(zip(names, take(len(names))))
    sib_send, sib_recv, g_send, g_recv, s_send, s_recv, in_sem, out_sem = refs
    loads = [
        pltpu.make_async_copy(far, near, in_sem.at[i])
        for i, (far, near) in enumerate(zip(far_in, near_in))
    ]
    for i in (4, *range(8, 17), 5, 6, 7, 0, 1, 2, 3):
        loads[i].start()
    stores = [
        pltpu.make_async_copy(near, far, out_sem.at[i])
        for i, (far, near) in enumerate(zip(far_out, near_out))
    ]
    fl, bf = jnp.float32, jnp.bfloat16
    rows, width = R.tokens.shape
    hidden = R.w[2].shape[1]
    half, hhalf, hquarter = width // 2, hidden // 2, hidden // 4
    size = width // HEADS
    scale = 1.0 / math.sqrt(size)
    me = lax.axis_index(AXIS)
    core = lax.rem(me, 2)
    pair = lax.div(me, 2)
    bits = [lax.rem(lax.div(pair, 1 << b), 2) for b in range(4)]
    sibling = me + 1 - 2 * core
    is_first = core == 0

    def pair_of(r):
        p = pair
        for b in range(4):
            if r >> b & 1:
                p = p + (1 << b) * (1 - 2 * bits[b])
        return p

    def quad_of(r):
        q = lax.div(pair, 2)
        for b in range(1, 4):
            if r >> b & 1:
                q = q + (1 << (b - 1)) * (1 - 2 * bits[b])
        return q

    def device_along(b):
        return me + (2 << b) * (1 - 2 * bits[b])

    def by_core(step, which=None):
        at = core if which is None else 1 - core
        return pl.multiple_of(at * step, step)

    own_rows, sib_rows = pl.ds(by_core(rows), rows), pl.ds(by_core(rows, 1), rows)
    own_half, sib_half = pl.ds(by_core(half), half), pl.ds(by_core(half, 1), half)
    own_hq, sib_hq = pl.ds(by_core(hquarter), hquarter), pl.ds(by_core(hquarter, 1), hquarter)
    x_at = bits[X]
    across = device_along(X)
    diagonal = across + 1 - 2 * core
    member = 2 * x_at + core

    def quad_rows(other_x, other_core, count=rows, skip=0):
        at = 2 * (1 - x_at if other_x else x_at) + (1 - core if other_core else core)
        return pl.ds(pl.multiple_of(at * rows + skip, 64), count)

    def chip_rows(other_x):
        return pl.ds(pl.multiple_of((1 - x_at if other_x else x_at) * 2 * rows, 128), 2 * rows)


    barrier = pltpu.get_barrier_semaphore()
    for other in [sibling, diagonal] + [device_along(b) for b in range(4)]:
        pl.semaphore_signal(barrier, inc=1, device_id=(other,), device_id_type=MESH_IDS)
    pl.semaphore_wait(barrier, 6)

    plan = Plan()
    sib = {}
    sent = []

    def to_sibling(i, src, dst, device=None):
        copy = pltpu.make_async_remote_copy(
            src_ref=src,
            dst_ref=dst,
            send_sem=sib_send.at[i],
            recv_sem=sib_recv.at[i],
            device_id=(sibling if device is None else device,),
            device_id_type=MESH_IDS,
        )
        copy.start()
        sib[i] = copy
        sent.append(copy)
        plan.travel(None if device is None else X, math.prod(src.shape) * src.dtype.itemsize, (None, i))

    def arrived(i):
        sib.pop(i).wait_recv()

    def side_by_side(own, other):
        return jnp.concatenate(
            [jnp.where(is_first, own, other), jnp.where(is_first, other, own)], axis=1
        )

    def shard_half(k, mine):
        which = core if mine else 1 - core
        if k < 3:
            cols = [
                R.w[0][:, pl.ds(pl.multiple_of(p * width + which * half + k * 128, 128), 128)]
                for p in range(3)
            ]
            return jnp.concatenate([c.astype(fl) for c in cols], axis=1)
        cols = PLACE_COLS[k]
        ref = R.w[1] if k == OUT else R.w[3]
        return ref[:, pl.ds(by_core(cols, None if mine else 1), cols)].astype(fl)

    def padded(value):
        short = -value.shape[0] % 16
        if short:
            value = jnp.concatenate([value, jnp.zeros((short, value.shape[1]), fl)], axis=0)
        return value.astype(bf)

    for load in loads[4:]:
        load.wait()
    R.vec32[pl.ds(0, 16), :] = jnp.zeros((16, 128), fl)
    for j in range(9):
        v = R.v[j]
        R.vec32[j : j + 1, 0 : v.shape[1]] = v[...].astype(fl)
    R.stage[VEC][...] = R.vec32[pl.ds(0, 16), :].astype(bf)
    def quarter(q):
        blocks = []
        for j in range(4):
            at = (q % 2) * hhalf + 2 * j * 192 + (q // 2) * 192
            blocks.append(R.w[2][:, at : at + 192].astype(fl))
        return jnp.concatenate(blocks, axis=1)

    for k in (0, VEC, 1, 2, OUT, DOWN):
        if k != VEC:
            R.stage[k][...] = padded(shard_half(k, False))
        to_sibling(50 + k, R.stage[k], R.peer[k])
    for q in range(QUAD):
        R.stage[UP][q] = padded(quarter(q))
    for i, device, q in (
        (54, None, member + 1 - 2 * core),
        (25, across, member + 2 - 4 * x_at),
        (26, diagonal, 3 - member),
    ):
        to_sibling(i, R.stage[UP].at[q], R.peer[UP].at[member], device)
    for load in loads[:4]:
        load.wait()
    to_sibling(5, R.tokens, R.tok.at[own_rows])
    own_marks = jnp.concatenate(
        [R.doc[...].astype(fl), R.pad[...].astype(fl), jnp.zeros((6, rows), fl)], axis=0
    )
    R.marks[core] = own_marks
    to_sibling(6, R.marks.at[core], R.marks.at[core])
    R.tok[own_rows, :] = R.tokens[...]

    plan.now = 3.0
    piece_bytes = [2 * PIECE_ROWS[k] * PIECE_COLS[k] for k in range(TRAVELLERS)]
    done = [1] * TRAVELLERS

    def place_at(k, r):
        n = PLACE_ROWS[k]
        place = pair_of(r) if PLACES[k] == PAIRS else quad_of(r)
        return pl.multiple_of(place * n, n)

    def piece_of(refs, k, r):
        to = BUFFER[k]
        row, col = place_at(to, r), 0
        if k > 0 and BUFFER[k - 1] == to:
            if to == UP:
                col = PIECE_COLS[k]
            else:
                row = pl.multiple_of(row + PIECE_ROWS[k], PIECE_ROWS[k])
        return refs[to].at[pl.ds(row, PIECE_ROWS[k]), pl.ds(col, PIECE_COLS[k])]

    def gather_move(k, r, b):
        slot = r | (1 << b)
        copy = pltpu.make_async_remote_copy(
            src_ref=piece_of(R.whole, k, r),
            dst_ref=piece_of(R.whole, k, r),
            send_sem=g_send.at[k, slot],
            recv_sem=g_recv.at[k, slot],
            device_id=(device_along(b),),
            device_id_type=MESH_IDS,
        )
        sent.append(copy)
        plan.ask(GATHER_FIRST[k], b, piece_bytes[k], (True, k, slot, b), copy.start)

    for k in (0, VEC, 1, 2, OUT, DOWN, UP):
        arrived(50 + k)
        if k == UP:
            R.peer[UP][member] = R.stage[UP][member]
            arrived(25)
            arrived(26)
            rows_in = [R.peer[UP][q].astype(fl)[: width // GROUP] for q in range(QUAD)]
        else:
            mine = R.vec32[pl.ds(0, 16), :] if k == VEC else shard_half(k, True)
            theirs = R.peer[k][...].astype(fl)[: mine.shape[0]]
            rows_in = [jnp.where(is_first, mine, theirs), jnp.where(is_first, theirs, mine)]
        R.whole[k][pl.ds(place_at(k, 0), PLACE_ROWS[k]), :] = jnp.concatenate(
            rows_in, axis=0
        ).astype(bf)
        for j in range(TRAVELLERS):
            if BUFFER[j] == k:
                for b in GATHER_ORDERS[j]:
                    gather_move(j, 0, b)
        plan.pump()

    def on_gather(k, r, b):
        here = piece_of(R.whole, k, r)
        pltpu.make_async_remote_copy(
            src_ref=here,
            dst_ref=here,
            send_sem=g_send.at[k, r],
            recv_sem=g_recv.at[k, r],
            device_id=(device_along(b),),
            device_id_type=MESH_IDS,
        ).wait_recv()
        order = GATHER_ORDERS[k]
        for later in order[order.index(b) + 1 :]:
            gather_move(k, r, later)
        done[k] += 1

    slot_of = []
    for k in range(TRAVELLERS):
        table = {}
        for step in range(len(SCATTER_ORDERS[k])):
            for r in subsets(SCATTER_ORDERS[k], step):
                table[step, r] = len(table)
        slot_of.append(table)
    copies = {}

    def held(k, step, r):
        if step < 0:
            return piece_of(R.part, k, r)
        return R.land[k].at[slot_of[k][step, r]]

    def scatter_move(k, step, r):
        b = SCATTER_ORDERS[k][step]
        low = r & ~(1 << b)
        slot = slot_of[k][step, low]
        copy = pltpu.make_async_remote_copy(
            src_ref=held(k, step - 1, r),
            dst_ref=R.land[k].at[slot],
            send_sem=s_send.at[k, slot],
            recv_sem=s_recv.at[k, slot],
            device_id=(device_along(b),),
            device_id_type=MESH_IDS,
        )
        sent.append(copy)
        copies[k, step, low] = copy
        plan.ask(SCATTER_FIRST[k], b, piece_bytes[k], (False, k, step, low), copy.start)

    def scatter_start(k):
        order = SCATTER_ORDERS[k]
        for r in subsets(order, 0):
            scatter_move(k, 0, r | (1 << order[0]))

    def finish(k):
        if k == VEC:
            R.gv[...] = R.fin[VEC][pl.ds(by_core(16), 16), :]
            stores[2].start()
            return
        if k == UP:
            at = pl.ds(pl.multiple_of(x_at * hhalf + core * hquarter, 128), hquarter)
            n = PLACE_ROWS[UP] // QUAD

            def share(q):
                return R.fin[UP].at[pl.ds(pl.multiple_of(q * n, n), n)]

            for i, device, q in (
                (22, None, member + 1 - 2 * core),
                (27, across, member + 2 - 4 * x_at),
                (28, diagonal, 3 - member),
            ):
                to_sibling(i, share(q), R.mixed.at[:, at], device)
            R.mixed[:, at] = share(member)[...]
            return
        n = PLACE_ROWS[k] // 2
        mine = R.fin[k].at[pl.ds(by_core(n), n)]
        theirs = R.fin[k].at[pl.ds(by_core(n, 1), n)]
        if k < 3:
            into, at = R.mixed_qkv, pl.ds(pl.multiple_of((3 * core + k) * 384, 384), 384)
        else:
            into, at = R.g[1 if k == OUT else 3], own_half
        to_sibling(18 + k, theirs, into.at[:, at])
        into[:, at] = mine[...]

    unfinished = [BUFFER.count(k) for k in range(COUNT)]
    summed = set()
    early = {}

    def on_scatter(k, step, r):
        if step and (k, step - 1, r) not in summed:
            early[k, step - 1, r] = step
            return
        summed.add((k, step, r))
        plan.now += ADD_US[k]
        add_piece(k, step, r)
        if (k, step, r) in early:
            on_scatter(k, early[k, step, r], r)

    def add_piece(k, step, r):
        copies[k, step, r].wait_recv()
        order = SCATTER_ORDERS[k]
        before, now = held(k, step - 1, r), held(k, step, r)
        if step == len(order) - 1:
            to = BUFFER[k]
            row, col = 0, 0
            if k > 0 and BUFFER[k - 1] == to:
                row, col = (0, PIECE_COLS[k]) if to == UP else (PIECE_ROWS[k], 0)
            R.fin[to][row : row + PIECE_ROWS[k], col : col + PIECE_COLS[k]] = now[...].astype(
                fl
            ) + before[...].astype(fl)
            unfinished[to] -= 1
            if not unfinished[to]:
                finish(to)
            return
        now[...] = now[...] + before[...]
        if r >> order[step + 1] & 1:
            scatter_move(k, step + 1, r)

    def column_of(n, period):
        return jnp.floor((n + 0.5) * (1.0 / period))

    def pick(count, period):
        n = lax.broadcasted_iota(jnp.int32, (128, count), 1).astype(fl)
        i = lax.broadcasted_iota(jnp.int32, (128, count), 0).astype(fl)
        return jnp.where(n - period * column_of(n, period) == i, 1.0, 0.0).astype(bf)

    def owner_is(count, period):
        n = lax.broadcasted_iota(jnp.int32, (GROUP, count), 1).astype(fl)
        d = lax.broadcasted_iota(jnp.int32, (GROUP, count), 0).astype(fl)
        return column_of(n, period) == d

    small, large = width // GROUP, hidden // GROUP

    def unit_owner():
        n = lax.broadcasted_iota(jnp.int32, (GROUP, hquarter), 1).astype(fl)
        d = lax.broadcasted_iota(jnp.int32, (GROUP, hquarter), 0).astype(fl)
        block = column_of(n, large)
        quad = column_of(block, 2)
        first = (16 * core + 2 * x_at).astype(fl)
        return first + 4.0 * quad + (block - 2.0 * quad) == d

    def task_vectors():
        R.vec32[...] = R.whole[VEC][...].astype(fl)
        chosen, owner = pick(width, small), owner_is(width, small)
        for j in range(8):
            v = R.vec32[pl.ds(j, GROUP, stride=16), :].astype(bf)
            R.vecs[j : j + 1, :] = jnp.sum(
                jnp.where(owner, dot(v, chosen), 0.0), axis=0, keepdims=True
            )
        v = R.vec32[pl.ds(8, GROUP, stride=16), :].astype(bf)
        R.upb[0:1, :] = jnp.sum(
            jnp.where(unit_owner(), dot(v, pick(hquarter, large)), 0.0),
            axis=0,
            keepdims=True,
        )

    def vec(j):
        return R.vecs[j : j + 1, :]

    def task_qkv(two):
        if two == 0:
            arrived(5)
            arrived(6)
        value = dot(R.tok[...], R.whole[two][...])
        for p in range(3):
            block = value[:, p * 128 : (p + 1) * 128]
            if p != 1:
                at = pl.ds(pl.multiple_of(core * half + two * 128, 128), 128)
                block = block + R.vecs[p // 2 : p // 2 + 1, at]
            R.qkv[:, two * 384 + p * 128 : two * 384 + (p + 1) * 128] = block.astype(bf)

    def seen(b):
        doc, pad = R.marks[b, 0:1, :], R.marks[b, 1:2, :]
        square = (rows, rows)
        wide = jnp.broadcast_to(doc, square)
        same = lax.broadcasted_iota(jnp.int32, square, 0) == lax.broadcasted_iota(
            jnp.int32, square, 1
        )
        return (wide.T == wide) & ((jnp.broadcast_to(pad, square) == 1.0) | same)

    def head_of(b, h):
        at = b * rows
        first = h // 2 * 384 + h % 2 * size
        return [
            R.qkv[at : at + rows, first + p * 128 : first + p * 128 + size] for p in range(3)
        ]

    def task_attention(b, two):
        visible = seen(b)
        found = []
        for h in (2 * two, 2 * two + 1):
            query, key_rows, value_rows = head_of(b, h)
            scores = jnp.where(visible, dot(query, key_rows, COLS_BOTH) * scale, -1e30)
            row_max = jnp.max(scores, axis=-1, keepdims=True)
            total = jnp.sum(jnp.exp(scores - row_max), axis=-1, keepdims=True)
            probs = jnp.exp(scores - (row_max + jnp.log(total)))
            R.probs[b * (HEADS // 2) + h] = probs
            found.append(dot(probs.astype(bf), value_rows))
        at = pl.ds(pl.multiple_of(core * half + two * 2 * size, 128), 2 * size)
        R.ctx[pl.ds(b * rows, rows), at] = jnp.concatenate(found, axis=1).astype(bf)
        if b == 1:
            to_sibling((7, 45, 46)[two], R.ctx.at[:, at], R.ctx.at[:, at])

    def task_project():
        arrived(7)
        arrived(45)
        arrived(46)
        R.proj_s[...] = dot(R.ctx[...], R.whole[OUT][...])
        to_sibling(8, R.proj_s.at[sib_rows], R.proj_r)

    def norm(values):
        centred = values - jnp.mean(values, axis=-1, keepdims=True)
        inverse = lax.rsqrt(jnp.mean(centred * centred, axis=-1, keepdims=True) + norm_eps)
        return centred * inverse, inverse

    def task_norm_one():
        arrived(8)
        attn = (
            R.tokens[...].astype(fl)
            + side_by_side(R.proj_s[own_rows, :], R.proj_r[...])
            + vec(2)
        )
        normed, inverse = norm(attn)
        hid = normed * vec(3) + vec(4)
        R.n1[...] = normed
        R.i1[...] = jnp.broadcast_to(inverse, (rows, 128))
        R.hid[...] = hid
        R.hb[quad_rows(0, 0), :] = hid.astype(bf)
        spread_rows(R.hb, 9, 29)

    tile = 384

    def spread_rows(ref, i, first):
        for skip in (0, 1):
            at = quad_rows(0, 0, rows // 2, skip * (rows // 2))
            to_sibling(first + skip, ref.at[at], ref.at[at], across)
        at = quad_rows(0, 0)
        to_sibling(i, ref.at[at], ref.at[at])

    def pass_on(ref, first):
        for skip in (0, 1):
            arrived(first + skip)
            at = quad_rows(1, 0, rows // 2, skip * (rows // 2))
            to_sibling(first + 2 + skip, ref.at[at], ref.at[at])

    def task_up(other):
        if other:
            arrived(31)
            arrived(32)
        else:
            arrived(9)
        to = chip_rows(other)

        def body(t, carry):
            at = pl.ds(pl.multiple_of(t * tile, tile), tile)
            pre = dot(R.hb[to, :], R.whole[UP][:, at]) + R.upb[0:1, at]
            cdf = 0.5 * (1.0 + lax.erf(pre * root_half))
            pdf = jnp.exp(-0.5 * pre * pre) * inv_root_two_pi
            R.fac[to, at] = cdf + pre * pdf
            R.act[to, pl.ds(pl.multiple_of(core * hquarter + t * tile, tile), tile)] = (
                pre * cdf
            ).astype(bf)
            return carry

        lax.fori_loop(0, hquarter // tile, body, 0)
        to_sibling(33 + other, R.act.at[to, own_hq], R.act.at[to, own_hq])

    def task_ffn():
        arrived(33)
        arrived(34)
        R.ffn_xs[...] = dot(R.act[chip_rows(1), :], R.whole[DOWN][...]).astype(bf)
        for part, ids in ((0, (35, 36)), (1, (47, 48))):
            for i, other_core in zip(ids, (1, 0)):
                at = local_rows(other_core, part)
                to_sibling(i, R.ffn_xs.at[at], R.ffn_xr.at[at], across)
        R.ffn_o[...] = dot(R.act[chip_rows(0), :], R.whole[DOWN][...])

    def local_rows(other_core, part):
        at = (1 - core if other_core else core) * rows + part * (rows // 2)
        return pl.ds(pl.multiple_of(at, 64), rows // 2)

    def task_ffn_sum(part):
        arrived((35, 47)[part])
        at, to = local_rows(1, part), pl.ds(part * (rows // 2), rows // 2)
        R.ffn_s[to, :] = R.ffn_o[at, :] + R.ffn_xr[at, :].astype(fl)
        to_sibling((11, 49)[part], R.ffn_s.at[to], R.ffn_r.at[to])
        arrived((36, 48)[part])

    def back_of_norm(upstream, normed, inverse, gain):
        scaled = upstream * gain
        return inverse * (
            scaled
            - jnp.mean(scaled, axis=-1, keepdims=True)
            - normed * jnp.mean(scaled * normed, axis=-1, keepdims=True)
        )

    def add_sum(j, values, more=False):
        total = jnp.sum(values, axis=0, keepdims=True)
        R.sums[j : j + 1, :] = R.sums[j : j + 1, :] + total if more else total

    def task_norm_two(part):
        arrived((11, 49)[part])
        at, to = local_rows(0, part), pl.ds(part * (rows // 2), rows // 2)
        mine = R.ffn_o[at, :] + R.ffn_xr[at, :].astype(fl)
        total = R.hid[to, :] + side_by_side(mine, R.ffn_r[to, :]) + vec(5)
        normed, inverse = norm(total)
        R.layer_out[to, :] = (normed * vec(6) + vec(7)).astype(bf)
        upstream = R.cotangent[to, :].astype(fl)
        d_ffn = back_of_norm(upstream, normed, inverse, vec(6))
        R.dff[to, :] = d_ffn
        rows_at = quad_rows(0, 0, rows // 2, part * (rows // 2))
        R.dfb[rows_at, :] = d_ffn.astype(bf)
        to_sibling(37 + part, R.dfb.at[rows_at], R.dfb.at[rows_at], across)
        add_sum(6, upstream * normed, part)
        add_sum(7, upstream, part)
        add_sum(5, d_ffn, part)
        if part:
            stores[0].start()
            rows_at = quad_rows(0, 0)
            to_sibling(12, R.dfb.at[rows_at], R.dfb.at[rows_at])

    def pass_half(ref, first, part):
        arrived(first + part)
        at = quad_rows(1, 0, rows // 2, part * (rows // 2))
        to_sibling(first + 2 + part, ref.at[at], ref.at[at])

    def task_grad_down():
        def body(t, carry):
            at = pl.ds(pl.multiple_of(t * tile, tile), tile)
            R.part[DOWN][at, :] = dot(R.act[:, at], R.dfb[:, own_half], ROWS_BOTH).astype(bf)
            return carry

        lax.fori_loop(0, hhalf // tile, body, 0)
        scatter_start(6)
        scatter_start(7)

    def task_d_act(other):
        if other:
            arrived(39)
            arrived(40)
        else:
            arrived(12)
        at = chip_rows(other)
        right = R.dfb[at, own_half]
        R.dact_s[at, :] = dot(right, R.whole[DOWN][sib_hq, :], COLS_BOTH)
        to_sibling(41 + other, R.dact_s.at[at], R.dact_r.at[at])
        R.dact_o[at, :] = dot(right, R.whole[DOWN][own_hq, :], COLS_BOTH)

    def task_d_pre():
        arrived(41)
        arrived(42)

        def body(t, carry):
            at = pl.ds(pl.multiple_of(t * tile, tile), tile)
            value = (R.dact_o[:, at] + R.dact_r[:, at]) * R.fac[:, at]
            R.upsum[0:1, at] = jnp.sum(value, axis=0, keepdims=True)
            R.dpre[:, at] = value.astype(bf)
            return carry

        lax.fori_loop(0, hquarter // tile, body, 0)

    def task_d_hidden():
        for other_core, into in ((1, R.dhid_s), (0, R.dhid_o)):
            left = jnp.concatenate(
                [R.dpre[quad_rows(other_x, other_core), :] for other_x in (0, 1)], axis=0
            )
            into[...] = dot(left, R.whole[UP][...], COLS_BOTH)
            if other_core:
                for i, other_x in ((14, 1), (43, 0)):
                    at = pl.ds(other_x * rows, rows)
                    to_sibling(i, R.dhid_s.at[at], R.dhid_r.at[at])

    def task_d_hidden_sum():
        arrived(14)
        at = pl.ds(rows, rows)
        R.dhid_xs[...] = (R.dhid_o[at, :] + R.dhid_r[at, :]).astype(bf)
        to_sibling(44, R.dhid_xs, R.dhid_xr, across)

    def task_grad_up():
        for t in range(2):
            at = pl.ds(t * tile, tile)
            R.part[UP][:, at] = dot(R.hb[...], R.dpre[:, at], ROWS_BOTH).astype(bf)
            scatter_start(4 + t)

    def task_norm_one_back():
        arrived(43)
        arrived(44)
        at = pl.ds(0, rows)
        d_hid = R.dff[...] + R.dhid_o[at, :] + R.dhid_r[at, :] + R.dhid_xr[...].astype(fl)
        normed = R.n1[...]
        d_attn = back_of_norm(d_hid, normed, R.i1[:, 0:1], vec(3))
        R.dat[...] = d_attn
        R.datb[own_rows, :] = d_attn.astype(bf)
        to_sibling(15, R.datb.at[own_rows], R.datb.at[own_rows])
        add_sum(3, d_hid * normed)
        add_sum(4, d_hid)
        add_sum(2, d_attn)

    def task_d_context():
        arrived(15)
        right = R.datb[:, own_half]
        R.dctx_s[...] = dot(right, R.whole[OUT][sib_half, :], COLS_BOTH)
        to_sibling(16, R.dctx_s, R.dctx_r)
        R.dctx_o[...] = dot(right, R.whole[OUT][own_half, :], COLS_BOTH)

    def task_grad_out():
        R.part[OUT][...] = dot(R.ctx[...], R.datb[:, own_half], ROWS_BOTH).astype(bf)
        scatter_start(OUT)

    def task_d_context_sum():
        arrived(16)
        R.dctx[...] = (R.dctx_o[...] + R.dctx_r[...]).astype(bf)

    bias_sums = {}

    def task_attention_back(b, two):
        found = []
        at = b * rows
        for h in (2 * two, 2 * two + 1):
            query, key_rows, value_rows = head_of(b, h)
            back = R.dctx[at : at + rows, h * size : (h + 1) * size]
            probs = R.probs[b * (HEADS // 2) + h]
            d_value = dot(probs.astype(bf), back, ROWS_BOTH)
            d_probs = dot(back, value_rows, COLS_BOTH)
            delta = jnp.sum(probs * d_probs, axis=-1, keepdims=True)
            d_scores = (probs * (d_probs - delta) * scale).astype(bf)
            found.append((dot(d_scores, key_rows), dot(d_scores, query, ROWS_BOTH), d_value))
        for p in range(3):
            block = jnp.concatenate([found[0][p], found[1][p]], axis=1)
            cols = two * 384 + p * 128
            R.dqkv[at : at + rows, cols : cols + 2 * size] = block.astype(bf)
            if p != 1:
                total = jnp.sum(block, axis=0, keepdims=True)
                if b == 0:
                    bias_sums[p, two] = total
                else:
                    to = pl.ds(pl.multiple_of(core * half + two * 2 * size, 128), 2 * size)
                    R.sums[p // 2 : p // 2 + 1, to] = total + bias_sums[p, two]

    def task_clear_sums():
        R.sums[...] = jnp.zeros(R.sums.shape, fl)

    def task_grad_qkv(two):
        at = pl.ds(two * 384, 384)
        R.part[two][...] = dot(R.tok[...], R.dqkv[:, at], ROWS_BOTH).astype(bf)
        scatter_start(two)

    def task_token_grad():
        R.tg_s[...] = sum(
            dot(R.dqkv[:, pl.ds(two * 384, 384)], R.whole[two][...], COLS_BOTH)
            for two in range(3)
        )
        to_sibling(17, R.tg_s.at[sib_rows], R.tg_r)

    def task_sums():
        chosen, owner = pick(width, small), owner_is(width, small)
        R.vec32[...] = jnp.zeros(R.vec32.shape, fl)
        for j in range(8):
            spread = jnp.where(owner, R.sums[j : j + 1, :], 0.0).astype(bf)
            R.vec32[pl.ds(j, GROUP, stride=16), :] = dot(spread, chosen, COLS_BOTH)
        spread = jnp.where(unit_owner(), R.upsum[0:1, :], 0.0).astype(bf)
        R.vec32[pl.ds(8, GROUP, stride=16), :] = dot(spread, pick(hquarter, large), COLS_BOTH)
        R.stage_vec[...] = R.vec32[...].astype(bf)
        to_sibling(24, R.stage_vec, R.peer_vec)

    def task_sums_send():
        arrived(24)
        R.part[VEC][...] = (R.vec32[...] + R.peer_vec[...].astype(fl)).astype(bf)
        scatter_start(8)

    def task_token_grad_sum():
        arrived(17)
        R.token_grad[...] = R.dat[...] + R.tg_s[own_rows, :] + R.tg_r[...]
        stores[1].start()

    def task_store_down():
        arrived(18 + DOWN)
        stores[6].start()

    def task_store_out():
        arrived(18 + OUT)
        stores[4].start()

    def task_store_up():
        for i in (22, 27, 28):
            arrived(i)
        for j in range(8):
            R.g[2][:, 2 * j * 192 : 2 * (j + 1) * 192] = jnp.concatenate(
                [R.mixed[:, x * hhalf + j * 192 : x * hhalf + (j + 1) * 192] for x in (0, 1)],
                axis=1,
            )
        stores[5].start()

    call = functools.partial
    tasks = [(task_clear_sums, (), (), 0.1), (task_vectors, (8,), (), 0.6)]
    for two in range(3):
        tasks += [(call(task_qkv, two), (two,), (5, 6), 0.4)]
        tasks += [(call(task_attention, b, two), (), (), 0.9) for b in range(2)]
    tasks += [
        (task_project, (OUT,), (7, 45, 46), 1.0),
        (task_norm_one, (), (8,), 1.0),
        (call(task_up, 0), (4, 5), (9,), 1.8),
        (call(pass_on, R.hb, 29), (), (29, 30), 0.2),
        (call(task_up, 1), (), (31, 32), 1.8),
        (task_ffn, (6, 7), (33, 34), 1.5),
        (call(task_ffn_sum, 0), (), (35, 36), 0.2),
        (call(task_norm_two, 0), (), (11,), 0.7),
        (call(task_ffn_sum, 1), (), (47, 48), 0.2),
        (call(task_norm_two, 1), (), (49,), 0.7),
        (call(task_d_act, 0), (), (12,), 1.2),
        (call(pass_half, R.dfb, 37, 0), (), (37,), 0.1),
        (call(pass_half, R.dfb, 37, 1), (), (38,), 0.1),
        (call(task_d_act, 1), (), (39, 40), 1.2),
        (task_grad_down, (), (), 1.7),
        (task_d_pre, (), (41, 42), 0.6),
        (task_d_hidden, (), (), 1.5),
        (task_grad_up, (), (), 1.0),
        (task_d_hidden_sum, (), (14,), 0.3),
        (task_norm_one_back, (), (43, 44), 1.0),
        (task_d_context, (), (15,), 0.7),
        (task_grad_out, (), (), 0.5),
        (task_d_context_sum, (), (16,), 0.2),
    ]
    for two in range(3):
        tasks += [(call(task_attention_back, b, two), (), (), 0.75) for b in range(2)]
        tasks += [(call(task_grad_qkv, two), (), (), 0.4)]
    tasks += [
        (task_sums, (), (), 0.7),
        (task_token_grad, (), (), 1.0),
        (task_sums_send, (), (24,), 0.3),
        (task_token_grad_sum, (), (17,), 0.3),
    ]
    tasks += [
        (task_store_down, (), (18 + DOWN,), 0.1),
        (task_store_up, (), (22, 27, 28), 1.0),
        (task_store_out, (), (18 + OUT,), 0.1),
    ]
    late, credit = [], 0
    while tasks or plan.pending or plan.waiting or late:
        plan.pump()
        while plan.pending and plan.pending[0][0] <= plan.now and not plan.pending[0][2][0]:
            key = heapq.heappop(plan.pending)[2]
            if key[0] is None:
                plan.here.add(key[1])
            else:
                late.append(key)
        ready = bool(tasks) and (
            all(done[k] == PIECES[k] for k in tasks[0][1]) and plan.here.issuperset(tasks[0][2])
        )
        if plan.pending and plan.pending[0][2][0] and plan.pending[0][0] <= plan.now:
            plan.now += 0.1
            on_gather(*heapq.heappop(plan.pending)[2][1:])
        elif late and (not ready or credit > 0):
            credit -= 1
            on_scatter(*late.pop(0)[1:])
        elif ready:
            task, _, _, cost = tasks.pop(0)
            plan.now += cost
            credit = ADDS_BETWEEN
            task()
        elif plan.pending:
            plan.now = max(plan.now, plan.pending[0][0])
        else:
            plan.now += 0.5
    for i in (18, 19, 20):
        arrived(i)
    for c in range(2):
        for two in range(3):
            for p in range(3):
                to = p * width + c * half + two * 128
                at = (3 * c + two) * 384 + p * 128
                R.g[0][:, to : to + 128] = R.mixed_qkv[:, at : at + 128]
    stores[3].start()
    for store in stores:
        store.wait()
    for copy in sent:
        copy.wait_send()


def deliver_kernel(*refs):
    found, given, near = refs[:OUTPUTS], refs[OUTPUTS : 2 * OUTPUTS + 8], refs[2 * OUTPUTS + 8 :]
    singles, (in_sem, out_sem) = near[OUTPUTS:-2], near[-2:]
    loads = [pltpu.make_async_copy(f, n, in_sem.at[i]) for i, (f, n) in enumerate(zip(found, near))]
    for load in loads:
        load.start()
    stores = []

    def store(src, dst):
        copy = pltpu.make_async_copy(src, dst, out_sem.at[len(stores)])
        copy.start()
        stores.append(copy)

    loads[2].wait()
    for j, single in enumerate(singles):
        single[...] = near[2][j : j + 1, 0 : single.shape[1]]
        store(single, given[OUTPUTS - 1 + j])
    for i in (0, 4, 3, 1, 5, 6):
        loads[i].wait()
        store(near[i], given[i - (i > 2)])
    for copy in stores:
        copy.wait()


def fused(tokens, doc_ids, pad_mask, matrices, vectors, cotangent):
    rows, width = tokens.shape
    hidden = matrices[2].shape[1]
    fl = jnp.float32
    lists, named = scratch_of(rows, width, hidden)
    operands = (
        [tokens, doc_ids[None], pad_mask[None], cotangent]
        + list(matrices)
        + [v[None] for v in vectors]
    )
    results = [
        jax.ShapeDtypeStruct(tokens.shape, jnp.bfloat16),
        jax.ShapeDtypeStruct(tokens.shape, fl),
        jax.ShapeDtypeStruct((16, 128), fl),
    ] + [jax.ShapeDtypeStruct(m.shape, fl) for m in matrices]
    far = pl.BlockSpec(memory_space=pl.ANY)
    dma = pltpu.SemaphoreType.DMA
    found = pl.pallas_call(
        functools.partial(layer_kernel, tuple(named)),
        out_shape=results,
        in_specs=[far] * INPUTS,
        out_specs=[far] * OUTPUTS,
        scratch_shapes=[pltpu.VMEM(a.shape, a.dtype) for a in operands + results]
        + [pltpu.VMEM(shape, kind) for shape, kind in lists + list(named.values())]
        + [
            dma((SIBLING_COPIES,)),
            dma((SIBLING_COPIES,)),
            dma((TRAVELLERS, PAIRS)),
            dma((TRAVELLERS, PAIRS)),
            dma((TRAVELLERS, PAIRS)),
            dma((TRAVELLERS, PAIRS)),
            dma((INPUTS,)),
            dma((OUTPUTS,)),
        ],
        compiler_params=pltpu.CompilerParams(
            collective_id=0, has_side_effects=True, vmem_limit_bytes=FUSED_VMEM
        ),
        name="layer",
    )(*operands)
    singles = [jax.ShapeDtypeStruct((1, v.shape[0]), fl) for v in vectors]
    large = [r for i, r in enumerate(results) if i != 2]
    given = pl.pallas_call(
        deliver_kernel,
        out_shape=large + singles,
        in_specs=[far] * OUTPUTS,
        out_specs=[far] * (len(large) + len(singles)),
        scratch_shapes=[pltpu.VMEM(a.shape, a.dtype) for a in results + singles]
        + [dma((OUTPUTS,)), dma((OUTPUTS + len(singles),))],
        name="deliver",
    )(*found)
    layer_out, token_grad, g0, g1, g2, g3 = given[: len(large)]
    s = [v[0] for v in given[len(large) :]]
    return (
        layer_out,
        token_grad,
        g0,
        s[0],
        s[1],
        g1,
        s[2],
        s[3],
        s[4],
        g2,
        s[8],
        g3,
        s[5],
        s[6],
        s[7],
    )


def local(
    tokens,
    doc_ids,
    pad_mask,
    qkv_matrix,
    query_bias,
    value_bias,
    out_matrix,
    out_bias,
    attn_gain,
    attn_shift,
    up_matrix,
    up_bias,
    down_matrix,
    down_bias,
    ffn_gain,
    ffn_shift,
    cotangent,
):
    fl = jnp.float32
    if lax.axis_size(AXIS) == GROUP:
        return fused(
            tokens,
            doc_ids,
            pad_mask,
            (qkv_matrix, out_matrix, up_matrix, down_matrix),
            (
                query_bias,
                value_bias,
                out_bias,
                attn_gain,
                attn_shift,
                down_bias,
                ffn_gain,
                ffn_shift,
                up_bias,
            ),
            cotangent,
        )
    owned_vectors = (
        query_bias,
        value_bias,
        out_bias,
        attn_gain,
        attn_shift,
        down_bias,
        ffn_gain,
        ffn_shift,
        up_bias,
    )
    vectors = vector_rows([v[None] for v in owned_vectors])[0]
    wholes = [
        lax.all_gather(w, AXIS, axis=0, tiled=True)
        for w in (qkv_matrix, out_matrix, up_matrix, down_matrix, vectors)
    ]
    qkv_full, outm_full, upm_full, downm_full, vectors_full = wholes
    vectors_full = vectors_full.reshape((-1,) + vectors.shape)
    (
        qbias_full,
        vbias_full,
        outb_full,
        gain_one,
        shift_one,
        downb_full,
        gain_two,
        shift_two,
        upb_full,
    ) = (vectors_full[:, j, : v.shape[0]].reshape(-1) for j, v in enumerate(owned_vectors))
    qkv_back, outm_back, upm_back, downm_back = qkv_full, outm_full, upm_full, downm_full
    gain_one_back, gain_two_back = gain_one, gain_two
    row_count, model_width = tokens.shape
    head_size = model_width // HEADS
    score_scale = 1.0 / math.sqrt(head_size)
    hidden_width = upm_full.shape[1]
    ratio = hidden_width // model_width
    zero_part = jnp.zeros((model_width,), fl)
    qkv = jnp.dot(tokens, qkv_full, preferred_element_type=fl)
    qkv = (qkv + jnp.concatenate([qbias_full.astype(fl), zero_part, vbias_full.astype(fl)])).astype(
        jnp.bfloat16
    )
    query = qkv[:, :model_width].reshape(row_count, HEADS, head_size)
    key_rows = qkv[:, model_width : 2 * model_width].reshape(row_count, HEADS, head_size)
    value_rows = qkv[:, 2 * model_width :].reshape(row_count, HEADS, head_size)
    positions = jnp.arange(row_count)
    visible = (doc_ids[:, None] == doc_ids[None, :]) & (
        (pad_mask[None, :] == 1) | (positions[:, None] == positions[None, :])
    )
    scores = masked_scores(query, key_rows, visible, score_scale)
    row_max = jnp.max(scores, axis=-1, keepdims=True)
    log_total = row_max + jnp.log(jnp.sum(jnp.exp(scores - row_max), axis=-1, keepdims=True))
    probs_b = jnp.exp(scores - log_total).astype(jnp.bfloat16)
    context = jnp.einsum("hqk,khd->qhd", probs_b, value_rows, preferred_element_type=fl)
    context = context.reshape(row_count, model_width).astype(jnp.bfloat16)
    attn_sum = (
        tokens.astype(fl)
        + jnp.dot(context, outm_full, preferred_element_type=fl)
        + outb_full.astype(fl)
    )
    hidden, normed_one, inverse_one = layer_norm(
        attn_sum, gain_one.astype(fl), shift_one.astype(fl)
    )
    hidden_b = hidden.astype(jnp.bfloat16)
    pre_act = jnp.dot(hidden_b, upm_full, preferred_element_type=fl) + upb_full.astype(fl)
    cdf_part = 0.5 * (1.0 + jax.scipy.special.erf(pre_act * root_half))
    pdf_part = jnp.exp(-0.5 * pre_act * pre_act) * inv_root_two_pi
    activation = (pre_act * cdf_part).astype(jnp.bfloat16)
    ffn_sum = (
        hidden + jnp.dot(activation, downm_full, preferred_element_type=fl) + downb_full.astype(fl)
    )
    normed_out, normed_two, inverse_two = layer_norm(
        ffn_sum, gain_two.astype(fl), shift_two.astype(fl)
    )
    layer_out = normed_out.astype(jnp.bfloat16)
    upstream = cotangent.astype(fl)
    g_gain_two = jnp.sum(upstream * normed_two, axis=0)
    g_shift_two = jnp.sum(upstream, axis=0)
    d_ffn = norm_back(upstream, normed_two, inverse_two, gain_two_back.astype(fl))
    g_down_b = jnp.sum(d_ffn, axis=0)
    d_ffn_b = d_ffn.astype(jnp.bfloat16)
    d_act = jnp.einsum("rd,fd->rf", d_ffn_b, downm_back, preferred_element_type=fl)
    d_pre = d_act * (cdf_part + pre_act * pdf_part)
    g_up_b = jnp.sum(d_pre, axis=0)
    d_pre_b = d_pre.astype(jnp.bfloat16)
    d_hidden = d_ffn + jnp.einsum("rf,df->rd", d_pre_b, upm_back, preferred_element_type=fl)
    g_gain_one = jnp.sum(d_hidden * normed_one, axis=0)
    g_shift_one = jnp.sum(d_hidden, axis=0)
    d_attn = norm_back(d_hidden, normed_one, inverse_one, gain_one_back.astype(fl))
    g_out_b = jnp.sum(d_attn, axis=0)
    d_attn_b = d_attn.astype(jnp.bfloat16)
    d_context = jnp.einsum("re,de->rd", d_attn_b, outm_back, preferred_element_type=fl).astype(
        jnp.bfloat16
    )
    d_qkv, attn_sums = attention_back(qkv, d_context, doc_ids, pad_mask)
    g_qbias, g_vbias = attn_sums[0], attn_sums[1]
    token_grad = d_attn + jnp.einsum("re,de->rd", d_qkv, qkv_back, preferred_element_type=fl)
    sums = vector_rows(
        [
            g.reshape((lax.axis_size(AXIS), -1))
            for g in (
                g_qbias,
                g_vbias,
                g_out_b,
                g_gain_one,
                g_shift_one,
                g_down_b,
                g_gain_two,
                g_shift_two,
                g_up_b,
            )
        ]
    )
    pairs = ((tokens, d_qkv), (context, d_attn_b), (hidden_b, d_pre_b), (activation, d_ffn_b))
    owned = [
        lax.psum_scatter(p, AXIS, scatter_dimension=0, tiled=True)
        for p in [grad_rows(left, right) for left, right in pairs]
        + [sums.reshape((-1, sums.shape[2]))]
    ]
    grad_qkv, grad_outmat, grad_upmat, grad_downmat, vec = owned
    owned_sums = [vec[j, : v.shape[0]] for j, v in enumerate(owned_vectors)]
    return (
        layer_out,
        token_grad,
        grad_qkv,
        owned_sums[0],
        owned_sums[1],
        grad_outmat,
        owned_sums[2],
        owned_sums[3],
        owned_sums[4],
        grad_upmat,
        owned_sums[8],
        grad_downmat,
        owned_sums[5],
        owned_sums[6],
        owned_sums[7],
    )


def solution(mesh):
    placed = (
        P("fsdp", None),
        P("fsdp"),
        P("fsdp"),
        P("fsdp", None),
        P("fsdp"),
        P("fsdp"),
        P("fsdp", None),
        P("fsdp"),
        P("fsdp"),
        P("fsdp"),
        P("fsdp", None),
        P("fsdp"),
        P("fsdp", None),
        P("fsdp"),
        P("fsdp"),
        P("fsdp"),
        P("fsdp", None),
    )
    return jax.shard_map(
        local,
        mesh=mesh,
        in_specs=placed,
        out_specs=(
            P("fsdp", None),
            P("fsdp", None),
            P("fsdp", None),
            P("fsdp"),
            P("fsdp"),
            P("fsdp", None),
            P("fsdp"),
            P("fsdp"),
            P("fsdp"),
            P("fsdp", None),
            P("fsdp"),
            P("fsdp", None),
            P("fsdp"),
            P("fsdp"),
            P("fsdp"),
        ),
        check_vma=False,
    )
```
